768 devices in a mesh: gx: 4 (over x), gy: 24 (over z, core), gz: 8 (over y).
Axes of the slice: x: 4, y: 8, z: 12, core: 2. Of those that a mesh axis runs over, the one named last changes fastest.
Arguments:
- fine_state: float32 [14, 32, 192, 1024], P(None, 'gx', 'gy', 'gz'), may hold values from -5 to 5, as said below
- diffusivity: float32 [14], replicated, may hold values from 0.2 to 1.5
- coarse_cells: float32 [14, 98304], P(None, ('gx', 'gy', 'gz')), may hold values from -5 to 5, as said below
- copy_sources: int32 [4, 24, 8, 96, 3], P('gx', 'gy', 'gz'), may hold values from -1 to 127, as said below
- copy_targets: int32 [4, 24, 8, 96, 3], P('gx', 'gy', 'gz'), may hold values from -1 to 255, as said below
Outputs:
- section_state: float32 [14, 32, 192, 1024], P(None, 'gx', 'gy', 'gz')
The draws below stay inside these ranges and needn't reach their ends.
Inputs may be any that keep to these rules, and one draw needn't show every extreme that they name: `fine_state`: field 9 (density) lies between 0.5 and 2. `coarse_cells`: field 9 (density) lies between 0.5 and 2. `copy_sources`: entry [a, b, c, p, s] is the row, among the 128 coarse cells of device (a, b, c), sent to peer p in slot s, or -1 for an empty slot; devices at the two x ends receive exactly 256 coarse cells each over all slots, the others none. `copy_targets`: entry [a, b, c, p, s] is the face cell of device (a, b, c) that slot s from peer p fills, or -1; it is -1 exactly where the matching copy_sources entry is; at the two x ends every face cell is filled once.
All inputs are finite; a program needn't handle non-finite values.
Results may differ from the reference program's by a relative error of at most 0.00002.
Values sent between devices are 32-bit elements; how exact they have to be, the bound alone decides.
A program may use at most 32 MiB of HBM per device.

```python
import math
import jax
import jax.numpy as jnp
from jax import lax

FIELDS = 14
CY = 8
CZ = 128
NX = 32
NY = 192
NZ = 1024
CAP = 3
CROWS = 128
COARSE_ROWS = 98304
N_GX = 4
N_GY = 24
N_GZ = 8


def field_values(key, shape):
    key_values, key_density = jax.random.split(key)
    full_shape = (FIELDS,) + shape
    dense_shape = (1,) + shape
    values = jnp.clip(jax.random.normal(key_values, full_shape, jnp.float32), -5.0, 5.0)
    density = jnp.exp(jax.random.uniform(key_density, dense_shape, jnp.float32, math.log(0.5), math.log(2.0)))
    return jnp.concatenate([values[:9], density, values[10:]], axis=0)


def draw_fine_state(key, part):
    key = jax.random.fold_in(key, 11)
    return field_values(key, (NX, NY, NZ))


def draw_coarse_cells(key, part):
    key = jax.random.fold_in(key, 12)
    return field_values(key, (COARSE_ROWS,))


def copy_lists(key):
    peer_count = N_GX * N_GY
    device_count = N_GX * N_GY * N_GZ
    half_cells = CY // 2 * (CZ // 2)
    key_order, key_shift, key_rows = jax.random.split(key, 3)
    orders = jax.vmap(lambda k: jax.random.permutation(k, half_cells))(jax.random.split(key_order, device_count)).astype(jnp.int32)
    shifts = jax.random.randint(key_shift, (device_count, 1), 0, peer_count, dtype=jnp.int32)
    picked_rows = jax.random.randint(key_rows, (device_count, half_cells), 0, CROWS, dtype=jnp.int32)
    picked_rows = picked_rows.at[:, 0].set(CROWS - 1)
    position = jnp.arange(half_cells, dtype=jnp.int32)[None, :]
    source = (position + shifts) % peer_count
    slot_index = jnp.broadcast_to(position // peer_count, source.shape)
    device = jnp.arange(device_count, dtype=jnp.int32)
    column_x = device // (N_GY * N_GZ)
    column_y = device // N_GZ % N_GY
    column_z = device % N_GZ
    active = ((column_x == 0) | (column_x == N_GX - 1))[:, None]
    receiver = jnp.broadcast_to(device[:, None], source.shape)
    targets = jnp.full((device_count, peer_count, CAP), -1, jnp.int32)
    targets = targets.at[receiver, source, slot_index].set(jnp.where(active, orders, -1))
    sender = source * N_GZ + column_z[:, None]
    seen_as = jnp.broadcast_to((column_x * N_GY + column_y)[:, None], source.shape)
    row_table = jnp.full((device_count, peer_count, CAP), -1, jnp.int32)
    row_table = row_table.at[sender, seen_as, slot_index].set(jnp.where(active, picked_rows, -1))
    shape = (N_GX, N_GY, N_GZ, peer_count, CAP)
    return (row_table.reshape(shape), targets.reshape(shape))


def draw_copy_sources(key, part):
    return copy_lists(key)[0]


def draw_copy_targets(key, part):
    return copy_lists(key)[1]


def setup_inputs(seed: int = 0) -> dict:
    seeds = jax.random.split(jax.random.key(seed), 6)
    fine_state = draw_fine_state(jax.random.fold_in(seeds[5], 71), 0)
    diffusivity = jnp.clip(jnp.exp(jax.random.uniform(seeds[1], (FIELDS,), jnp.float32, math.log(0.2), math.log(1.5))), 0.2, 1.5)
    coarse_cells = draw_coarse_cells(jax.random.fold_in(seeds[5], 71), 0)
    copy_sources = draw_copy_sources(jax.random.fold_in(seeds[5], 71), 0)
    copy_targets = draw_copy_targets(jax.random.fold_in(seeds[5], 71), 0)
    return dict(fine_state=fine_state, diffusivity=diffusivity, coarse_cells=coarse_cells, copy_sources=copy_sources, copy_targets=copy_targets)


time_step = 0.15


def face_divergence(padded, direction, diffusivity):
    face_count = padded.shape[direction] - 3

    def planes_at(offset):
        return lax.slice_in_dim(padded, offset, offset + face_count, axis=direction)

    left_far, left_cell, right_cell, right_far = planes_at(0), planes_at(1), planes_at(2), planes_at(3)
    component = 9 + direction
    rho_left = left_cell[9:10]
    rho_right = right_cell[9:10]
    velocity = 0.5 * (left_cell[component:component + 1] / rho_left + right_cell[component:component + 1] / rho_right)
    from_left = left_cell + 0.25 * (right_cell - left_far)
    from_right = right_cell - 0.25 * (right_far - left_cell)
    advect = jnp.maximum(velocity, 0.0) * from_left + jnp.minimum(velocity, 0.0) * from_right
    spread = diffusivity.reshape(-1, 1, 1, 1) * (0.5 * (rho_left + rho_right)) * (right_cell / rho_right - left_cell / rho_left)
    face_flux = advect - spread
    cell_count = face_count - 1
    return lax.slice_in_dim(face_flux, 1, cell_count + 1, axis=direction) - lax.slice_in_dim(face_flux, 0, cell_count, axis=direction)


def coarse_faces(coarse_cells, copy_sources, copy_targets):
    fields = coarse_cells.shape[0]
    peer_count = N_GX * N_GY
    half_cells = (CY // 2) * (CZ // 2)
    source_rows = jnp.transpose(copy_sources.reshape(peer_count, N_GZ, peer_count, CAP), (2, 1, 0, 3))
    target = copy_targets.reshape(peer_count, N_GZ, peer_count, CAP)
    sender = jnp.arange(peer_count, dtype=jnp.int32)[None, None, :, None]
    layer_index = jnp.arange(N_GZ, dtype=jnp.int32)[None, :, None, None]
    owner_row = (sender * N_GZ + layer_index) * CROWS + jnp.maximum(source_rows, 0)
    values = jnp.take(coarse_cells, owner_row.reshape(-1), axis=1).reshape(fields, peer_count, N_GZ, peer_count, CAP)
    target = jnp.where(target >= 0, target, half_cells).astype(jnp.int32)
    receiver = jnp.broadcast_to(jnp.arange(peer_count, dtype=jnp.int32)[:, None, None, None], target.shape)
    layer_full = jnp.broadcast_to(layer_index, target.shape)
    planes = jnp.zeros((fields, peer_count, N_GZ, half_cells + 1), jnp.float32)
    planes = planes.at[:, receiver, layer_full, target].add(values)
    planes = planes[..., :half_cells].reshape(fields, N_GX, N_GY, N_GZ, CY // 2, CZ // 2)

    def to_fine(face_block):
        face_grid = jnp.transpose(face_block, (0, 1, 3, 2, 4)).reshape(fields, N_GY * (CY // 2), N_GZ * (CZ // 2))
        return jnp.repeat(jnp.repeat(face_grid, 2, axis=1), 2, axis=2)

    return to_fine(planes[:, 0]), to_fine(planes[:, N_GX - 1])


def reference(fine_state, diffusivity, coarse_cells, copy_sources, copy_targets):
    low_plane, high_plane = coarse_faces(coarse_cells, copy_sources, copy_targets)

    def one_plane(plane_index, result):
        plane_index = plane_index.astype(jnp.int32)
        plane_rows = plane_index + jnp.arange(-2, 3, dtype=jnp.int32)
        window = jnp.take(fine_state, jnp.clip(plane_rows, 0, NX - 1), axis=1)
        window = jnp.where((plane_rows < 0)[None, :, None, None], low_plane[:, None], window)
        window = jnp.where((plane_rows >= NX)[None, :, None, None], high_plane[:, None], window)
        window = jnp.pad(window, ((0, 0), (0, 0), (2, 2), (2, 2)), mode="wrap")
        divergence = face_divergence(window[:, :, 2:-2, 2:-2], 1, diffusivity)
        divergence = divergence + face_divergence(window[:, 2:3, :, 2:-2], 2, diffusivity)
        divergence = divergence + face_divergence(window[:, 2:3, 2:-2, :], 3, diffusivity)
        updated = window[:, 2:3, 2:-2, 2:-2] - time_step * divergence
        return lax.dynamic_update_slice_in_dim(result, updated, plane_index, axis=1)

    return lax.fori_loop(0, NX, one_plane, jnp.zeros_like(fine_state))
```

```python
import functools

import jax
import jax.numpy as jnp
from jax import lax
from jax.experimental import pallas as pl
from jax.experimental.pallas import tpu as pltpu
from jax.sharding import PartitionSpec as P

MESH = pl.DeviceIdType.MESH
time_step = 0.15
SLOT = 16


def split3(value):
    hi = value.astype(jnp.bfloat16)
    rest = value - hi.astype(jnp.float32)
    mid = rest.astype(jnp.bfloat16)
    low = (rest - mid.astype(jnp.float32)).astype(jnp.bfloat16)
    return jnp.concatenate([hi, mid, low], axis=0)


def face_terms(rho_left, rho_right, mom_left, mom_right):
    inv_left, inv_right = 1.0 / rho_left, 1.0 / rho_right
    velocity = (0.5 * time_step) * (mom_left * inv_left + mom_right * inv_right)
    up, down = jnp.maximum(velocity, 0.0), jnp.minimum(velocity, 0.0)
    quarter_up, quarter_down = 0.25 * up, 0.25 * down
    mean_rho = (0.5 * time_step) * (rho_left + rho_right)
    return (
        up + quarter_down,
        down + quarter_up,
        quarter_up,
        quarter_down,
        mean_rho * inv_left,
        mean_rho * inv_right,
    )


def face_flux(terms, diff, far_left, left, right, far_right):
    a_left, a_right, b_left, b_right, e_left, e_right = terms
    return (
        left * (a_left + diff * e_left)
        + right * (a_right - diff * e_right)
        - b_left * far_left
        - b_right * far_right
    )


def kernel(
    n_x, n_y, n_z, fields,
    fine, diff, coarse, sources, targets,
    out,
    qx, y_own, y_low, y_high, y_rows, y_flux, z_own, z_low, z_high, z_flux,
    cells, src, tgt, msg, first, second, arrived, order, spread, plane, terms,
    load_sem, halo_send, halo_recv, first_send, first_recv, second_send, second_recv,
):
    a, b, c = lax.axis_index("gx"), lax.axis_index("gy"), lax.axis_index("gz")
    is_end = jnp.logical_or(a == 0, a == n_x - 1)
    peers = n_x * n_y

    def x_at(k):
        return (lax.rem(a + (k + n_x), n_x), b, c)

    def y_at(k):
        return (a, lax.rem(b + (k + n_y), n_y), c)

    def z_at(k):
        return (a, b, lax.rem(c + (k + n_z), n_z))

    load_cells = pltpu.make_async_copy(coarse, cells, load_sem.at[0])
    load_src = pltpu.make_async_copy(sources, src, load_sem.at[1])
    load_fine = pltpu.make_async_copy(fine, qx.at[:, pl.ds(16, 64)], load_sem.at[2])
    load_tgt = pltpu.make_async_copy(targets, tgt, load_sem.at[3])
    load_cells.start()
    load_src.start()
    load_fine.start()
    load_tgt.start()

    barrier = pltpu.get_barrier_semaphore()

    def greet(device):
        pl.semaphore_signal(barrier, inc=1, device_id=device, device_id_type=MESH)

    for k in range(1, n_x):
        greet(x_at(k))
    greet(y_at(1))
    greet(y_at(-1))
    greet(z_at(1))
    greet(z_at(-1))

    @pl.when(is_end)
    def _():
        for k in range(2, n_y - 1):
            greet(y_at(k))

    load_cells.wait()
    load_src.wait()
    owned = jnp.concatenate([cells[...], jnp.zeros((SLOT - fields, 128), jnp.float32)], axis=0)
    owned = split3(owned)
    row = lax.broadcasted_iota(jnp.int32, (128, 128), 0)
    blank = jnp.full((1, 128 - peers), -1, jnp.int32)
    picked = []
    for s in range(3):
        wanted = jnp.concatenate([src[s], blank], axis=1)
        chosen = jnp.where(row == wanted, 1.0, 0.0).astype(jnp.bfloat16)
        part = jnp.dot(owned, chosen, preferred_element_type=jnp.float32)
        picked.append(part[:SLOT] + part[SLOT : 2 * SLOT] + part[2 * SLOT :])
    picked.append(jnp.zeros((128 - 3 * SLOT, 128), jnp.float32))
    picked = jnp.concatenate(picked, axis=0).T
    msg[0] = picked[:n_y]
    msg[1] = picked[peers - n_y : peers]

    load_fine.wait()
    lane = lax.broadcasted_iota(jnp.int32, (8, 128), 1)
    line = lax.broadcasted_iota(jnp.int32, (8, 128), 0)
    for f in range(fields):
        y_own[0, f, 0] = qx[f, pl.ds(16, 8, stride=8), :]
        y_own[0, f, 1] = qx[f, pl.ds(17, 8, stride=8), :]
        y_own[1, f, 0] = qx[f, pl.ds(22, 8, stride=8), :]
        y_own[1, f, 1] = qx[f, pl.ds(23, 8, stride=8), :]
        packed = pltpu.roll(qx[f, pl.ds(16, 8), :], 2, 1)
        for x in range(1, 8):
            moved = pltpu.roll(qx[f, pl.ds(16 + 8 * x, 8), :], 4 * x + 2, 1)
            packed = jnp.where(lane >= 4 * x, moved, packed)
        z_own[f] = packed

    @pl.when(is_end)
    def _():
        pl.semaphore_wait(barrier, n_x - 1 + n_y - 1 + 2)

    @pl.when(jnp.logical_not(is_end))
    def _():
        pl.semaphore_wait(barrier, n_x - 1 + 2 + 2)

    def to_end(which):
        end = (0, n_x - 1)[which]
        return pltpu.make_async_remote_copy(
            src_ref=msg.at[which], dst_ref=first.at[a],
            send_sem=first_send.at[which], recv_sem=first_recv.at[a],
            device_id=(end, b, c), device_id_type=MESH,
        )

    for which in range(2):
        end = (0, n_x - 1)[which]

        @pl.when(a != end)
        def _():
            to_end(which).start()

        @pl.when(a == end)
        def _():
            first[end] = msg[which]

    def halo(i, source, target, device):
        return pltpu.make_async_remote_copy(
            src_ref=source, dst_ref=target, send_sem=halo_send.at[i], recv_sem=halo_recv.at[i],
            device_id=device, device_id_type=MESH,
        )

    halos = [
        halo(0, y_own.at[0], y_high, y_at(-1)),
        halo(1, y_own.at[1], y_low, y_at(1)),
        halo(2, z_own, z_high, z_at(-1)),
        halo(3, z_own, z_low, z_at(1)),
        halo(4, qx.at[:, pl.ds(16, 16)], qx.at[:, pl.ds(80, 16)], x_at(-1)),
        halo(5, qx.at[:, pl.ds(64, 16)], qx.at[:, pl.ds(0, 16)], x_at(1)),
    ]
    for copy in halos:
        copy.start()

    load_tgt.wait()

    def to_peer(k):
        return pltpu.make_async_remote_copy(
            src_ref=second.at[pl.ds(pl.multiple_of(8 * lax.rem(b + k, n_y), 8), 8)], dst_ref=arrived.at[b],
            send_sem=second_send, recv_sem=second_recv,
            device_id=y_at(k), device_id_type=MESH,
        )

    @pl.when(is_end)
    def _():
        wide = [jnp.concatenate([tgt[s], blank], axis=1) for s in range(3)]
        wide.append(jnp.full((125, 128), -1, jnp.int32))
        wide = jnp.concatenate(wide, axis=0).astype(jnp.float32).T
        order[...] = jnp.full(order.shape, -1.0, jnp.float32)
        for k in range(n_x):
            order[pl.ds(k, n_y, stride=8), :] = wide[k * n_y : (k + 1) * n_y]
        half = (lax.broadcasted_iota(jnp.int32, (256, 128), 1) // 2).astype(jnp.float32)
        filled = order[...]
        for s in range(3):
            cell = filled[:, s : s + 1]
            for h in range(4):
                spread[256 * s : 256 * (s + 1), 128 * h : 128 * (h + 1)] = jnp.where(
                    cell - 64.0 * h == half, 1.0, 0.0
                ).astype(jnp.bfloat16)
        second[...] = jnp.zeros(second.shape, jnp.float32)
        if n_y < 32:
            arrived[n_y:] = jnp.zeros((32 - n_y, 8, 128), jnp.float32)
        for k in range(1, n_x):
            pltpu.make_async_remote_copy(
                src_ref=msg.at[0], dst_ref=first.at[lax.rem(a + k, n_x)],
                send_sem=first_send.at[0], recv_sem=first_recv.at[lax.rem(a + k, n_x)],
                device_id=x_at(k), device_id_type=MESH,
            ).wait_recv()
        for k in range(n_x):
            second[pl.ds(k, n_y, stride=8), :] = first[k]
        for k in range(1, n_y):
            to_peer(k).start()
        arrived[b] = second[pl.ds(pl.multiple_of(8 * b, 8), 8), :]

    for i in range(4):
        halos[i].wait_recv()

    def tile(f, x):
        return qx[f, pl.ds(16 + 8 * x, 8), :]

    def z_next(f, x):
        kept = jnp.where(lane % 4 < 2, z_low[f], z_high[f])
        return pltpu.roll(kept, 126 - 4 * x, 1)

    def shifted(value, beyond, index, size, axis):
        far_left = pltpu.roll(jnp.where(index >= size - 2, beyond, value), 2, axis)
        left = pltpu.roll(jnp.where(index == size - 1, beyond, value), 1, axis)
        far_right = pltpu.roll(jnp.where(index == 0, beyond, value), size - 1, axis)
        return far_left, left, far_right

    last_y = face_terms(y_own[1, 9, 1], y_high[9, 0], y_own[1, 11, 1], y_high[11, 0])

    def z_last(f):
        cells4 = jnp.where(lane % 4 < 2, z_own[f], z_high[f])
        return cells4, pltpu.roll(cells4, 127, 1), pltpu.roll(cells4, 126, 1), pltpu.roll(cells4, 125, 1)

    _, rho_left, rho_right, _ = z_last(9)
    _, mom_left, mom_right, _ = z_last(12)
    last_z = face_terms(rho_left, rho_right, mom_left, mom_right)
    for f in range(fields):
        y_rows[f, pl.ds(6, 8, stride=8), :] = y_low[f, 0]
        y_rows[f, pl.ds(7, 8, stride=8), :] = y_low[f, 1]
        y_rows[f, pl.ds(0, 8, stride=8), :] = y_high[f, 0]
        y_flux[f, pl.ds(7, 8, stride=8), :] = face_flux(
            last_y, diff[f], y_own[1, f, 0], y_own[1, f, 1], y_high[f, 0], y_high[f, 1]
        )
        z_flux[f] = face_flux(last_z, diff[f], *z_last(f))

    for x in range(8):
        _, rho_left, _ = shifted(tile(9, x), y_rows[9, pl.ds(8 * x, 8), :], line, 8, 0)
        _, mom_left, _ = shifted(tile(11, x), y_rows[11, pl.ds(8 * x, 8), :], line, 8, 0)
        found = face_terms(rho_left, tile(9, x), mom_left, tile(11, x))
        _, rho_left, _ = shifted(tile(9, x), z_next(9, x), lane, 128, 1)
        _, mom_left, _ = shifted(tile(12, x), z_next(12, x), lane, 128, 1)
        found = found + face_terms(rho_left, tile(9, x), mom_left, tile(12, x))
        for i in range(12):
            terms[x, i] = found[i]

    def along_yz(f, carry):
        for x in range(8):
            here = tile(f, x)
            rows = pl.ds(8 * x, 8)
            far_left, left, far_right = shifted(here, y_rows[f, rows, :], line, 8, 0)
            low = face_flux([terms[x, i] for i in range(6)], diff[f], far_left, left, here, far_right)
            high = jnp.where(line == 7, y_flux[f, rows, :], pltpu.roll(low, 7, 0))
            total = here + (low - high)
            far_left, left, far_right = shifted(here, z_next(f, x), lane, 128, 1)
            low = face_flux([terms[x, 6 + i] for i in range(6)], diff[f], far_left, left, here, far_right)
            last = pltpu.roll(z_flux[f], 127 - 4 * x, 1)
            high = jnp.where(lane == 127, last, pltpu.roll(low, 127, 1))
            out[f, rows, :] = total + (low - high)
        return carry

    lax.fori_loop(0, fields, along_yz, 0)

    halos[4].wait_recv()
    halos[5].wait_recv()

    @pl.when(is_end)
    def _():
        every = pltpu.make_async_remote_copy(
            src_ref=arrived.at[pl.ds(0, n_y - 1)], dst_ref=arrived.at[pl.ds(0, n_y - 1)],
            send_sem=second_send, recv_sem=second_recv,
            device_id=y_at(1), device_id_type=MESH,
        )
        every.wait_recv()
        by_slot = arrived[...].reshape(256, 128).T
        by_slot = jnp.concatenate([by_slot[SLOT * s : SLOT * (s + 1)] for s in range(3)], axis=1)
        face = jnp.dot(split3(by_slot), spread[...], preferred_element_type=jnp.float32)
        face = face[:SLOT] + face[SLOT : 2 * SLOT] + face[2 * SLOT :]
        for y in range(8):
            h = y // 2
            plane[SLOT * y : SLOT * (y + 1), :] = face[:, 128 * h : 128 * (h + 1)]
        for end, start in ((0, 0), (n_x - 1, 80)):

            @pl.when(a == end)
            def _():
                for f in range(fields):
                    ghost = plane[pl.ds(f, 8, stride=SLOT), :]
                    qx[f, pl.ds(start, 8), :] = ghost
                    qx[f, pl.ds(start + 8, 8), :] = ghost

        every.wait_send()

    for i in range(9):
        left, right = pl.ds(8 * i + 8, 8), pl.ds(8 * i + 16, 8)
        found = face_terms(qx[9, left, :], qx[9, right, :], qx[10, left, :], qx[10, right, :])
        for j in range(6):
            terms[i, j] = found[j]

    def along_x(f, carry):
        low = None
        for i in range(9):
            cells4 = [qx[f, pl.ds(8 * (i + j), 8), :] for j in range(4)]
            high = face_flux([terms[i, j] for j in range(6)], diff[f], *cells4)
            if i > 0:
                rows = pl.ds(8 * (i - 1), 8)
                out[f, rows, :] = out[f, rows, :] + (low - high)
            low = high
        return carry

    lax.fori_loop(0, fields, along_x, 0)

    for which in range(2):

        @pl.when(a != (0, n_x - 1)[which])
        def _():
            to_end(which).wait_send()

    for copy in halos:
        copy.wait_send()


def solution(mesh):
    n_x, n_y, n_z = (mesh.shape[name] for name in ("gx", "gy", "gz"))

    def on_device(fine_state, diffusivity, coarse_cells, copy_sources, copy_targets):
        fields, cells_x, cells_y, cells_z = fine_state.shape
        rows = cells_x * cells_y
        peers = n_x * n_y
        sources = jnp.transpose(copy_sources, (0, 1, 4, 2, 3)).reshape(3, 1, peers)
        targets = jnp.transpose(copy_targets, (0, 1, 4, 2, 3)).reshape(3, 1, peers)
        f32 = jnp.float32
        vmem = pltpu.VMEM
        anywhere = pl.BlockSpec(memory_space=pl.ANY)
        result = pl.pallas_call(
            functools.partial(kernel, n_x, n_y, n_z, fields),
            out_shape=jax.ShapeDtypeStruct((fields, rows, cells_z), f32),
            in_specs=[anywhere, pl.BlockSpec(memory_space=pltpu.SMEM), anywhere, anywhere, anywhere],
            out_specs=pl.BlockSpec(memory_space=pltpu.VMEM),
            scratch_shapes=[
                vmem((fields, rows + 32, cells_z), f32),
                vmem((2, fields, 2, 8, 128), f32),
                vmem((fields, 2, 8, 128), f32),
                vmem((fields, 2, 8, 128), f32),
                vmem((fields, rows, 128), f32),
                vmem((fields, rows, 128), f32),
                vmem((fields, 8, 128), f32),
                vmem((fields, 8, 128), f32),
                vmem((fields, 8, 128), f32),
                vmem((fields, 8, 128), f32),
                vmem((fields, 128), f32),
                vmem((3, 1, peers), jnp.int32),
                vmem((3, 1, peers), jnp.int32),
                vmem((2, n_y, 128), f32),
                vmem((n_x, n_y, 128), f32),
                vmem((8 * n_y, 128), f32),
                vmem((32, 8, 128), f32),
                vmem((256, 128), f32),
                vmem((768, 512), jnp.bfloat16),
                vmem((8 * SLOT, 128), f32),
                vmem((9, 12, 8, 128), f32),
                pltpu.SemaphoreType.DMA((4,)),
                pltpu.SemaphoreType.DMA((6,)),
                pltpu.SemaphoreType.DMA((6,)),
                pltpu.SemaphoreType.DMA((2,)),
                pltpu.SemaphoreType.DMA((n_x,)),
                pltpu.SemaphoreType.DMA,
                pltpu.SemaphoreType.DMA,
            ],
            compiler_params=pltpu.CompilerParams(
                collective_id=0, has_side_effects=True, vmem_limit_bytes=56 * 1024 * 1024
            ),
        )(fine_state.reshape(fields, rows, cells_z), diffusivity, coarse_cells, sources, targets)
        return result.reshape(fine_state.shape)

    return jax.shard_map(
        on_device,
        mesh=mesh,
        in_specs=(
            P(None, "gx", "gy", "gz"),
            P(),
            P(None, ("gx", "gy", "gz")),
            P("gx", "gy", "gz", None, None),
            P("gx", "gy", "gz", None, None),
        ),
        out_specs=P(None, "gx", "gy", "gz"),
        check_vma=False,
    )
```

```python
import functools

import jax
import jax.numpy as jnp
from jax import lax
from jax.experimental import pallas as pl
from jax.experimental.pallas import tpu as pltpu
from jax.sharding import PartitionSpec as P

MESH = pl.DeviceIdType.MESH
time_step = 0.15
SLOT = 16


def hubs_of(n_y):
    n_hubs = max(1, n_y // 4)
    return n_hubs, n_y // n_hubs


def split3(value):
    hi = value.astype(jnp.bfloat16)
    rest = value - hi.astype(jnp.float32)
    mid = rest.astype(jnp.bfloat16)
    low = (rest - mid.astype(jnp.float32)).astype(jnp.bfloat16)
    return jnp.concatenate([hi, mid, low], axis=0)


def face_terms(rho_left, rho_right, mom_left, mom_right):
    inv_left, inv_right = 1.0 / rho_left, 1.0 / rho_right
    velocity = (0.5 * time_step) * (mom_left * inv_left + mom_right * inv_right)
    up, down = jnp.maximum(velocity, 0.0), jnp.minimum(velocity, 0.0)
    quarter_up, quarter_down = 0.25 * up, 0.25 * down
    mean_rho = (0.5 * time_step) * (rho_left + rho_right)
    return (
        up + quarter_down,
        down + quarter_up,
        quarter_up,
        quarter_down,
        mean_rho * inv_left,
        mean_rho * inv_right,
    )


def cell_terms(low, high):
    a_left, a_right, b_left, b_right, e_left, e_right = low
    next_left, next_right, next_b_left, next_b_right, next_e_left, next_e_right = high
    around = (
        -b_left,
        a_left + next_b_left,
        e_left,
        -(b_right + next_right),
        next_e_right,
        next_b_right,
    )
    return around, (a_right - next_left, -(e_right + next_e_left))


def weighted(found, diff, far_low, low, high, far_high):
    w_far_low, w_low, d_low, w_high, d_high, w_far_high = found
    return (
        (w_far_low * far_low + w_far_high * far_high)
        + (w_low + diff * d_low) * low
        + (w_high + diff * d_high) * high
    )


def work(n_x, n_y, fields, diff, out, qx, y_own, y_low, y_high, y_pad, z_own, z_low, z_high, z_rows,
         cells, src, tgt, msg, relay, arrived, order, spread, plane, terms):
    peers = n_x * n_y
    n_hubs, per_hub = hubs_of(n_y)
    lane = lax.broadcasted_iota(jnp.int32, (8, 128), 1)
    line = lax.broadcasted_iota(jnp.int32, (8, 128), 0)
    blank = jnp.full((1, 128 - peers), -1, jnp.int32)

    def pick():
        owned = jnp.concatenate([cells[...], jnp.zeros((SLOT - fields, 128), jnp.float32)], axis=0)
        owned = split3(owned)
        row = lax.broadcasted_iota(jnp.int32, (128, 128), 0)
        picked = []
        for s in range(3):
            wanted = jnp.concatenate([src[s], blank], axis=1)
            chosen = jnp.where(row == wanted, 1.0, 0.0).astype(jnp.bfloat16)
            part = jnp.dot(owned, chosen, preferred_element_type=jnp.float32)
            picked.append(part[:SLOT] + part[SLOT : 2 * SLOT] + part[2 * SLOT :])
        picked.append(jnp.zeros((128 - 3 * SLOT, 128), jnp.float32))
        picked = jnp.concatenate(picked, axis=0).T
        n_early = n_y // 2
        for which, start in enumerate((0, peers - n_y)):
            msg[which, : n_y - n_early] = picked[start + n_early : start + n_y].reshape(n_y - n_early, 1, 128)
            msg[which, n_y - n_early :] = picked[start : start + n_early].reshape(n_early, 1, 128)

    def pack():
        for f in range(fields):
            y_own[0, f, 0] = qx[f, pl.ds(16, 8, stride=8), :]
            y_own[0, f, 1] = qx[f, pl.ds(17, 8, stride=8), :]
            y_own[1, f, 0] = qx[f, pl.ds(22, 8, stride=8), :]
            y_own[1, f, 1] = qx[f, pl.ds(23, 8, stride=8), :]
            packed = pltpu.roll(qx[f, pl.ds(16, 8), :], 2, 1)
            for x in range(1, 8):
                moved = pltpu.roll(qx[f, pl.ds(16 + 8 * x, 8), :], 4 * x + 2, 1)
                packed = jnp.where(lane >= 4 * x, moved, packed)
            z_own[f] = packed

    def pad():
        for f in range(fields):
            for x in range(8):
                y_pad[f, pl.ds(16 * x + 8, 8), :] = tile(f, x)

    def place():
        wide = [jnp.concatenate([tgt[s], blank], axis=1) for s in range(3)]
        wide.append(jnp.full((125, 128), -1, jnp.int32))
        wide = jnp.concatenate(wide, axis=0).astype(jnp.float32).T
        order[...] = jnp.full(order.shape, -1.0, jnp.float32)
        count = n_x * per_hub
        for a in range(n_x):
            for k in range(per_hub):
                start = a * n_y + k * n_hubs
                order[pl.ds(a * per_hub + k, n_hubs, stride=count), :] = wide[start : start + n_hubs]
        half = (lax.broadcasted_iota(jnp.int32, (128, 128), 1) // 2).astype(jnp.float32)
        filled = order[...]
        for s in range(3):
            cell = filled[:, s : s + 1]
            for h in range(4):
                spread[128 * s : 128 * (s + 1), 128 * h : 128 * (h + 1)] = jnp.where(
                    cell - 64.0 * h == half, 1.0, 0.0
                ).astype(jnp.bfloat16)
        if peers < 128:
            arrived[peers:] = jnp.zeros((128 - peers, 1, 128), jnp.float32)

    def tile(f, x):
        return qx[f, pl.ds(16 + 8 * x, 8), :]

    def spread_halos():
        for f in range(fields):
            y_pad[f, pl.ds(6, 8, stride=16), :] = y_low[f, 0]
            y_pad[f, pl.ds(7, 8, stride=16), :] = y_low[f, 1]
            y_pad[f, pl.ds(16, 8, stride=16), :] = y_high[f, 0]
            y_pad[f, pl.ds(17, 8, stride=16), :] = y_high[f, 1]
            kept = jnp.where(lane % 4 < 2, z_low[f], z_high[f])
            for x in range(8):
                z_rows[f, pl.ds(8 * x, 8), :] = pltpu.roll(kept, 126 - 4 * x, 1)

    def y_at(f, x, k):
        return y_pad[f, pl.ds(16 * x + 8 + k, 8), :]

    def x_at(f, x, k):
        return qx[f, pl.ds(8 * (x + k) + 16, 8), :]

    def z_all(f, x, here):
        beyond = z_rows[f, pl.ds(8 * x, 8), :]
        return (
            pltpu.roll(jnp.where(lane >= 126, beyond, here), 2, 1),
            pltpu.roll(jnp.where(lane == 127, beyond, here), 1, 1),
            pltpu.roll(jnp.where(lane == 0, beyond, here), 127, 1),
            pltpu.roll(jnp.where(lane < 2, beyond, here), 126, 1),
        )

    def three(rho, mom):
        low = face_terms(rho[0], rho[1], mom[0], mom[1])
        high = face_terms(rho[1], rho[2], mom[1], mom[2])
        return cell_terms(low, high)

    def x_terms(x):
        return three([x_at(9, x, k) for k in (-1, 0, 1)], [x_at(10, x, k) for k in (-1, 0, 1)])

    def cell_weights():
        for x in range(8):
            found, (centre, d_centre) = three([y_at(9, x, k) for k in (-1, 0, 1)], [y_at(11, x, k) for k in (-1, 0, 1)])
            rho, mom = tile(9, x), tile(12, x)
            _, rho_low, rho_high, _ = z_all(9, x, rho)
            _, mom_low, mom_high, _ = z_all(12, x, mom)
            more, (c, d) = three([rho_low, rho, rho_high], [mom_low, mom, mom_high])
            found, centre, d_centre = found + more, centre + c, d_centre + d
            if 2 <= x < 6:
                more, (c, d) = x_terms(x)
                found, centre, d_centre = found + more, centre + c, d_centre + d
            found = found + (1.0 + centre, d_centre)
            for i, value in enumerate(found):
                terms[x, i] = value

    def main_flux():
        def one_field(g, carry):
            for x in range(8):
                for f in (2 * g, 2 * g + 1):
                    here = tile(f, x)
                    inner = 2 <= x < 6
                    found = [terms[x, i] for i in range(20 if inner else 14)]
                    total = here * (found[-2] + diff[f] * found[-1])
                    total = total + weighted(found[:6], diff[f], *[y_at(f, x, k) for k in (-2, -1, 1, 2)])
                    if inner:
                        total = total + weighted(found[12:18], diff[f], *[x_at(f, x, k) for k in (-2, -1, 1, 2)])
                    total = total + weighted(found[6:12], diff[f], *z_all(f, x, here))
                    out[f, pl.ds(8 * x, 8), :] = total
            return carry

        lax.fori_loop(0, fields // 2, one_field, 0)

    def edge_flux(first_x):
        kept = []
        for x in (first_x, first_x + 1):
            found, centre = x_terms(x)
            kept.append(found + centre)
        for f in range(fields):
            for x, found in zip((first_x, first_x + 1), kept):
                rows = pl.ds(8 * x, 8)
                total = tile(f, x) * (found[-2] + diff[f] * found[-1])
                total = total + weighted(found[:6], diff[f], *[x_at(f, x, k) for k in (-2, -1, 1, 2)])
                out[f, rows, :] = out[f, rows, :] + total

    def ghost():
        by_slot = arrived[...].reshape(128, 128).T
        by_slot = jnp.concatenate([by_slot[SLOT * s : SLOT * (s + 1)] for s in range(3)], axis=1)
        face = jnp.dot(split3(by_slot), spread[...], preferred_element_type=jnp.float32)
        face = face[:SLOT] + face[SLOT : 2 * SLOT] + face[2 * SLOT :]
        for y in range(8):
            h = y // 2
            plane[SLOT * y : SLOT * (y + 1), :] = face[:, 128 * h : 128 * (h + 1)]

    def use_ghost(start):
        for f in range(fields):
            cover = plane[pl.ds(f, 8, stride=SLOT), :]
            qx[f, pl.ds(start, 8), :] = cover
            qx[f, pl.ds(start + 8, 8), :] = cover

    return dict(
        pick=pick, pack=pack, pad=pad, place=place, spread_halos=spread_halos, cell_weights=cell_weights,
        main_flux=main_flux, ghost=ghost, use_ghost=use_ghost, edge_flux=edge_flux,
    )


def kernel(
    n_x, n_y, n_z, fields,
    fine, diff, coarse, sources, targets,
    out,
    qx, y_own, y_low, y_high, y_pad, z_own, z_low, z_high, z_rows,
    cells, src, tgt, msg, relay, arrived, order, spread, plane, terms,
    load_sem, halo_send, halo_recv, row_send, row_recv, block_send, block_recv, pass_send, pass_recv, ready,
):
    a, b, c = lax.axis_index("gx"), lax.axis_index("gy"), lax.axis_index("gz")
    is_end = jnp.logical_or(a == 0, a == n_x - 1)
    peers = n_x * n_y
    n_hubs, per_hub = hubs_of(n_y)
    served = n_x * per_hub
    step = work(
        n_x, n_y, fields, diff, out, qx, y_own, y_low, y_high, y_pad, z_own, z_low, z_high, z_rows,
        cells, src, tgt, msg, relay, arrived, order, spread, plane, terms,
    )

    n_early = n_y // 2
    ends = (0, n_x - 1)
    corner = jnp.logical_and(jnp.logical_and(a == 0, b == 0), c == 0)
    is_first = jnp.logical_and(jnp.logical_and(is_end, b < n_early), jnp.logical_not(corner))
    is_hub = jnp.logical_and(jnp.logical_and(is_end, b < n_early), b >= n_early - n_hubs)
    is_late = jnp.logical_and(is_end, jnp.logical_not(is_first))
    with_corner = c == 0
    n_late = n_y - n_early
    row = lax.rem(b, n_hubs) * served + a * per_hub + lax.div(b, n_hubs)

    def x_at(k):
        return (lax.rem(a + (k + n_x), n_x), b, c)

    def y_at(k):
        return (a, lax.rem(b + (k + n_y), n_y), c)

    def z_at(k):
        return (a, b, lax.rem(c + (k + n_z), n_z))

    load_cells = pltpu.make_async_copy(coarse, cells, load_sem.at[0])
    load_src = pltpu.make_async_copy(sources, src, load_sem.at[1])
    load_fine = pltpu.make_async_copy(fine, qx.at[:, pl.ds(16, 64)], load_sem.at[2])
    load_tgt = pltpu.make_async_copy(targets, tgt, load_sem.at[3])
    load_cells.start()
    load_src.start()
    load_fine.start()
    load_tgt.start()

    barrier = pltpu.get_barrier_semaphore()

    def greet(device):
        pl.semaphore_signal(barrier, inc=1, device_id=device, device_id_type=MESH)

    for k in (1, -1):
        greet(x_at(k))
        greet(y_at(k))
        greet(z_at(k))

    @pl.when(is_first)
    def _():
        for k in range(n_x):
            for peer in range(n_y):

                @pl.when(jnp.logical_or(a != k, b != peer))
                def _():
                    greet((k, peer, c))

    load_cells.wait()
    load_src.wait()
    step["pick"]()
    pl.semaphore_wait(barrier, 6 + 2 * n_early - jnp.where(with_corner, 1, 0) - jnp.where(is_first, 1, 0))

    def to_first(which, peer):
        return pltpu.make_async_remote_copy(
            src_ref=msg.at[which, pl.ds(n_late + peer, 1)], dst_ref=arrived.at[pl.ds(row, 1)],
            send_sem=row_send, recv_sem=row_recv,
            device_id=(ends[which], peer, c), device_id_type=MESH,
        )

    def to_hub(which):
        slot = a * per_hub + lax.div(b, n_hubs)
        return pltpu.make_async_remote_copy(
            src_ref=msg.at[which, pl.ds(0, n_late + 1)], dst_ref=relay.at[slot],
            send_sem=block_send.at[which], recv_sem=block_recv,
            device_id=(ends[which], n_early - n_hubs + lax.rem(b, n_hubs), c), device_id_type=MESH,
        )

    for peer in range(n_early):
        for which in range(2):
            itself = jnp.logical_and(a == ends[which], b == peer)
            meant = jnp.logical_not(itself)
            if peer == 0 and which == 0:
                meant = jnp.logical_and(meant, jnp.logical_not(with_corner))
                itself = jnp.logical_and(itself, jnp.logical_not(with_corner))

            @pl.when(meant)
            def _():
                to_first(which, peer).start()

            @pl.when(itself)
            def _():
                arrived[pl.ds(row, 1)] = msg[which, pl.ds(n_late + peer, 1)]

    def own_hub(which):
        return jnp.logical_and(a == ends[which], b == n_early - n_hubs + lax.rem(b, n_hubs))

    for which in range(2):

        @pl.when(jnp.logical_not(own_hub(which)))
        def _():
            to_hub(which).start()

        @pl.when(own_hub(which))
        def _():
            relay[a * per_hub + lax.div(b, n_hubs)] = msg[which, pl.ds(0, n_late + 1)]

    @pl.when(is_late)
    def _():
        for h in range(n_hubs):
            pl.semaphore_signal(ready, inc=1, device_id=(a, n_early - n_hubs + h, c), device_id_type=MESH)

    def halo(i, source, target, device):
        return pltpu.make_async_remote_copy(
            src_ref=source, dst_ref=target, send_sem=halo_send.at[i], recv_sem=halo_recv.at[i],
            device_id=device, device_id_type=MESH,
        )

    load_fine.wait()
    step["pack"]()
    to_low = halo(4, qx.at[:, pl.ds(16, 16)], qx.at[:, pl.ds(80, 16)], x_at(-1))
    to_high = halo(5, qx.at[:, pl.ds(64, 16)], qx.at[:, pl.ds(0, 16)], x_at(1))
    has_low, has_high = a > 0, a < n_x - 1
    halos = [
        halo(1, y_own.at[1], y_low, y_at(1)),
        halo(0, y_own.at[0], y_high, y_at(-1)),
        halo(2, z_own, z_high, z_at(-1)),
        halo(3, z_own, z_low, z_at(1)),
    ]
    for copy in halos:
        copy.start()

    @pl.when(has_low)
    def _():
        to_low.start()

    @pl.when(has_high)
    def _():
        to_high.start()

    load_tgt.wait()

    @pl.when(is_end)
    def _():
        step["place"]()

    step["pad"]()
    for copy in halos:
        copy.wait_recv()
    step["spread_halos"]()
    step["cell_weights"]()
    step["main_flux"]()

    @pl.when(has_high)
    def _():
        to_low.wait_recv()
        step["edge_flux"](6)

    @pl.when(has_low)
    def _():
        to_high.wait_recv()
        step["edge_flux"](0)

    def to_late(peer):
        return pltpu.make_async_remote_copy(
            src_ref=relay.at[:, (peer - n_early) % n_y],
            dst_ref=arrived.at[pl.ds((b - (n_early - n_hubs)) * served, served)],
            send_sem=pass_send, recv_sem=pass_recv,
            device_id=(a, peer, c), device_id_type=MESH,
        )

    def rows_of(count, send, recv):
        rows = arrived.at[pl.ds(0, count)]
        return pltpu.make_async_remote_copy(
            src_ref=rows, dst_ref=rows, send_sem=send, recv_sem=recv, device_id=y_at(1), device_id_type=MESH
        )

    has_corner = jnp.logical_and(with_corner, a == 0)

    @pl.when(is_hub)
    def _():
        blocks = relay.at[pl.ds(0, served - 1)]
        pltpu.make_async_remote_copy(
            src_ref=blocks, dst_ref=blocks, send_sem=block_send.at[0], recv_sem=block_recv,
            device_id=y_at(1), device_id_type=MESH,
        ).wait_recv()
        pl.semaphore_wait(ready, n_late + jnp.where(has_corner, 1, 0))
        for peer in range(n_early, n_y):
            to_late(peer).start()

        @pl.when(has_corner)
        def _():
            to_late(0).start()

    @pl.when(is_first)
    def _():
        rows_of(peers - 1, row_send, row_recv).wait_recv()

    @pl.when(is_late)
    def _():
        rows_of(peers, pass_send, pass_recv).wait_recv()

    @pl.when(is_end)
    def _():
        step["ghost"]()
        for end, start, first_x in ((0, 0, 0), (n_x - 1, 80, 6)):

            @pl.when(a == end)
            def _():
                step["use_ghost"](start)
                step["edge_flux"](first_x)

    @pl.when(is_hub)
    def _():
        for _ in range(n_late * served // peers):
            rows_of(peers, pass_send, pass_recv).wait_send()

        @pl.when(has_corner)
        def _():
            rows_of(served, pass_send, pass_recv).wait_send()

    rows_of(2 * n_early - 2, row_send, row_recv).wait_send()

    @pl.when(jnp.logical_not(is_first))
    def _():
        rows_of(1, row_send, row_recv).wait_send()

    @pl.when(jnp.logical_not(with_corner))
    def _():
        rows_of(1, row_send, row_recv).wait_send()

    for which in range(2):

        @pl.when(jnp.logical_not(own_hub(which)))
        def _():
            to_hub(which).wait_send()

    for copy in halos:
        copy.wait_send()

    @pl.when(has_low)
    def _():
        to_low.wait_send()

    @pl.when(has_high)
    def _():
        to_high.wait_send()


def solution(mesh):
    n_x, n_y, n_z = (mesh.shape[name] for name in ("gx", "gy", "gz"))

    def on_device(fine_state, diffusivity, coarse_cells, copy_sources, copy_targets):
        fields, cells_x, cells_y, cells_z = fine_state.shape
        rows = cells_x * cells_y
        peers = n_x * n_y
        n_hubs, per_hub = hubs_of(n_y)
        sources = jnp.transpose(copy_sources, (0, 1, 4, 2, 3)).reshape(3, 1, peers)
        targets = jnp.transpose(copy_targets, (0, 1, 4, 2, 3)).reshape(3, 1, peers)
        f32 = jnp.float32
        vmem = pltpu.VMEM
        anywhere = pl.BlockSpec(memory_space=pl.ANY)
        result = pl.pallas_call(
            functools.partial(kernel, n_x, n_y, n_z, fields),
            out_shape=jax.ShapeDtypeStruct((fields, rows, cells_z), f32),
            in_specs=[anywhere, pl.BlockSpec(memory_space=pltpu.SMEM), anywhere, anywhere, anywhere],
            out_specs=pl.BlockSpec(memory_space=pltpu.VMEM),
            scratch_shapes=[
                vmem((fields, rows + 32, cells_z), f32),
                vmem((2, fields, 2, 8, 128), f32),
                vmem((fields, 2, 8, 128), f32),
                vmem((fields, 2, 8, 128), f32),
                vmem((fields, 16 * 8 + 16, 128), f32),
                vmem((fields, 8, 128), f32),
                vmem((fields, 8, 128), f32),
                vmem((fields, 8, 128), f32),
                vmem((fields, rows, 128), f32),
                vmem((fields, 128), f32),
                vmem((3, 1, peers), jnp.int32),
                vmem((3, 1, peers), jnp.int32),
                vmem((2, n_y, 1, 128), f32),
                vmem((n_x * per_hub, n_y - n_y // 2 + 1, 1, 128), f32),
                vmem((128, 1, 128), f32),
                vmem((128, 128), f32),
                vmem((384, 512), jnp.bfloat16),
                vmem((8 * SLOT, 128), f32),
                vmem((8, 20, 8, 128), f32),
                pltpu.SemaphoreType.DMA((4,)),
                pltpu.SemaphoreType.DMA((6,)),
                pltpu.SemaphoreType.DMA((6,)),
                pltpu.SemaphoreType.DMA,
                pltpu.SemaphoreType.DMA,
                pltpu.SemaphoreType.DMA((2,)),
                pltpu.SemaphoreType.DMA,
                pltpu.SemaphoreType.DMA,
                pltpu.SemaphoreType.DMA,
                pltpu.SemaphoreType.REGULAR,
            ],
            compiler_params=pltpu.CompilerParams(
                collective_id=0, has_side_effects=True, vmem_limit_bytes=56 * 1024 * 1024
            ),
        )(fine_state.reshape(fields, rows, cells_z), diffusivity, coarse_cells, sources, targets)
        return result.reshape(fine_state.shape)

    return jax.shard_map(
        on_device,
        mesh=mesh,
        in_specs=(
            P(None, "gx", "gy", "gz"),
            P(),
            P(None, ("gx", "gy", "gz")),
            P("gx", "gy", "gz", None, None),
            P("gx", "gy", "gz", None, None),
        ),
        out_specs=P(None, "gx", "gy", "gz"),
        check_vma=False,
    )
```

```python
import functools

import jax
import jax.numpy as jnp
from jax import lax
from jax.experimental import pallas as pl
from jax.experimental.pallas import tpu as pltpu
from jax.sharding import PartitionSpec as P

MESH = pl.DeviceIdType.MESH
time_step = 0.15
SLOT = 16


def hubs_of(n_y):
    n_hubs = max(1, n_y // 4)
    return n_hubs, n_y // n_hubs


def split3(value):
    hi = value.astype(jnp.bfloat16)
    rest = value - hi.astype(jnp.float32)
    mid = rest.astype(jnp.bfloat16)
    low = (rest - mid.astype(jnp.float32)).astype(jnp.bfloat16)
    return jnp.concatenate([hi, mid, low], axis=0)


def face_terms(rho_left, rho_right, mom_left, mom_right):
    inv_left, inv_right = 1.0 / rho_left, 1.0 / rho_right
    velocity = (0.5 * time_step) * (mom_left * inv_left + mom_right * inv_right)
    up, down = jnp.maximum(velocity, 0.0), jnp.minimum(velocity, 0.0)
    quarter_up, quarter_down = 0.25 * up, 0.25 * down
    mean_rho = (0.5 * time_step) * (rho_left + rho_right)
    return (
        up + quarter_down,
        down + quarter_up,
        quarter_up,
        quarter_down,
        mean_rho * inv_left,
        mean_rho * inv_right,
    )


def cell_terms(low, high):
    a_left, a_right, b_left, b_right, e_left, e_right = low
    next_left, next_right, next_b_left, next_b_right, next_e_left, next_e_right = high
    around = (
        -b_left,
        a_left + next_b_left,
        e_left,
        -(b_right + next_right),
        next_e_right,
        next_b_right,
    )
    return around, (a_right - next_left, -(e_right + next_e_left))


def weighted(found, diff, far_low, low, high, far_high):
    w_far_low, w_low, d_low, w_high, d_high, w_far_high = found
    return (
        (w_far_low * far_low + w_far_high * far_high)
        + (w_low + diff * d_low) * low
        + (w_high + diff * d_high) * high
    )


def work(n_x, n_y, fields, diff, out, qx, y_own, y_low, y_high, y_pad, z_own, z_low, z_high, z_rows,
         cells, src, tgt, msg, relay, arrived, order, spread, plane, terms):
    peers = n_x * n_y
    n_hubs, per_hub = hubs_of(n_y)
    lane = lax.broadcasted_iota(jnp.int32, (8, 128), 1)
    line = lax.broadcasted_iota(jnp.int32, (8, 128), 0)
    blank = jnp.full((1, 128 - peers), -1, jnp.int32)

    def pick():
        owned = jnp.concatenate([cells[...], jnp.zeros((SLOT - fields, 128), jnp.float32)], axis=0)
        owned = split3(owned)
        row = lax.broadcasted_iota(jnp.int32, (128, 128), 0)
        picked = []
        for s in range(3):
            wanted = jnp.concatenate([src[s], blank], axis=1)
            chosen = jnp.where(row == wanted, 1.0, 0.0).astype(jnp.bfloat16)
            part = jnp.dot(owned, chosen, preferred_element_type=jnp.float32)
            picked.append(part[:SLOT] + part[SLOT : 2 * SLOT] + part[2 * SLOT :])
        picked.append(jnp.zeros((128 - 3 * SLOT, 128), jnp.float32))
        picked = jnp.concatenate(picked, axis=0).T
        n_early = n_y // 2
        for which, start in enumerate((0, peers - n_y)):
            msg[which, : n_y - n_early] = picked[start + n_early : start + n_y].reshape(n_y - n_early, 1, 128)
            msg[which, n_y - n_early :] = picked[start : start + n_early].reshape(n_early, 1, 128)

    def pack():
        for f in range(fields):
            y_own[0, f, 0] = qx[f, pl.ds(16, 8, stride=8), :]
            y_own[0, f, 1] = qx[f, pl.ds(17, 8, stride=8), :]
            y_own[1, f, 0] = qx[f, pl.ds(22, 8, stride=8), :]
            y_own[1, f, 1] = qx[f, pl.ds(23, 8, stride=8), :]
            packed = pltpu.roll(qx[f, pl.ds(16, 8), :], 2, 1)
            for x in range(1, 8):
                moved = pltpu.roll(qx[f, pl.ds(16 + 8 * x, 8), :], 4 * x + 2, 1)
                packed = jnp.where(lane >= 4 * x, moved, packed)
            z_own[f] = packed

    def pad():
        for f in range(fields):
            for x in range(8):
                y_pad[f, pl.ds(16 * x + 8, 8), :] = tile(f, x)

    def place():
        wide = [jnp.concatenate([tgt[s], blank], axis=1) for s in range(3)]
        wide.append(jnp.full((125, 128), -1, jnp.int32))
        wide = jnp.concatenate(wide, axis=0).astype(jnp.float32).T
        order[...] = jnp.full(order.shape, -1.0, jnp.float32)
        count = n_x * per_hub
        for a in range(n_x):
            for k in range(per_hub):
                start = a * n_y + k * n_hubs
                order[pl.ds(a * per_hub + k, n_hubs, stride=count), :] = wide[start : start + n_hubs]
        half = (lax.broadcasted_iota(jnp.int32, (128, 128), 1) // 2).astype(jnp.float32)
        filled = order[...]
        for s in range(3):
            cell = filled[:, s : s + 1]
            for h in range(4):
                spread[128 * s : 128 * (s + 1), 128 * h : 128 * (h + 1)] = jnp.where(
                    cell - 64.0 * h == half, 1.0, 0.0
                ).astype(jnp.bfloat16)
        if peers < 128:
            arrived[peers:] = jnp.zeros((128 - peers, 1, 128), jnp.float32)

    def tile(f, x):
        return qx[f, pl.ds(16 + 8 * x, 8), :]

    def spread_halos():
        for f in range(fields):
            y_pad[f, pl.ds(6, 8, stride=16), :] = y_low[f, 0]
            y_pad[f, pl.ds(7, 8, stride=16), :] = y_low[f, 1]
            y_pad[f, pl.ds(16, 8, stride=16), :] = y_high[f, 0]
            y_pad[f, pl.ds(17, 8, stride=16), :] = y_high[f, 1]
            kept = jnp.where(lane % 4 < 2, z_low[f], z_high[f])
            for x in range(8):
                z_rows[f, pl.ds(8 * x, 8), :] = pltpu.roll(kept, 126 - 4 * x, 1)

    def y_at(f, x, k):
        return y_pad[f, pl.ds(16 * x + 8 + k, 8), :]

    def x_at(f, x, k):
        return qx[f, pl.ds(8 * (x + k) + 16, 8), :]

    def z_all(f, x, here):
        beyond = z_rows[f, pl.ds(8 * x, 8), :]
        return (
            pltpu.roll(jnp.where(lane >= 126, beyond, here), 2, 1),
            pltpu.roll(jnp.where(lane == 127, beyond, here), 1, 1),
            pltpu.roll(jnp.where(lane == 0, beyond, here), 127, 1),
            pltpu.roll(jnp.where(lane < 2, beyond, here), 126, 1),
        )

    def three(rho, mom):
        low = face_terms(rho[0], rho[1], mom[0], mom[1])
        high = face_terms(rho[1], rho[2], mom[1], mom[2])
        return cell_terms(low, high)

    def x_terms(x):
        return three([x_at(9, x, k) for k in (-1, 0, 1)], [x_at(10, x, k) for k in (-1, 0, 1)])

    def cell_weights():
        for x in range(8):
            found, (centre, d_centre) = three([y_at(9, x, k) for k in (-1, 0, 1)], [y_at(11, x, k) for k in (-1, 0, 1)])
            rho, mom = tile(9, x), tile(12, x)
            _, rho_low, rho_high, _ = z_all(9, x, rho)
            _, mom_low, mom_high, _ = z_all(12, x, mom)
            more, (c, d) = three([rho_low, rho, rho_high], [mom_low, mom, mom_high])
            found, centre, d_centre = found + more, centre + c, d_centre + d
            if 2 <= x < 6:
                more, (c, d) = x_terms(x)
                found, centre, d_centre = found + more, centre + c, d_centre + d
            found = found + (1.0 + centre, d_centre)
            for i, value in enumerate(found):
                terms[x, i] = value

    def main_flux():
        def one_field(g, carry):
            for x in range(8):
                for f in (2 * g, 2 * g + 1):
                    here = tile(f, x)
                    inner = 2 <= x < 6
                    found = [terms[x, i] for i in range(20 if inner else 14)]
                    total = here * (found[-2] + diff[f] * found[-1])
                    total = total + weighted(found[:6], diff[f], *[y_at(f, x, k) for k in (-2, -1, 1, 2)])
                    if inner:
                        total = total + weighted(found[12:18], diff[f], *[x_at(f, x, k) for k in (-2, -1, 1, 2)])
                    total = total + weighted(found[6:12], diff[f], *z_all(f, x, here))
                    out[f, pl.ds(8 * x, 8), :] = total
            return carry

        lax.fori_loop(0, fields // 2, one_field, 0)

    def edge_flux(first_x):
        kept = []
        for x in (first_x, first_x + 1):
            found, centre = x_terms(x)
            kept.append(found + centre)
        for f in range(fields):
            for x, found in zip((first_x, first_x + 1), kept):
                rows = pl.ds(8 * x, 8)
                total = tile(f, x) * (found[-2] + diff[f] * found[-1])
                total = total + weighted(found[:6], diff[f], *[x_at(f, x, k) for k in (-2, -1, 1, 2)])
                out[f, rows, :] = out[f, rows, :] + total

    def ghost():
        by_slot = arrived[...].reshape(128, 128).T
        by_slot = jnp.concatenate([by_slot[SLOT * s : SLOT * (s + 1)] for s in range(3)], axis=1)
        face = jnp.dot(split3(by_slot), spread[...], preferred_element_type=jnp.float32)
        face = face[:SLOT] + face[SLOT : 2 * SLOT] + face[2 * SLOT :]
        for y in range(8):
            h = y // 2
            plane[SLOT * y : SLOT * (y + 1), :] = face[:, 128 * h : 128 * (h + 1)]

    def use_ghost(start):
        for f in range(fields):
            cover = plane[pl.ds(f, 8, stride=SLOT), :]
            qx[f, pl.ds(start, 8), :] = cover
            qx[f, pl.ds(start + 8, 8), :] = cover

    return dict(
        pick=pick, pack=pack, pad=pad, place=place, spread_halos=spread_halos, cell_weights=cell_weights,
        main_flux=main_flux, ghost=ghost, use_ghost=use_ghost, edge_flux=edge_flux,
    )


def kernel(
    n_x, n_y, n_z, fields,
    fine, diff, coarse, sources, targets,
    out,
    qx, y_own, y_low, y_high, y_pad, z_own, z_low, z_high, z_rows,
    cells, src, tgt, msg, relay, arrived, order, spread, plane, terms,
    load_sem, halo_send, halo_recv, row_send, row_recv, block_send, block_recv, pass_send, pass_recv, ready, open_sem,
):
    a, b, c = lax.axis_index("gx"), lax.axis_index("gy"), lax.axis_index("gz")
    is_end = jnp.logical_or(a == 0, a == n_x - 1)
    peers = n_x * n_y
    n_hubs, per_hub = hubs_of(n_y)
    served = n_x * per_hub
    step = work(
        n_x, n_y, fields, diff, out, qx, y_own, y_low, y_high, y_pad, z_own, z_low, z_high, z_rows,
        cells, src, tgt, msg, relay, arrived, order, spread, plane, terms,
    )

    n_early = n_y // 2
    ends = (0, n_x - 1)
    corner = jnp.logical_and(jnp.logical_and(a == 0, b == 0), c == 0)
    is_first = jnp.logical_and(jnp.logical_and(is_end, b < n_early), jnp.logical_not(corner))
    is_hub = jnp.logical_and(jnp.logical_and(is_end, b < n_early), b >= n_early - n_hubs)
    is_late = jnp.logical_and(is_end, jnp.logical_not(is_first))
    with_corner = c == 0
    n_late = n_y - n_early
    row = lax.rem(b, n_hubs) * served + a * per_hub + lax.div(b, n_hubs)

    def x_at(k):
        return (lax.rem(a + (k + n_x), n_x), b, c)

    def y_at(k):
        return (a, lax.rem(b + (k + n_y), n_y), c)

    def z_at(k):
        return (a, b, lax.rem(c + (k + n_z), n_z))

    load_cells = pltpu.make_async_copy(coarse, cells, load_sem.at[0])
    load_src = pltpu.make_async_copy(sources, src, load_sem.at[1])
    load_fine = pltpu.make_async_copy(fine, qx.at[:, pl.ds(16, 64)], load_sem.at[2])
    load_tgt = pltpu.make_async_copy(targets, tgt, load_sem.at[3])
    load_cells.start()
    load_src.start()
    load_fine.start()
    load_tgt.start()

    barrier = pltpu.get_barrier_semaphore()

    def greet(device):
        pl.semaphore_signal(barrier, inc=1, device_id=device, device_id_type=MESH)

    has_low, has_high = a > 0, a < n_x - 1
    y_later = (b < n_y - 1, b == 0)
    z_later = (c < n_z // 2, jnp.logical_or(c == 0, c > n_z // 2))
    neighbours = [
        (y_at(1), y_later[0], jnp.logical_not(y_later[0]), 1),
        (y_at(-1), y_later[1], jnp.logical_not(y_later[1]), 0),
        (z_at(1), z_later[0], jnp.logical_not(z_later[0]), 3),
        (z_at(-1), z_later[1], jnp.logical_not(z_later[1]), 2),
        (x_at(1), has_high, False, 5),
        (x_at(-1), False, has_low, 4),
    ]
    n_earlier = 0
    for device, later, earlier, _ in neighbours:
        if later is not False:
            pl.when(later)(functools.partial(greet, device))
        if earlier is not False:
            n_earlier = n_earlier + jnp.where(earlier, 1, 0)

    @pl.when(is_first)
    def _():
        for k in range(n_x):
            for peer in range(n_y):

                @pl.when(jnp.logical_or(a != k, b != peer))
                def _():
                    greet((k, peer, c))

    load_cells.wait()
    load_src.wait()
    step["pick"]()
    pl.semaphore_wait(barrier, n_earlier + 2 * n_early - jnp.where(with_corner, 1, 0) - jnp.where(is_first, 1, 0))

    def tell(device, number):
        pl.semaphore_signal(open_sem.at[number], inc=1, device_id=device, device_id_type=MESH)

    for device, _, earlier, number in neighbours:
        if earlier is not False:
            pl.when(earlier)(functools.partial(tell, device, number))

    def to_first(which, peer):
        return pltpu.make_async_remote_copy(
            src_ref=msg.at[which, pl.ds(n_late + peer, 1)], dst_ref=arrived.at[pl.ds(row, 1)],
            send_sem=row_send, recv_sem=row_recv,
            device_id=(ends[which], peer, c), device_id_type=MESH,
        )

    def to_hub(which):
        slot = a * per_hub + lax.div(b, n_hubs)
        return pltpu.make_async_remote_copy(
            src_ref=msg.at[which, pl.ds(0, n_late + 1)], dst_ref=relay.at[slot],
            send_sem=block_send.at[which], recv_sem=block_recv,
            device_id=(ends[which], n_early - n_hubs + lax.rem(b, n_hubs), c), device_id_type=MESH,
        )

    for peer in range(n_early):
        for which in range(2):
            itself = jnp.logical_and(a == ends[which], b == peer)
            meant = jnp.logical_not(itself)
            if peer == 0 and which == 0:
                meant = jnp.logical_and(meant, jnp.logical_not(with_corner))
                itself = jnp.logical_and(itself, jnp.logical_not(with_corner))

            @pl.when(meant)
            def _():
                to_first(which, peer).start()

            @pl.when(itself)
            def _():
                arrived[pl.ds(row, 1)] = msg[which, pl.ds(n_late + peer, 1)]

    def own_hub(which):
        return jnp.logical_and(a == ends[which], b == n_early - n_hubs + lax.rem(b, n_hubs))

    for which in range(2):

        @pl.when(jnp.logical_not(own_hub(which)))
        def _():
            to_hub(which).start()

        @pl.when(own_hub(which))
        def _():
            relay[a * per_hub + lax.div(b, n_hubs)] = msg[which, pl.ds(0, n_late + 1)]

    @pl.when(is_late)
    def _():
        for h in range(n_hubs):
            pl.semaphore_signal(ready, inc=1, device_id=(a, n_early - n_hubs + h, c), device_id_type=MESH)

    def halo(i, source, target, device):
        return pltpu.make_async_remote_copy(
            src_ref=source, dst_ref=target, send_sem=halo_send.at[i], recv_sem=halo_recv.at[i],
            device_id=device, device_id_type=MESH,
        )

    load_fine.wait()
    step["pack"]()
    halos = [
        halo(0, y_own.at[1], y_low, y_at(1)),
        halo(1, y_own.at[0], y_high, y_at(-1)),
        halo(2, z_own, z_low, z_at(1)),
        halo(3, z_own, z_high, z_at(-1)),
        halo(4, qx.at[:, pl.ds(64, 16)], qx.at[:, pl.ds(0, 16)], x_at(1)),
        halo(5, qx.at[:, pl.ds(16, 16)], qx.at[:, pl.ds(80, 16)], x_at(-1)),
    ]
    to_high, to_low = halos[4:]

    def send_later(i):
        pl.semaphore_wait(open_sem.at[i], 1)
        halos[i].start()

    for i, (_, _, earlier, _) in enumerate(neighbours):
        if earlier is not False:
            pl.when(earlier)(halos[i].start)
    for i in (5, 4, 3, 2, 0, 1):
        later = neighbours[i][1]
        if later is not False:
            pl.when(later)(functools.partial(send_later, i))
    halos = halos[:4]
    load_tgt.wait()

    @pl.when(is_end)
    def _():
        step["place"]()

    step["pad"]()
    for copy in halos:
        copy.wait_recv()
    step["spread_halos"]()
    step["cell_weights"]()
    step["main_flux"]()

    @pl.when(has_high)
    def _():
        to_low.wait_recv()
        step["edge_flux"](6)

    @pl.when(has_low)
    def _():
        to_high.wait_recv()
        step["edge_flux"](0)

    def to_late(peer):
        return pltpu.make_async_remote_copy(
            src_ref=relay.at[:, (peer - n_early) % n_y],
            dst_ref=arrived.at[pl.ds((b - (n_early - n_hubs)) * served, served)],
            send_sem=pass_send, recv_sem=pass_recv,
            device_id=(a, peer, c), device_id_type=MESH,
        )

    def rows_of(count, send, recv):
        rows = arrived.at[pl.ds(0, count)]
        return pltpu.make_async_remote_copy(
            src_ref=rows, dst_ref=rows, send_sem=send, recv_sem=recv, device_id=y_at(1), device_id_type=MESH
        )

    has_corner = jnp.logical_and(with_corner, a == 0)

    @pl.when(is_hub)
    def _():
        blocks = relay.at[pl.ds(0, served - 1)]
        pltpu.make_async_remote_copy(
            src_ref=blocks, dst_ref=blocks, send_sem=block_send.at[0], recv_sem=block_recv,
            device_id=y_at(1), device_id_type=MESH,
        ).wait_recv()
        pl.semaphore_wait(ready, n_late + jnp.where(has_corner, 1, 0))
        for peer in range(n_early, n_y):
            to_late(peer).start()

        @pl.when(has_corner)
        def _():
            to_late(0).start()

    @pl.when(is_first)
    def _():
        rows_of(peers - 1, row_send, row_recv).wait_recv()

    @pl.when(is_late)
    def _():
        rows_of(peers, pass_send, pass_recv).wait_recv()

    @pl.when(is_end)
    def _():
        step["ghost"]()
        for end, start, first_x in ((0, 0, 0), (n_x - 1, 80, 6)):

            @pl.when(a == end)
            def _():
                step["use_ghost"](start)
                step["edge_flux"](first_x)

    @pl.when(is_hub)
    def _():
        for _ in range(n_late * served // peers):
            rows_of(peers, pass_send, pass_recv).wait_send()

        @pl.when(has_corner)
        def _():
            rows_of(served, pass_send, pass_recv).wait_send()

    rows_of(2 * n_early - 2, row_send, row_recv).wait_send()

    @pl.when(jnp.logical_not(is_first))
    def _():
        rows_of(1, row_send, row_recv).wait_send()

    @pl.when(jnp.logical_not(with_corner))
    def _():
        rows_of(1, row_send, row_recv).wait_send()

    for which in range(2):

        @pl.when(jnp.logical_not(own_hub(which)))
        def _():
            to_hub(which).wait_send()

    for copy in halos:
        copy.wait_send()

    @pl.when(has_low)
    def _():
        to_low.wait_send()

    @pl.when(has_high)
    def _():
        to_high.wait_send()


def solution(mesh):
    n_x, n_y, n_z = (mesh.shape[name] for name in ("gx", "gy", "gz"))

    def on_device(fine_state, diffusivity, coarse_cells, copy_sources, copy_targets):
        fields, cells_x, cells_y, cells_z = fine_state.shape
        rows = cells_x * cells_y
        peers = n_x * n_y
        n_hubs, per_hub = hubs_of(n_y)
        sources = jnp.transpose(copy_sources, (0, 1, 4, 2, 3)).reshape(3, 1, peers)
        targets = jnp.transpose(copy_targets, (0, 1, 4, 2, 3)).reshape(3, 1, peers)
        f32 = jnp.float32
        vmem = pltpu.VMEM
        anywhere = pl.BlockSpec(memory_space=pl.ANY)
        result = pl.pallas_call(
            functools.partial(kernel, n_x, n_y, n_z, fields),
            out_shape=pltpu.VMEM((fields, rows, cells_z), f32),
            in_specs=[anywhere, pl.BlockSpec(memory_space=pltpu.SMEM), anywhere, anywhere, anywhere],
            out_specs=pl.BlockSpec(memory_space=pltpu.VMEM),
            scratch_shapes=[
                vmem((fields, rows + 32, cells_z), f32),
                vmem((2, fields, 2, 8, 128), f32),
                vmem((fields, 2, 8, 128), f32),
                vmem((fields, 2, 8, 128), f32),
                vmem((fields, 16 * 8 + 16, 128), f32),
                vmem((fields, 8, 128), f32),
                vmem((fields, 8, 128), f32),
                vmem((fields, 8, 128), f32),
                vmem((fields, rows, 128), f32),
                vmem((fields, 128), f32),
                vmem((3, 1, peers), jnp.int32),
                vmem((3, 1, peers), jnp.int32),
                vmem((2, n_y, 1, 128), f32),
                vmem((n_x * per_hub, n_y - n_y // 2 + 1, 1, 128), f32),
                vmem((128, 1, 128), f32),
                vmem((128, 128), f32),
                vmem((384, 512), jnp.bfloat16),
                vmem((8 * SLOT, 128), f32),
                vmem((8, 20, 8, 128), f32),
                pltpu.SemaphoreType.DMA((4,)),
                pltpu.SemaphoreType.DMA((6,)),
                pltpu.SemaphoreType.DMA((6,)),
                pltpu.SemaphoreType.DMA,
                pltpu.SemaphoreType.DMA,
                pltpu.SemaphoreType.DMA((2,)),
                pltpu.SemaphoreType.DMA,
                pltpu.SemaphoreType.DMA,
                pltpu.SemaphoreType.DMA,
                pltpu.SemaphoreType.REGULAR,
                pltpu.SemaphoreType.REGULAR((6,)),
            ],
            compiler_params=pltpu.CompilerParams(
                collective_id=0, has_side_effects=True, vmem_limit_bytes=56 * 1024 * 1024
            ),
        )(fine_state.reshape(fields, rows, cells_z), diffusivity, coarse_cells, sources, targets)
        return result.reshape(fine_state.shape)

    return jax.shard_map(
        on_device,
        mesh=mesh,
        in_specs=(
            P(None, "gx", "gy", "gz"),
            P(),
            P(None, ("gx", "gy", "gz")),
            P("gx", "gy", "gz", None, None),
            P("gx", "gy", "gz", None, None),
        ),
        out_specs=P(None, "gx", "gy", "gz"),
        check_vma=False,
    )
```

```python
import functools

import jax
import jax.numpy as jnp
from jax import lax
from jax.experimental import pallas as pl
from jax.experimental.pallas import tpu as pltpu
from jax.sharding import PartitionSpec as P

MESH = pl.DeviceIdType.MESH
time_step = 0.15
SLOT = 16


def hubs_of(n_y):
    n_hubs = max(1, n_y // 4)
    return n_hubs, n_y // n_hubs


def early_of(n_y):
    return max(2, 5 * n_y // 12)


def split3(value):
    hi = value.astype(jnp.bfloat16)
    rest = value - hi.astype(jnp.float32)
    mid = rest.astype(jnp.bfloat16)
    low = (rest - mid.astype(jnp.float32)).astype(jnp.bfloat16)
    return jnp.concatenate([hi, mid, low], axis=0)


def face_terms(rho_left, rho_right, mom_left, mom_right):
    inv_left, inv_right = 1.0 / rho_left, 1.0 / rho_right
    velocity = (0.5 * time_step) * (mom_left * inv_left + mom_right * inv_right)
    up, down = jnp.maximum(velocity, 0.0), jnp.minimum(velocity, 0.0)
    quarter_up, quarter_down = 0.25 * up, 0.25 * down
    mean_rho = (0.5 * time_step) * (rho_left + rho_right)
    return (
        up + quarter_down,
        down + quarter_up,
        quarter_up,
        quarter_down,
        mean_rho * inv_left,
        mean_rho * inv_right,
    )


def cell_terms(low, high):
    a_left, a_right, b_left, b_right, e_left, e_right = low
    next_left, next_right, next_b_left, next_b_right, next_e_left, next_e_right = high
    around = (
        -b_left,
        a_left + next_b_left,
        e_left,
        -(b_right + next_right),
        next_e_right,
        next_b_right,
    )
    return around, (a_right - next_left, -(e_right + next_e_left))


def weighted(found, diff, far_low, low, high, far_high):
    w_far_low, w_low, d_low, w_high, d_high, w_far_high = found
    return (
        (w_far_low * far_low + w_far_high * far_high)
        + (w_low + diff * d_low) * low
        + (w_high + diff * d_high) * high
    )


def work(n_x, n_y, fields, diff, out, qx, y_own, y_low, y_high, y_pad, z_own, z_low, z_high, z_rows,
         cells, src, tgt, msg, relay, arrived, order, spread, plane, terms):
    peers = n_x * n_y
    n_hubs, per_hub = hubs_of(n_y)
    lane = lax.broadcasted_iota(jnp.int32, (8, 128), 1)
    line = lax.broadcasted_iota(jnp.int32, (8, 128), 0)
    blank = jnp.full((1, 128 - peers), -1, jnp.int32)

    def pick():
        owned = jnp.concatenate([cells[...], jnp.zeros((SLOT - fields, 128), jnp.float32)], axis=0)
        owned = split3(owned)
        row = lax.broadcasted_iota(jnp.int32, (128, 128), 0)
        picked = []
        for s in range(3):
            wanted = jnp.concatenate([src[s], blank], axis=1)
            chosen = jnp.where(row == wanted, 1.0, 0.0).astype(jnp.bfloat16)
            part = jnp.dot(owned, chosen, preferred_element_type=jnp.float32)
            picked.append(part[:SLOT] + part[SLOT : 2 * SLOT] + part[2 * SLOT :])
        picked.append(jnp.zeros((128 - 3 * SLOT, 128), jnp.float32))
        picked = jnp.concatenate(picked, axis=0).T
        n_early = early_of(n_y)
        for which, start in enumerate((0, peers - n_y)):
            msg[which, : n_y - n_early] = picked[start + n_early : start + n_y].reshape(n_y - n_early, 1, 128)
            msg[which, n_y - n_early :] = picked[start : start + n_early].reshape(n_early, 1, 128)

    def pack():
        for f in range(fields):
            y_own[0, f, 0] = qx[f, pl.ds(16, 8, stride=8), :]
            y_own[0, f, 1] = qx[f, pl.ds(17, 8, stride=8), :]
            y_own[1, f, 0] = qx[f, pl.ds(22, 8, stride=8), :]
            y_own[1, f, 1] = qx[f, pl.ds(23, 8, stride=8), :]
            packed = pltpu.roll(qx[f, pl.ds(16, 8), :], 2, 1)
            for x in range(1, 8):
                moved = pltpu.roll(qx[f, pl.ds(16 + 8 * x, 8), :], 4 * x + 2, 1)
                packed = jnp.where(lane >= 4 * x, moved, packed)
            z_own[f] = packed

    def pad():
        for f in range(fields):
            for x in range(8):
                y_pad[f, pl.ds(16 * x + 8, 8), :] = tile(f, x)

    def place():
        wide = [jnp.concatenate([tgt[s], blank], axis=1) for s in range(3)]
        wide.append(jnp.full((125, 128), -1, jnp.int32))
        wide = jnp.concatenate(wide, axis=0).astype(jnp.float32).T
        order[...] = jnp.full(order.shape, -1.0, jnp.float32)
        count = n_x * per_hub
        for a in range(n_x):
            for k in range(per_hub):
                start = a * n_y + k * n_hubs
                order[pl.ds(a * per_hub + k, n_hubs, stride=count), :] = wide[start : start + n_hubs]
        half = (lax.broadcasted_iota(jnp.int32, (128, 128), 1) // 2).astype(jnp.float32)
        filled = order[...]
        for s in range(3):
            cell = filled[:, s : s + 1]
            for h in range(4):
                spread[128 * s : 128 * (s + 1), 128 * h : 128 * (h + 1)] = jnp.where(
                    cell - 64.0 * h == half, 1.0, 0.0
                ).astype(jnp.bfloat16)
        if peers < 128:
            arrived[peers:] = jnp.zeros((128 - peers, 1, 128), jnp.float32)

    def tile(f, x):
        return qx[f, pl.ds(16 + 8 * x, 8), :]

    def spread_z():
        for f in range(fields):
            kept = jnp.where(lane % 4 < 2, z_low[f], z_high[f])
            for x in range(8):
                z_rows[f, pl.ds(8 * x, 8), :] = pltpu.roll(kept, 126 - 4 * x, 1)

    def spread_y():
        for f in range(fields):
            y_pad[f, pl.ds(6, 8, stride=16), :] = y_low[f, 0]
            y_pad[f, pl.ds(7, 8, stride=16), :] = y_low[f, 1]
            y_pad[f, pl.ds(16, 8, stride=16), :] = y_high[f, 0]
            y_pad[f, pl.ds(17, 8, stride=16), :] = y_high[f, 1]

    def y_at(f, x, k):
        return y_pad[f, pl.ds(16 * x + 8 + k, 8), :]

    def x_at(f, x, k):
        return qx[f, pl.ds(8 * (x + k) + 16, 8), :]

    def z_all(f, x, here):
        beyond = z_rows[f, pl.ds(8 * x, 8), :]
        return (
            pltpu.roll(jnp.where(lane >= 126, beyond, here), 2, 1),
            pltpu.roll(jnp.where(lane == 127, beyond, here), 1, 1),
            pltpu.roll(jnp.where(lane == 0, beyond, here), 127, 1),
            pltpu.roll(jnp.where(lane < 2, beyond, here), 126, 1),
        )

    def three(rho, mom):
        low = face_terms(rho[0], rho[1], mom[0], mom[1])
        high = face_terms(rho[1], rho[2], mom[1], mom[2])
        return cell_terms(low, high)

    def x_terms(x):
        return three([x_at(9, x, k) for k in (-1, 0, 1)], [x_at(10, x, k) for k in (-1, 0, 1)])

    def store_terms(x, first, found):
        for i, value in enumerate(found):
            terms[x, first + i] = value

    def weights_zx():
        for x in range(8):
            rho, mom = tile(9, x), tile(12, x)
            _, rho_low, rho_high, _ = z_all(9, x, rho)
            _, mom_low, mom_high, _ = z_all(12, x, mom)
            found, (centre, d_centre) = three([rho_low, rho, rho_high], [mom_low, mom, mom_high])
            if 2 <= x < 6:
                more, (c, d) = x_terms(x)
                found, centre, d_centre = found + more, centre + c, d_centre + d
            store_terms(x, 0, found + (1.0 + centre, d_centre))

    def weights_y():
        for x in range(8):
            found, centre = three([y_at(9, x, k) for k in (-1, 0, 1)], [y_at(11, x, k) for k in (-1, 0, 1)])
            store_terms(x, 14, found + centre)

    def flux_zx():
        def two_fields(g, carry):
            for x in range(8):
                for f in (2 * g, 2 * g + 1):
                    here = tile(f, x)
                    inner = 2 <= x < 6
                    found = [terms[x, i] for i in range(14 if inner else 8)]
                    total = here * (found[-2] + diff[f] * found[-1])
                    if inner:
                        total = total + weighted(found[6:12], diff[f], *[x_at(f, x, k) for k in (-2, -1, 1, 2)])
                    out[f, pl.ds(8 * x, 8), :] = total + weighted(found[:6], diff[f], *z_all(f, x, here))
            return carry

        lax.fori_loop(0, fields // 2, two_fields, 0)

    def flux_y():
        def two_fields(g, carry):
            for x in range(8):
                for f in (2 * g, 2 * g + 1):
                    rows = pl.ds(8 * x, 8)
                    found = [terms[x, 14 + i] for i in range(8)]
                    total = tile(f, x) * (found[6] + diff[f] * found[7])
                    total = total + weighted(found[:6], diff[f], *[y_at(f, x, k) for k in (-2, -1, 1, 2)])
                    out[f, rows, :] = out[f, rows, :] + total
            return carry

        lax.fori_loop(0, fields // 2, two_fields, 0)

    def edge_flux(first_x):
        kept = []
        for x in (first_x, first_x + 1):
            found, centre = x_terms(x)
            kept.append(found + centre)
        for f in range(fields):
            for x, found in zip((first_x, first_x + 1), kept):
                rows = pl.ds(8 * x, 8)
                total = tile(f, x) * (found[-2] + diff[f] * found[-1])
                total = total + weighted(found[:6], diff[f], *[x_at(f, x, k) for k in (-2, -1, 1, 2)])
                out[f, rows, :] = out[f, rows, :] + total

    def ghost():
        by_slot = arrived[...].reshape(128, 128).T
        by_slot = jnp.concatenate([by_slot[SLOT * s : SLOT * (s + 1)] for s in range(3)], axis=1)
        face = jnp.dot(split3(by_slot), spread[...], preferred_element_type=jnp.float32)
        face = face[:SLOT] + face[SLOT : 2 * SLOT] + face[2 * SLOT :]
        for y in range(8):
            h = y // 2
            plane[SLOT * y : SLOT * (y + 1), :] = face[:, 128 * h : 128 * (h + 1)]

    def use_ghost(start):
        for f in range(fields):
            cover = plane[pl.ds(f, 8, stride=SLOT), :]
            qx[f, pl.ds(start, 8), :] = cover
            qx[f, pl.ds(start + 8, 8), :] = cover

    return dict(
        pick=pick, pack=pack, pad=pad, place=place, spread_z=spread_z, spread_y=spread_y, weights_zx=weights_zx,
        weights_y=weights_y, flux_zx=flux_zx, flux_y=flux_y, ghost=ghost, use_ghost=use_ghost, edge_flux=edge_flux,
    )


def kernel(
    n_x, n_y, n_z, fields,
    fine, diffusivity, coarse, sources, targets,
    out,
    qx, y_own, y_low, y_high, y_pad, z_own, z_low, z_high, z_rows,
    cells, src, tgt, msg, relay, arrived, order, spread, plane, terms,
    diff, load_sem, halo_send, halo_recv, row_send, row_recv, block_send, block_recv, pass_send, pass_recv, ready, open_sem,
):
    a, b, c = lax.axis_index("gx"), lax.axis_index("gy"), lax.axis_index("gz")
    is_end = jnp.logical_or(a == 0, a == n_x - 1)
    peers = n_x * n_y
    n_hubs, per_hub = hubs_of(n_y)
    served = n_x * per_hub
    step = work(
        n_x, n_y, fields, diff, out, qx, y_own, y_low, y_high, y_pad, z_own, z_low, z_high, z_rows,
        cells, src, tgt, msg, relay, arrived, order, spread, plane, terms,
    )

    n_early = early_of(n_y)
    ends = (0, n_x - 1)
    corner = jnp.logical_and(jnp.logical_and(a == 0, b == 0), c == 0)
    is_first = jnp.logical_and(jnp.logical_and(is_end, b < n_early), jnp.logical_not(corner))
    is_hub = jnp.logical_and(jnp.logical_and(is_end, b < n_early), b >= n_early - n_hubs)
    is_late = jnp.logical_and(is_end, jnp.logical_not(is_first))
    with_corner = c == 0
    n_late = n_y - n_early
    first_hub = n_early - n_hubs
    hub_y = first_hub + lax.rem(b + (n_y * n_hubs - first_hub), n_hubs)
    row = lax.rem(b, n_hubs) * served + a * per_hub + lax.div(b, n_hubs)

    def x_at(k):
        return (lax.rem(a + (k + n_x), n_x), b, c)

    def y_at(k):
        return (a, lax.rem(b + (k + n_y), n_y), c)

    def z_at(k):
        return (a, b, lax.rem(c + (k + n_z), n_z))

    load_cells = pltpu.make_async_copy(coarse, cells, load_sem.at[0])
    load_src = pltpu.make_async_copy(sources, src, load_sem.at[1])
    load_fine = pltpu.make_async_copy(fine, qx.at[:, pl.ds(16, 64)], load_sem.at[2])
    load_tgt = pltpu.make_async_copy(targets, tgt, load_sem.at[3])
    load_cells.start()
    load_src.start()
    load_fine.start()
    load_tgt.start()
    load_diff = pltpu.make_async_copy(diffusivity, diff, load_sem.at[4])
    load_diff.start()

    barrier = pltpu.get_barrier_semaphore()

    def greet(device):
        pl.semaphore_signal(barrier, inc=1, device_id=device, device_id_type=MESH)

    has_low, has_high = a > 0, a < n_x - 1
    y_later = (b < n_y - 1, b == 0)
    z_later = (c < n_z // 2, jnp.logical_or(c == 0, c > n_z // 2))
    neighbours = [
        (y_at(1), y_later[0], jnp.logical_not(y_later[0]), 1),
        (y_at(-1), y_later[1], jnp.logical_not(y_later[1]), 0),
        (z_at(1), z_later[0], jnp.logical_not(z_later[0]), 3),
        (z_at(-1), z_later[1], jnp.logical_not(z_later[1]), 2),
        (x_at(1), has_high, False, 5),
        (x_at(-1), False, has_low, 4),
    ]
    n_earlier = 0
    for device, later, earlier, _ in neighbours:
        if later is not False:
            pl.when(later)(functools.partial(greet, device))
        if earlier is not False:
            n_earlier = n_earlier + jnp.where(earlier, 1, 0)

    @pl.when(is_first)
    def _():
        for k in range(n_x):
            for peer in range(n_y):

                @pl.when(jnp.logical_or(a != k, b != peer))
                def _():
                    greet((k, peer, c))

    load_cells.wait()
    load_src.wait()
    step["pick"]()
    pl.semaphore_wait(barrier, n_earlier + 2 * n_early - jnp.where(with_corner, 1, 0) - jnp.where(is_first, 1, 0))

    def tell(device, number):
        pl.semaphore_signal(open_sem.at[number], inc=1, device_id=device, device_id_type=MESH)

    for device, _, earlier, number in neighbours:
        if earlier is not False:
            pl.when(earlier)(functools.partial(tell, device, number))

    def to_first(which, peer):
        return pltpu.make_async_remote_copy(
            src_ref=msg.at[which, pl.ds(n_late + peer, 1)], dst_ref=arrived.at[pl.ds(row, 1)],
            send_sem=row_send, recv_sem=row_recv,
            device_id=(ends[which], peer, c), device_id_type=MESH,
        )

    def to_hub(which):
        slot = a * per_hub + lax.div(b, n_hubs)
        return pltpu.make_async_remote_copy(
            src_ref=msg.at[which, pl.ds(0, n_late + 1)], dst_ref=relay.at[slot],
            send_sem=block_send.at[which], recv_sem=block_recv,
            device_id=(ends[which], hub_y, c), device_id_type=MESH,
        )

    for peer in range(n_early):
        for which in range(2):
            itself = jnp.logical_and(a == ends[which], b == peer)
            meant = jnp.logical_not(itself)
            if peer == 0 and which == 0:
                meant = jnp.logical_and(meant, jnp.logical_not(with_corner))
                itself = jnp.logical_and(itself, jnp.logical_not(with_corner))

            @pl.when(meant)
            def _():
                to_first(which, peer).start()

            @pl.when(itself)
            def _():
                arrived[pl.ds(row, 1)] = msg[which, pl.ds(n_late + peer, 1)]

    def own_hub(which):
        return jnp.logical_and(a == ends[which], b == hub_y)

    for which in range(2):

        @pl.when(jnp.logical_not(own_hub(which)))
        def _():
            to_hub(which).start()

        @pl.when(own_hub(which))
        def _():
            relay[a * per_hub + lax.div(b, n_hubs)] = msg[which, pl.ds(0, n_late + 1)]

    @pl.when(is_late)
    def _():
        for h in range(n_hubs):
            pl.semaphore_signal(ready, inc=1, device_id=(a, first_hub + h, c), device_id_type=MESH)

    def halo(i, source, target, device):
        return pltpu.make_async_remote_copy(
            src_ref=source, dst_ref=target, send_sem=halo_send.at[i], recv_sem=halo_recv.at[i],
            device_id=device, device_id_type=MESH,
        )

    load_fine.wait()
    step["pack"]()
    halos = [
        halo(0, y_own.at[1], y_low, y_at(1)),
        halo(1, y_own.at[0], y_high, y_at(-1)),
        halo(2, z_own, z_low, z_at(1)),
        halo(3, z_own, z_high, z_at(-1)),
        halo(4, qx.at[:, pl.ds(64, 16)], qx.at[:, pl.ds(0, 16)], x_at(1)),
        halo(5, qx.at[:, pl.ds(16, 16)], qx.at[:, pl.ds(80, 16)], x_at(-1)),
    ]
    to_high, to_low = halos[4:]

    def send_later(i):
        pl.semaphore_wait(open_sem.at[i], 1)
        halos[i].start()

    for i, (_, _, earlier, _) in enumerate(neighbours):
        if earlier is not False:
            pl.when(earlier)(halos[i].start)
    for i in (5, 4, 3, 2, 0, 1):
        later = neighbours[i][1]
        if later is not False:
            pl.when(later)(functools.partial(send_later, i))
    halos = halos[:4]
    load_tgt.wait()
    load_diff.wait()

    @pl.when(is_end)
    def _():
        step["place"]()

    step["pad"]()
    for copy in halos[2:]:
        copy.wait_recv()
    step["spread_z"]()
    step["weights_zx"]()
    step["flux_zx"]()

    @pl.when(has_high)
    def _():
        to_low.wait_recv()
        step["edge_flux"](6)

    @pl.when(has_low)
    def _():
        to_high.wait_recv()
        step["edge_flux"](0)

    for copy in halos[:2]:
        copy.wait_recv()
    step["spread_y"]()
    step["weights_y"]()
    step["flux_y"]()

    def to_late(peer):
        return pltpu.make_async_remote_copy(
            src_ref=relay.at[:, (peer - n_early) % n_y],
            dst_ref=arrived.at[pl.ds(lax.rem(b, n_hubs) * served, served)],
            send_sem=pass_send, recv_sem=pass_recv,
            device_id=(a, peer, c), device_id_type=MESH,
        )

    def rows_of(count, send, recv):
        rows = arrived.at[pl.ds(0, count)]
        return pltpu.make_async_remote_copy(
            src_ref=rows, dst_ref=rows, send_sem=send, recv_sem=recv, device_id=y_at(1), device_id_type=MESH
        )

    has_corner = jnp.logical_and(with_corner, a == 0)

    @pl.when(is_hub)
    def _():
        blocks = relay.at[pl.ds(0, served - 1)]
        pltpu.make_async_remote_copy(
            src_ref=blocks, dst_ref=blocks, send_sem=block_send.at[0], recv_sem=block_recv,
            device_id=y_at(1), device_id_type=MESH,
        ).wait_recv()
        pl.semaphore_wait(ready, n_late + jnp.where(has_corner, 1, 0))
        for peer in range(n_early, n_y):
            to_late(peer).start()

        @pl.when(has_corner)
        def _():
            to_late(0).start()

    @pl.when(is_first)
    def _():
        rows_of(peers - 1, row_send, row_recv).wait_recv()

    @pl.when(is_late)
    def _():
        rows_of(peers, pass_send, pass_recv).wait_recv()

    @pl.when(is_end)
    def _():
        step["ghost"]()
        for end, start, first_x in ((0, 0, 0), (n_x - 1, 80, 6)):

            @pl.when(a == end)
            def _():
                step["use_ghost"](start)
                step["edge_flux"](first_x)

    @pl.when(is_hub)
    def _():
        for _ in range(n_late):
            rows_of(served, pass_send, pass_recv).wait_send()

        @pl.when(has_corner)
        def _():
            rows_of(served, pass_send, pass_recv).wait_send()

    rows_of(2 * n_early - 2, row_send, row_recv).wait_send()

    @pl.when(jnp.logical_not(is_first))
    def _():
        rows_of(1, row_send, row_recv).wait_send()

    @pl.when(jnp.logical_not(with_corner))
    def _():
        rows_of(1, row_send, row_recv).wait_send()

    for which in range(2):

        @pl.when(jnp.logical_not(own_hub(which)))
        def _():
            to_hub(which).wait_send()

    for copy in halos:
        copy.wait_send()

    @pl.when(has_low)
    def _():
        to_low.wait_send()

    @pl.when(has_high)
    def _():
        to_high.wait_send()


def solution(mesh):
    n_x, n_y, n_z = (mesh.shape[name] for name in ("gx", "gy", "gz"))

    def on_device(fine_state, diffusivity, coarse_cells, copy_sources, copy_targets):
        fields, cells_x, cells_y, cells_z = fine_state.shape
        rows = cells_x * cells_y
        peers = n_x * n_y
        n_hubs, per_hub = hubs_of(n_y)
        sources = jnp.transpose(copy_sources, (0, 1, 4, 2, 3)).reshape(3, 1, peers)
        targets = jnp.transpose(copy_targets, (0, 1, 4, 2, 3)).reshape(3, 1, peers)
        f32 = jnp.float32
        vmem = pltpu.VMEM
        anywhere = pl.BlockSpec(memory_space=pl.ANY)
        result = pl.pallas_call(
            functools.partial(kernel, n_x, n_y, n_z, fields),
            out_shape=pltpu.VMEM((fields, rows, cells_z), f32),
            in_specs=[anywhere] * 5,
            out_specs=pl.BlockSpec(memory_space=pltpu.VMEM),
            scratch_shapes=[
                vmem((fields, rows + 32, cells_z), f32),
                vmem((2, fields, 2, 8, 128), f32),
                vmem((fields, 2, 8, 128), f32),
                vmem((fields, 2, 8, 128), f32),
                vmem((fields, 16 * 8 + 16, 128), f32),
                vmem((fields, 8, 128), f32),
                vmem((fields, 8, 128), f32),
                vmem((fields, 8, 128), f32),
                vmem((fields, rows, 128), f32),
                vmem((fields, 128), f32),
                vmem((3, 1, peers), jnp.int32),
                vmem((3, 1, peers), jnp.int32),
                vmem((2, n_y, 1, 128), f32),
                vmem((n_x * per_hub, n_y - early_of(n_y) + 1, 1, 128), f32),
                vmem((128, 1, 128), f32),
                vmem((128, 128), f32),
                vmem((384, 512), jnp.bfloat16),
                vmem((8 * SLOT, 128), f32),
                vmem((8, 22, 8, 128), f32),
                pltpu.SMEM((fields,), f32),
                pltpu.SemaphoreType.DMA((5,)),
                pltpu.SemaphoreType.DMA((6,)),
                pltpu.SemaphoreType.DMA((6,)),
                pltpu.SemaphoreType.DMA,
                pltpu.SemaphoreType.DMA,
                pltpu.SemaphoreType.DMA((2,)),
                pltpu.SemaphoreType.DMA,
                pltpu.SemaphoreType.DMA,
                pltpu.SemaphoreType.DMA,
                pltpu.SemaphoreType.REGULAR,
                pltpu.SemaphoreType.REGULAR((6,)),
            ],
            compiler_params=pltpu.CompilerParams(
                collective_id=0, has_side_effects=True, vmem_limit_bytes=56 * 1024 * 1024
            ),
        )(fine_state.reshape(fields, rows, cells_z), diffusivity, coarse_cells, sources, targets)
        return result.reshape(fine_state.shape)

    return jax.shard_map(
        on_device,
        mesh=mesh,
        in_specs=(
            P(None, "gx", "gy", "gz"),
            P(),
            P(None, ("gx", "gy", "gz")),
            P("gx", "gy", "gz", None, None),
            P("gx", "gy", "gz", None, None),
        ),
        out_specs=P(None, "gx", "gy", "gz"),
        check_vma=False,
    )
```

```python
import functools

import jax
import jax.numpy as jnp
from jax import lax
from jax.experimental import pallas as pl
from jax.experimental.pallas import tpu as pltpu
from jax.sharding import PartitionSpec as P

MESH = pl.DeviceIdType.MESH
time_step = 0.15
SLOT = 16


def hubs_of(n_y):
    n_hubs = max(1, n_y // 6)
    return n_hubs, n_y // n_hubs


def early_of(n_y):
    return max(2, n_y // 3)


def split3(value):
    hi = value.astype(jnp.bfloat16)
    rest = value - hi.astype(jnp.float32)
    mid = rest.astype(jnp.bfloat16)
    low = (rest - mid.astype(jnp.float32)).astype(jnp.bfloat16)
    return jnp.concatenate([hi, mid, low], axis=0)


def face_terms(rho_left, rho_right, mom_left, mom_right):
    inv_left, inv_right = 1.0 / rho_left, 1.0 / rho_right
    velocity = (0.5 * time_step) * (mom_left * inv_left + mom_right * inv_right)
    up, down = jnp.maximum(velocity, 0.0), jnp.minimum(velocity, 0.0)
    quarter_up, quarter_down = 0.25 * up, 0.25 * down
    mean_rho = (0.5 * time_step) * (rho_left + rho_right)
    return (
        up + quarter_down,
        down + quarter_up,
        quarter_up,
        quarter_down,
        mean_rho * inv_left,
        mean_rho * inv_right,
    )


def cell_terms(low, high):
    a_left, a_right, b_left, b_right, e_left, e_right = low
    next_left, next_right, next_b_left, next_b_right, next_e_left, next_e_right = high
    around = (
        -b_left,
        a_left + next_b_left,
        e_left,
        -(b_right + next_right),
        next_e_right,
        next_b_right,
    )
    return around, (a_right - next_left, -(e_right + next_e_left))


def weighted(found, diff, far_low, low, high, far_high):
    w_far_low, w_low, d_low, w_high, d_high, w_far_high = found
    return (
        (w_far_low * far_low + w_far_high * far_high)
        + (w_low + diff * d_low) * low
        + (w_high + diff * d_high) * high
    )


def work(n_x, n_y, fields, diff, out, qx, y_own, y_low, y_high, y_pad, z_own, z_low, z_high, z_rows,
         cells, src, tgt, msg, relay, merged, arrived, order, spread, plane, terms):
    peers = n_x * n_y
    n_hubs, per_hub = hubs_of(n_y)
    lane = lax.broadcasted_iota(jnp.int32, (8, 128), 1)
    line = lax.broadcasted_iota(jnp.int32, (8, 128), 0)
    blank = jnp.full((1, 128 - peers), -1, jnp.int32)

    def pick(upper):
        owned = jnp.concatenate([cells[...], jnp.zeros((SLOT - fields, 128), jnp.float32)], axis=0)
        owned = split3(owned)
        row = lax.broadcasted_iota(jnp.int32, (128, 128), 0)
        picked = []
        for s in range(3):
            wanted = jnp.concatenate([src[s], blank], axis=1)
            chosen = jnp.where(row == wanted, 1.0, 0.0).astype(jnp.bfloat16)
            part = jnp.dot(owned, chosen, preferred_element_type=jnp.float32)
            picked.append(part[:SLOT] + part[SLOT : 2 * SLOT] + part[2 * SLOT :])
        none = jnp.zeros((SLOT, 128), jnp.float32)
        low = jnp.concatenate(picked + [none] * 5, axis=0)
        high = jnp.concatenate([none] * 4 + picked + [none], axis=0)
        picked = jnp.where(upper, high, low).T
        n_early = early_of(n_y)
        for which, start in enumerate((0, peers - n_y)):
            msg[which, : n_y - n_early] = picked[start + n_early : start + n_y].reshape(n_y - n_early, 1, 128)
            msg[which, n_y - n_early :] = picked[start : start + n_early].reshape(n_early, 1, 128)

    def pack():
        for f in range(fields):
            y_own[0, f, 0] = qx[f, pl.ds(16, 8, stride=8), :]
            y_own[0, f, 1] = qx[f, pl.ds(17, 8, stride=8), :]
            y_own[1, f, 0] = qx[f, pl.ds(22, 8, stride=8), :]
            y_own[1, f, 1] = qx[f, pl.ds(23, 8, stride=8), :]
            packed = pltpu.roll(qx[f, pl.ds(16, 8), :], 2, 1)
            for x in range(1, 8):
                moved = pltpu.roll(qx[f, pl.ds(16 + 8 * x, 8), :], 4 * x + 2, 1)
                packed = jnp.where(lane >= 4 * x, moved, packed)
            z_own[f] = packed

    def pad():
        for f in range(fields):
            for x in range(8):
                y_pad[f, pl.ds(16 * x + 8, 8), :] = tile(f, x)

    def place():
        wide = [jnp.concatenate([tgt[s], blank], axis=1) for s in range(3)]
        wide.append(jnp.full((125, 128), -1, jnp.int32))
        wide = jnp.concatenate(wide, axis=0).astype(jnp.float32).T
        order[...] = jnp.full(order.shape, -1.0, jnp.float32)
        count = n_x // 2 * per_hub
        for a in range(n_x):
            for k in range(per_hub):
                start = a * n_y + k * n_hubs
                first = 64 * (2 * a // n_x) + a % (n_x // 2) * per_hub + k
                order[pl.ds(first, n_hubs, stride=count), :] = wide[start : start + n_hubs]
        half = (lax.broadcasted_iota(jnp.int32, (128, 128), 1) // 2).astype(jnp.float32)
        filled = order[...]
        for s in range(3):
            cell = filled[:, s : s + 1]
            for h in range(4):
                spread[128 * s : 128 * (s + 1), 128 * h : 128 * (h + 1)] = jnp.where(
                    cell - 64.0 * h == half, 1.0, 0.0
                ).astype(jnp.bfloat16)
        if peers < 128:
            unused = jnp.zeros((64 - peers // 2, 1, 128), jnp.float32)
            arrived[peers // 2 : 64] = unused
            arrived[64 + peers // 2 :] = unused

    def clear_upper():
        arrived[64 : 64 + peers // 2] = jnp.zeros((peers // 2, 1, 128), jnp.float32)

    def merge():
        half = n_x // 2 * per_hub
        for k in range(half):
            merged[:, k] = relay[k] + relay[half + k]

    def tile(f, x):
        return qx[f, pl.ds(16 + 8 * x, 8), :]

    def spread_z():
        for f in range(fields):
            kept = jnp.where(lane % 4 < 2, z_low[f], z_high[f])
            for x in range(8):
                z_rows[f, pl.ds(8 * x, 8), :] = pltpu.roll(kept, 126 - 4 * x, 1)

    def spread_y():
        for f in range(fields):
            y_pad[f, pl.ds(6, 8, stride=16), :] = y_low[f, 0]
            y_pad[f, pl.ds(7, 8, stride=16), :] = y_low[f, 1]
            y_pad[f, pl.ds(16, 8, stride=16), :] = y_high[f, 0]
            y_pad[f, pl.ds(17, 8, stride=16), :] = y_high[f, 1]

    def y_at(f, x, k):
        return y_pad[f, pl.ds(16 * x + 8 + k, 8), :]

    def x_at(f, x, k):
        return qx[f, pl.ds(8 * (x + k) + 16, 8), :]

    def z_all(f, x, here):
        beyond = z_rows[f, pl.ds(8 * x, 8), :]
        return (
            pltpu.roll(jnp.where(lane >= 126, beyond, here), 2, 1),
            pltpu.roll(jnp.where(lane == 127, beyond, here), 1, 1),
            pltpu.roll(jnp.where(lane == 0, beyond, here), 127, 1),
            pltpu.roll(jnp.where(lane < 2, beyond, here), 126, 1),
        )

    def three(rho, mom):
        low = face_terms(rho[0], rho[1], mom[0], mom[1])
        high = face_terms(rho[1], rho[2], mom[1], mom[2])
        return cell_terms(low, high)

    def x_terms(x):
        return three([x_at(9, x, k) for k in (-1, 0, 1)], [x_at(10, x, k) for k in (-1, 0, 1)])

    def store_terms(x, first, found):
        for i, value in enumerate(found):
            terms[x, first + i] = value

    def weights_zx():
        for x in range(8):
            rho, mom = tile(9, x), tile(12, x)
            _, rho_low, rho_high, _ = z_all(9, x, rho)
            _, mom_low, mom_high, _ = z_all(12, x, mom)
            found, (centre, d_centre) = three([rho_low, rho, rho_high], [mom_low, mom, mom_high])
            if 2 <= x < 6:
                more, (c, d) = x_terms(x)
                found, centre, d_centre = found + more, centre + c, d_centre + d
            store_terms(x, 0, found + (1.0 + centre, d_centre))

    def weights_y():
        for x in range(8):
            found, centre = three([y_at(9, x, k) for k in (-1, 0, 1)], [y_at(11, x, k) for k in (-1, 0, 1)])
            store_terms(x, 14, found + centre)

    def flux_zx():
        def two_fields(g, carry):
            for x in range(8):
                for f in (2 * g, 2 * g + 1):
                    here = tile(f, x)
                    inner = 2 <= x < 6
                    found = [terms[x, i] for i in range(14 if inner else 8)]
                    total = here * (found[-2] + diff[f] * found[-1])
                    if inner:
                        total = total + weighted(found[6:12], diff[f], *[x_at(f, x, k) for k in (-2, -1, 1, 2)])
                    out[f, pl.ds(8 * x, 8), :] = total + weighted(found[:6], diff[f], *z_all(f, x, here))
            return carry

        lax.fori_loop(0, fields // 2, two_fields, 0)

    def flux_y():
        def two_fields(g, carry):
            for x in range(8):
                for f in (2 * g, 2 * g + 1):
                    rows = pl.ds(8 * x, 8)
                    found = [terms[x, 14 + i] for i in range(8)]
                    total = tile(f, x) * (found[6] + diff[f] * found[7])
                    total = total + weighted(found[:6], diff[f], *[y_at(f, x, k) for k in (-2, -1, 1, 2)])
                    out[f, rows, :] = out[f, rows, :] + total
            return carry

        lax.fori_loop(0, fields // 2, two_fields, 0)

    def edge_flux(first_x):
        kept = []
        for x in (first_x, first_x + 1):
            found, centre = x_terms(x)
            kept.append(found + centre)
        for f in range(fields):
            for x, found in zip((first_x, first_x + 1), kept):
                rows = pl.ds(8 * x, 8)
                total = tile(f, x) * (found[-2] + diff[f] * found[-1])
                total = total + weighted(found[:6], diff[f], *[x_at(f, x, k) for k in (-2, -1, 1, 2)])
                out[f, rows, :] = out[f, rows, :] + total

    def ghost():
        both = (arrived[:64] + arrived[64:]).reshape(64, 128)
        both = jnp.concatenate([both, jnp.zeros((64, 128), jnp.float32)], axis=0).T
        parts = [both[SLOT * i : SLOT * (i + 1), :64] for s in range(3) for i in (s, 4 + s)]
        by_slot = jnp.concatenate(parts, axis=1)
        face = jnp.dot(split3(by_slot), spread[...], preferred_element_type=jnp.float32)
        face = face[:SLOT] + face[SLOT : 2 * SLOT] + face[2 * SLOT :]
        for y in range(8):
            h = y // 2
            plane[SLOT * y : SLOT * (y + 1), :] = face[:, 128 * h : 128 * (h + 1)]

    def use_ghost(start):
        for f in range(fields):
            cover = plane[pl.ds(f, 8, stride=SLOT), :]
            qx[f, pl.ds(start, 8), :] = cover
            qx[f, pl.ds(start + 8, 8), :] = cover

    return dict(
        pick=pick, pack=pack, pad=pad, place=place, clear_upper=clear_upper, merge=merge, spread_z=spread_z,
        spread_y=spread_y, weights_zx=weights_zx, weights_y=weights_y, flux_zx=flux_zx, flux_y=flux_y, ghost=ghost,
        use_ghost=use_ghost, edge_flux=edge_flux,
    )


def kernel(
    n_x, n_y, n_z, fields,
    fine, diffusivity, coarse, sources, targets,
    out,
    qx, y_own, y_low, y_high, y_pad, z_own, z_low, z_high, z_rows,
    cells, src, tgt, msg, relay, merged, arrived, order, spread, plane, terms,
    diff, load_sem, halo_send, halo_recv, row_send, row_recv, block_send, block_recv, pass_send, pass_recv, ready, open_sem,
):
    a, b, c = lax.axis_index("gx"), lax.axis_index("gy"), lax.axis_index("gz")
    is_end = jnp.logical_or(a == 0, a == n_x - 1)
    peers = n_x * n_y
    n_hubs, per_hub = hubs_of(n_y)
    served = n_x * per_hub
    step = work(
        n_x, n_y, fields, diff, out, qx, y_own, y_low, y_high, y_pad, z_own, z_low, z_high, z_rows,
        cells, src, tgt, msg, relay, merged, arrived, order, spread, plane, terms,
    )

    n_early = early_of(n_y)
    ends = (0, n_x - 1)
    corner = jnp.logical_and(jnp.logical_and(a == 0, b == 0), c == 0)
    is_first = jnp.logical_and(jnp.logical_and(is_end, b < n_early), jnp.logical_not(corner))
    is_hub = jnp.logical_and(jnp.logical_and(is_end, b < n_early), b >= n_early - n_hubs)
    is_late = jnp.logical_and(is_end, jnp.logical_not(is_first))
    with_corner = c == 0
    n_late = n_y - n_early
    first_hub = n_early - n_hubs
    hub_y = first_hub + lax.rem(b + (n_y * n_hubs - first_hub), n_hubs)
    half_served = served // 2
    row = 64 * lax.div(2 * a, n_x) + lax.rem(b, n_hubs) * half_served + lax.rem(a, n_x // 2) * per_hub + lax.div(b, n_hubs)

    def x_at(k):
        return (lax.rem(a + (k + n_x), n_x), b, c)

    def y_at(k):
        return (a, lax.rem(b + (k + n_y), n_y), c)

    def z_at(k):
        return (a, b, lax.rem(c + (k + n_z), n_z))

    load_cells = pltpu.make_async_copy(coarse, cells, load_sem.at[0])
    load_src = pltpu.make_async_copy(sources, src, load_sem.at[1])
    load_fine = pltpu.make_async_copy(fine, qx.at[:, pl.ds(16, 64)], load_sem.at[2])
    load_tgt = pltpu.make_async_copy(targets, tgt, load_sem.at[3])
    load_cells.start()
    load_src.start()
    load_fine.start()
    load_tgt.start()
    load_diff = pltpu.make_async_copy(diffusivity, diff, load_sem.at[4])
    load_diff.start()

    barrier = pltpu.get_barrier_semaphore()

    def greet(device):
        pl.semaphore_signal(barrier, inc=1, device_id=device, device_id_type=MESH)

    has_low, has_high = a > 0, a < n_x - 1
    y_later = (b < n_y - 1, b == 0)
    z_later = (c < n_z // 2, jnp.logical_or(c == 0, c > n_z // 2))
    mutual = b < n_y // 2
    mutual_up, mutual_down = b < n_y // 2 - 1, jnp.logical_and(mutual, b > 0)

    def either(p, q):
        return jnp.logical_or(p, q)

    neighbours = [
        (y_at(1), either(jnp.logical_not(y_later[0]), mutual_up), either(y_later[0], mutual_up), 1),
        (y_at(-1), either(jnp.logical_not(y_later[1]), mutual_down), either(y_later[1], mutual_down), 0),
        (z_at(1), either(jnp.logical_not(z_later[0]), mutual), either(z_later[0], mutual), 3),
        (z_at(-1), either(jnp.logical_not(z_later[1]), mutual), either(z_later[1], mutual), 2),
        (x_at(1), jnp.logical_and(has_high, mutual), has_high, 5),
        (x_at(-1), has_low, jnp.logical_and(has_low, mutual), 4),
    ]
    n_greeting = 0
    for device, greeting, greeted, _ in neighbours:
        pl.when(greeted)(functools.partial(greet, device))
        n_greeting = n_greeting + jnp.where(greeting, 1, 0)

    @pl.when(is_first)
    def _():
        for k in range(n_x):
            for peer in range(n_y):

                @pl.when(jnp.logical_or(a != k, b != peer))
                def _():
                    greet((k, peer, c))

    load_cells.wait()
    load_src.wait()
    step["pick"](a >= n_x // 2)
    pl.semaphore_wait(barrier, n_greeting + 2 * n_early - jnp.where(with_corner, 1, 0) - jnp.where(is_first, 1, 0))

    def tell(device, number):
        pl.semaphore_signal(open_sem.at[number], inc=1, device_id=device, device_id_type=MESH)

    for device, greeting, greeted, number in neighbours:
        pl.when(jnp.logical_and(greeting, jnp.logical_not(greeted)))(functools.partial(tell, device, number))

    def to_first(which, peer):
        return pltpu.make_async_remote_copy(
            src_ref=msg.at[which, pl.ds(n_late + peer, 1)], dst_ref=arrived.at[pl.ds(row, 1)],
            send_sem=row_send, recv_sem=row_recv,
            device_id=(ends[which], peer, c), device_id_type=MESH,
        )

    def to_hub(which):
        slot = a * per_hub + lax.div(b, n_hubs)
        return pltpu.make_async_remote_copy(
            src_ref=msg.at[which, pl.ds(0, n_late + 1)], dst_ref=relay.at[slot],
            send_sem=block_send.at[which], recv_sem=block_recv,
            device_id=(ends[which], hub_y, c), device_id_type=MESH,
        )

    for peer in range(n_early):
        for which in range(2):
            itself = jnp.logical_and(a == ends[which], b == peer)
            meant = jnp.logical_not(itself)
            if peer == 0 and which == 0:
                meant = jnp.logical_and(meant, jnp.logical_not(with_corner))
                itself = jnp.logical_and(itself, jnp.logical_not(with_corner))

            @pl.when(meant)
            def _():
                to_first(which, peer).start()

            @pl.when(itself)
            def _():
                arrived[pl.ds(row, 1)] = msg[which, pl.ds(n_late + peer, 1)]

    def own_hub(which):
        return jnp.logical_and(a == ends[which], b == hub_y)

    for which in range(2):

        @pl.when(jnp.logical_not(own_hub(which)))
        def _():
            to_hub(which).start()

        @pl.when(own_hub(which))
        def _():
            relay[a * per_hub + lax.div(b, n_hubs)] = msg[which, pl.ds(0, n_late + 1)]

    @pl.when(is_late)
    def _():
        for h in range(n_hubs):
            pl.semaphore_signal(ready, inc=1, device_id=(a, first_hub + h, c), device_id_type=MESH)

    def halo(i, source, target, device):
        return pltpu.make_async_remote_copy(
            src_ref=source, dst_ref=target, send_sem=halo_send.at[i], recv_sem=halo_recv.at[i],
            device_id=device, device_id_type=MESH,
        )

    load_fine.wait()
    step["pack"]()
    halos = [
        halo(0, y_own.at[1], y_low, y_at(1)),
        halo(1, y_own.at[0], y_high, y_at(-1)),
        halo(2, z_own, z_low, z_at(1)),
        halo(3, z_own, z_high, z_at(-1)),
        halo(4, qx.at[:, pl.ds(64, 16)], qx.at[:, pl.ds(0, 16)], x_at(1)),
        halo(5, qx.at[:, pl.ds(16, 16)], qx.at[:, pl.ds(80, 16)], x_at(-1)),
    ]
    to_high, to_low = halos[4:]

    def send_later(i):
        pl.semaphore_wait(open_sem.at[i], 1)
        halos[i].start()

    for i, (_, greeting, _, _) in enumerate(neighbours):
        pl.when(greeting)(halos[i].start)
    for i in (5, 4, 3, 2, 0, 1):
        unknown = jnp.logical_and(neighbours[i][2], jnp.logical_not(neighbours[i][1]))
        pl.when(unknown)(functools.partial(send_later, i))
    halos = halos[:4]
    load_tgt.wait()
    load_diff.wait()

    @pl.when(is_end)
    def _():
        step["place"]()

        @pl.when(is_late)
        def _():
            step["clear_upper"]()


    step["pad"]()
    for copy in halos[2:]:
        copy.wait_recv()
    step["spread_z"]()
    step["weights_zx"]()
    step["flux_zx"]()

    @pl.when(has_high)
    def _():
        to_low.wait_recv()
        step["edge_flux"](6)

    @pl.when(has_low)
    def _():
        to_high.wait_recv()
        step["edge_flux"](0)

    for copy in halos[:2]:
        copy.wait_recv()
    step["spread_y"]()
    step["weights_y"]()
    step["flux_y"]()

    def to_late(peer):
        return pltpu.make_async_remote_copy(
            src_ref=merged.at[(peer - n_early) % n_y],
            dst_ref=arrived.at[pl.ds(lax.rem(b, n_hubs) * half_served, half_served)],
            send_sem=pass_send, recv_sem=pass_recv,
            device_id=(a, peer, c), device_id_type=MESH,
        )

    def rows_of(count, send, recv):
        rows = arrived.at[pl.ds(0, count)]
        return pltpu.make_async_remote_copy(
            src_ref=rows, dst_ref=rows, send_sem=send, recv_sem=recv, device_id=y_at(1), device_id_type=MESH
        )

    has_corner = jnp.logical_and(with_corner, a == 0)

    @pl.when(is_hub)
    def _():
        blocks = relay.at[pl.ds(0, served - 1)]
        pltpu.make_async_remote_copy(
            src_ref=blocks, dst_ref=blocks, send_sem=block_send.at[0], recv_sem=block_recv,
            device_id=y_at(1), device_id_type=MESH,
        ).wait_recv()
        step["merge"]()
        pl.semaphore_wait(ready, n_late + jnp.where(has_corner, 1, 0))
        for peer in range(n_early, n_y):
            to_late(peer).start()

        @pl.when(has_corner)
        def _():
            to_late(0).start()

    @pl.when(is_first)
    def _():
        rows_of(peers - 1, row_send, row_recv).wait_recv()

    @pl.when(is_late)
    def _():
        rows_of(peers // 2, pass_send, pass_recv).wait_recv()

    @pl.when(is_end)
    def _():
        step["ghost"]()
        for end, start, first_x in ((0, 0, 0), (n_x - 1, 80, 6)):

            @pl.when(a == end)
            def _():
                step["use_ghost"](start)
                step["edge_flux"](first_x)

    @pl.when(is_hub)
    def _():
        for _ in range(n_late):
            rows_of(half_served, pass_send, pass_recv).wait_send()

        @pl.when(has_corner)
        def _():
            rows_of(half_served, pass_send, pass_recv).wait_send()

    rows_of(2 * n_early - 2, row_send, row_recv).wait_send()

    @pl.when(jnp.logical_not(is_first))
    def _():
        rows_of(1, row_send, row_recv).wait_send()

    @pl.when(jnp.logical_not(with_corner))
    def _():
        rows_of(1, row_send, row_recv).wait_send()

    for which in range(2):

        @pl.when(jnp.logical_not(own_hub(which)))
        def _():
            to_hub(which).wait_send()

    for copy in halos:
        copy.wait_send()

    @pl.when(has_low)
    def _():
        to_low.wait_send()

    @pl.when(has_high)
    def _():
        to_high.wait_send()


def solution(mesh):
    n_x, n_y, n_z = (mesh.shape[name] for name in ("gx", "gy", "gz"))

    def on_device(fine_state, diffusivity, coarse_cells, copy_sources, copy_targets):
        fields, cells_x, cells_y, cells_z = fine_state.shape
        rows = cells_x * cells_y
        peers = n_x * n_y
        n_hubs, per_hub = hubs_of(n_y)
        sources = jnp.transpose(copy_sources, (0, 1, 4, 2, 3)).reshape(3, 1, peers)
        targets = jnp.transpose(copy_targets, (0, 1, 4, 2, 3)).reshape(3, 1, peers)
        f32 = jnp.float32
        vmem = pltpu.VMEM
        anywhere = pl.BlockSpec(memory_space=pl.ANY)
        result = pl.pallas_call(
            functools.partial(kernel, n_x, n_y, n_z, fields),
            out_shape=pltpu.VMEM((fields, rows, cells_z), f32),
            in_specs=[anywhere] * 5,
            out_specs=pl.BlockSpec(memory_space=pltpu.VMEM),
            scratch_shapes=[
                vmem((fields, rows + 32, cells_z), f32),
                vmem((2, fields, 2, 8, 128), f32),
                vmem((fields, 2, 8, 128), f32),
                vmem((fields, 2, 8, 128), f32),
                vmem((fields, 16 * 8 + 16, 128), f32),
                vmem((fields, 8, 128), f32),
                vmem((fields, 8, 128), f32),
                vmem((fields, 8, 128), f32),
                vmem((fields, rows, 128), f32),
                vmem((fields, 128), f32),
                vmem((3, 1, peers), jnp.int32),
                vmem((3, 1, peers), jnp.int32),
                vmem((2, n_y, 1, 128), f32),
                vmem((n_x * per_hub, n_y - early_of(n_y) + 1, 1, 128), f32),
                vmem((n_y - early_of(n_y) + 1, n_x // 2 * per_hub, 1, 128), f32),
                vmem((128, 1, 128), f32),
                vmem((128, 128), f32),
                vmem((384, 512), jnp.bfloat16),
                vmem((8 * SLOT, 128), f32),
                vmem((8, 22, 8, 128), f32),
                pltpu.SMEM((fields,), f32),
                pltpu.SemaphoreType.DMA((5,)),
                pltpu.SemaphoreType.DMA((6,)),
                pltpu.SemaphoreType.DMA((6,)),
                pltpu.SemaphoreType.DMA,
                pltpu.SemaphoreType.DMA,
                pltpu.SemaphoreType.DMA((2,)),
                pltpu.SemaphoreType.DMA,
                pltpu.SemaphoreType.DMA,
                pltpu.SemaphoreType.DMA,
                pltpu.SemaphoreType.REGULAR,
                pltpu.SemaphoreType.REGULAR((6,)),
            ],
            compiler_params=pltpu.CompilerParams(
                collective_id=0, has_side_effects=True, vmem_limit_bytes=56 * 1024 * 1024
            ),
        )(fine_state.reshape(fields, rows, cells_z), diffusivity, coarse_cells, sources, targets)
        return result.reshape(fine_state.shape)

    return jax.shard_map(
        on_device,
        mesh=mesh,
        in_specs=(
            P(None, "gx", "gy", "gz"),
            P(),
            P(None, ("gx", "gy", "gz")),
            P("gx", "gy", "gz", None, None),
            P("gx", "gy", "gz", None, None),
        ),
        out_specs=P(None, "gx", "gy", "gz"),
        check_vma=False,
    )
```

```python
import functools

import jax
import jax.numpy as jnp
from jax import lax
from jax.experimental import pallas as pl
from jax.experimental.pallas import tpu as pltpu
from jax.sharding import PartitionSpec as P

MESH = pl.DeviceIdType.MESH
time_step = 0.15
SLOT = 16


def hubs_of(n_y):
    n_hubs = max(1, n_y // 6)
    return n_hubs, n_y // n_hubs


def early_of(n_y):
    return max(2, n_y // 3)


def split3(value):
    hi = value.astype(jnp.bfloat16)
    rest = value - hi.astype(jnp.float32)
    mid = rest.astype(jnp.bfloat16)
    low = (rest - mid.astype(jnp.float32)).astype(jnp.bfloat16)
    return jnp.concatenate([hi, mid, low], axis=0)


def face_terms(rho_left, rho_right, mom_left, mom_right):
    inv_left, inv_right = 1.0 / rho_left, 1.0 / rho_right
    velocity = (0.5 * time_step) * (mom_left * inv_left + mom_right * inv_right)
    up, down = jnp.maximum(velocity, 0.0), jnp.minimum(velocity, 0.0)
    quarter_up, quarter_down = 0.25 * up, 0.25 * down
    mean_rho = (0.5 * time_step) * (rho_left + rho_right)
    return (
        up + quarter_down,
        down + quarter_up,
        quarter_up,
        quarter_down,
        mean_rho * inv_left,
        mean_rho * inv_right,
    )


def cell_terms(low, high):
    a_left, a_right, b_left, b_right, e_left, e_right = low
    next_left, next_right, next_b_left, next_b_right, next_e_left, next_e_right = high
    around = (
        -b_left,
        a_left + next_b_left,
        e_left,
        -(b_right + next_right),
        next_e_right,
        next_b_right,
    )
    return around, (a_right - next_left, -(e_right + next_e_left))


def weighted(found, diff, far_low, low, high, far_high):
    w_far_low, w_low, d_low, w_high, d_high, w_far_high = found
    return (
        (w_far_low * far_low + w_far_high * far_high)
        + (w_low + diff * d_low) * low
        + (w_high + diff * d_high) * high
    )


def work(n_x, n_y, fields, diff, out, qx, y_own, y_low, y_high, y_pad, z_own, z_low, z_high, z_rows,
         cells, src, tgt, msg, relay, merged, arrived, order, spread, plane, terms):
    peers = n_x * n_y
    n_hubs, per_hub = hubs_of(n_y)
    lane = lax.broadcasted_iota(jnp.int32, (8, 128), 1)
    line = lax.broadcasted_iota(jnp.int32, (8, 128), 0)
    blank = jnp.full((1, 128 - peers), -1, jnp.int32)

    def pick(upper):
        owned = jnp.concatenate([cells[...], jnp.zeros((SLOT - fields, 128), jnp.float32)], axis=0)
        owned = split3(owned)
        row = lax.broadcasted_iota(jnp.int32, (128, 128), 0)
        picked = []
        for s in range(3):
            wanted = jnp.concatenate([src[s], blank], axis=1)
            chosen = jnp.where(row == wanted, 1.0, 0.0).astype(jnp.bfloat16)
            part = jnp.dot(owned, chosen, preferred_element_type=jnp.float32)
            picked.append(part[:SLOT] + part[SLOT : 2 * SLOT] + part[2 * SLOT :])
        none = jnp.zeros((SLOT, 128), jnp.float32)
        low = jnp.concatenate(picked + [none] * 5, axis=0)
        high = jnp.concatenate([none] * 4 + picked + [none], axis=0)
        picked = jnp.where(upper, high, low).T
        n_early = early_of(n_y)
        for which, start in enumerate((0, peers - n_y)):
            msg[which, : n_y - n_early] = picked[start + n_early : start + n_y].reshape(n_y - n_early, 1, 128)
            msg[which, n_y - n_early :] = picked[start : start + n_early].reshape(n_early, 1, 128)

    def pack():
        for f in range(fields):
            y_own[0, f, 0] = qx[f, pl.ds(16, 8, stride=8), :]
            y_own[0, f, 1] = qx[f, pl.ds(17, 8, stride=8), :]
            y_own[1, f, 0] = qx[f, pl.ds(22, 8, stride=8), :]
            y_own[1, f, 1] = qx[f, pl.ds(23, 8, stride=8), :]
            packed = pltpu.roll(qx[f, pl.ds(16, 8), :], 2, 1)
            for x in range(1, 8):
                moved = pltpu.roll(qx[f, pl.ds(16 + 8 * x, 8), :], 4 * x + 2, 1)
                packed = jnp.where(lane >= 4 * x, moved, packed)
            z_own[f] = packed

    def pad():
        for f in range(fields):
            for x in range(8):
                y_pad[f, pl.ds(16 * x + 8, 8), :] = tile(f, x)

    def place():
        wide = [jnp.concatenate([tgt[s], blank], axis=1) for s in range(3)]
        wide.append(jnp.full((125, 128), -1, jnp.int32))
        wide = jnp.concatenate(wide, axis=0).astype(jnp.float32).T
        order[...] = jnp.full(order.shape, -1.0, jnp.float32)
        count = n_x // 2 * per_hub
        for a in range(n_x):
            for k in range(per_hub):
                start = a * n_y + k * n_hubs
                first = 64 * (2 * a // n_x) + a % (n_x // 2) * per_hub + k
                order[pl.ds(first, n_hubs, stride=count), :] = wide[start : start + n_hubs]
        half = (lax.broadcasted_iota(jnp.int32, (128, 128), 1) // 2).astype(jnp.float32)
        filled = order[...]
        for s in range(3):
            cell = filled[:, s : s + 1]
            for h in range(4):
                spread[128 * s : 128 * (s + 1), 128 * h : 128 * (h + 1)] = jnp.where(
                    cell - 64.0 * h == half, 1.0, 0.0
                ).astype(jnp.bfloat16)
        if peers < 128:
            unused = jnp.zeros((64 - peers // 2, 1, 128), jnp.float32)
            arrived[peers // 2 : 64] = unused
            arrived[64 + peers // 2 :] = unused

    def clear_upper():
        arrived[64 : 64 + peers // 2] = jnp.zeros((peers // 2, 1, 128), jnp.float32)

    def merge():
        half = n_x // 2 * per_hub
        for k in range(half):
            merged[:, k] = relay[k] + relay[half + k]

    def tile(f, x):
        return qx[f, pl.ds(16 + 8 * x, 8), :]

    def spread_z():
        for f in range(fields):
            kept = jnp.where(lane % 4 < 2, z_low[f], z_high[f])
            for x in range(8):
                z_rows[f, pl.ds(8 * x, 8), :] = pltpu.roll(kept, 126 - 4 * x, 1)

    def spread_y():
        for f in range(fields):
            y_pad[f, pl.ds(6, 8, stride=16), :] = y_low[f, 0]
            y_pad[f, pl.ds(7, 8, stride=16), :] = y_low[f, 1]
            y_pad[f, pl.ds(16, 8, stride=16), :] = y_high[f, 0]
            y_pad[f, pl.ds(17, 8, stride=16), :] = y_high[f, 1]

    def y_at(f, x, k):
        return y_pad[f, pl.ds(16 * x + 8 + k, 8), :]

    def x_at(f, x, k):
        return qx[f, pl.ds(8 * (x + k) + 16, 8), :]

    def z_all(f, x, here):
        beyond = z_rows[f, pl.ds(8 * x, 8), :]
        return (
            pltpu.roll(jnp.where(lane >= 126, beyond, here), 2, 1),
            pltpu.roll(jnp.where(lane == 127, beyond, here), 1, 1),
            pltpu.roll(jnp.where(lane == 0, beyond, here), 127, 1),
            pltpu.roll(jnp.where(lane < 2, beyond, here), 126, 1),
        )

    def three(rho, mom):
        low = face_terms(rho[0], rho[1], mom[0], mom[1])
        high = face_terms(rho[1], rho[2], mom[1], mom[2])
        return cell_terms(low, high)

    def x_terms(x):
        return three([x_at(9, x, k) for k in (-1, 0, 1)], [x_at(10, x, k) for k in (-1, 0, 1)])

    def store_terms(x, first, found):
        for i, value in enumerate(found):
            terms[x, first + i] = value

    def weights_zx():
        for x in range(8):
            rho, mom = tile(9, x), tile(12, x)
            _, rho_low, rho_high, _ = z_all(9, x, rho)
            _, mom_low, mom_high, _ = z_all(12, x, mom)
            found, (centre, d_centre) = three([rho_low, rho, rho_high], [mom_low, mom, mom_high])
            if 2 <= x < 6:
                more, (c, d) = x_terms(x)
                found, centre, d_centre = found + more, centre + c, d_centre + d
            store_terms(x, 0, found + (1.0 + centre, d_centre))

    def weights_y():
        for x in range(8):
            found, centre = three([y_at(9, x, k) for k in (-1, 0, 1)], [y_at(11, x, k) for k in (-1, 0, 1)])
            store_terms(x, 14, found + centre)

    def flux_zx():
        def two_fields(g, carry):
            for x in range(8):
                for f in (2 * g, 2 * g + 1):
                    here = tile(f, x)
                    inner = 2 <= x < 6
                    found = [terms[x, i] for i in range(14 if inner else 8)]
                    total = here * (found[-2] + diff[f] * found[-1])
                    if inner:
                        total = total + weighted(found[6:12], diff[f], *[x_at(f, x, k) for k in (-2, -1, 1, 2)])
                    out[f, pl.ds(8 * x, 8), :] = total + weighted(found[:6], diff[f], *z_all(f, x, here))
            return carry

        lax.fori_loop(0, fields // 2, two_fields, 0)

    def flux_y():
        def two_fields(g, carry):
            for x in range(8):
                for f in (2 * g, 2 * g + 1):
                    rows = pl.ds(8 * x, 8)
                    found = [terms[x, 14 + i] for i in range(8)]
                    total = tile(f, x) * (found[6] + diff[f] * found[7])
                    total = total + weighted(found[:6], diff[f], *[y_at(f, x, k) for k in (-2, -1, 1, 2)])
                    out[f, rows, :] = out[f, rows, :] + total
            return carry

        lax.fori_loop(0, fields // 2, two_fields, 0)

    def edge_flux(first_x):
        kept = []
        for x in (first_x, first_x + 1):
            found, centre = x_terms(x)
            kept.append(found + centre)
        for f in range(fields):
            for x, found in zip((first_x, first_x + 1), kept):
                rows = pl.ds(8 * x, 8)
                total = tile(f, x) * (found[-2] + diff[f] * found[-1])
                total = total + weighted(found[:6], diff[f], *[x_at(f, x, k) for k in (-2, -1, 1, 2)])
                out[f, rows, :] = out[f, rows, :] + total

    def ghost():
        both = (arrived[:64] + arrived[64:]).reshape(64, 128)
        both = both.T
        parts = [both[SLOT * i : SLOT * (i + 1)] for s in range(3) for i in (s, 4 + s)]
        by_slot = jnp.concatenate(parts, axis=1)
        face = jnp.dot(split3(by_slot), spread[...], preferred_element_type=jnp.float32)
        face = face[:SLOT] + face[SLOT : 2 * SLOT] + face[2 * SLOT :]
        for y in range(8):
            h = y // 2
            plane[SLOT * y : SLOT * (y + 1), :] = face[:, 128 * h : 128 * (h + 1)]

    def ghost_flux(first_x):
        def at(f, x):
            if 0 <= x < 8:
                return tile(f, x)
            return plane[pl.ds(f, 8, stride=SLOT), :]

        planes = (first_x, first_x + 1)
        weights = [three([at(9, x + k) for k in (-1, 0, 1)], [at(10, x + k) for k in (-1, 0, 1)]) for x in planes]
        for f in range(fields):
            for x, (found, (centre, d_centre)) in zip(planes, weights):
                rows = pl.ds(8 * x, 8)
                total = tile(f, x) * (centre + diff[f] * d_centre)
                total = total + weighted(found, diff[f], *[at(f, x + k) for k in (-2, -1, 1, 2)])
                out[f, rows, :] = out[f, rows, :] + total

    return dict(
        pick=pick, pack=pack, pad=pad, place=place, clear_upper=clear_upper, merge=merge, spread_z=spread_z,
        spread_y=spread_y, weights_zx=weights_zx, weights_y=weights_y, flux_zx=flux_zx, flux_y=flux_y, ghost=ghost,
        ghost_flux=ghost_flux, edge_flux=edge_flux,
    )


def kernel(
    n_x, n_y, n_z, fields,
    fine, diffusivity, coarse, sources, targets,
    out,
    qx, y_own, y_low, y_high, y_pad, z_own, z_low, z_high, z_rows,
    cells, src, tgt, msg, relay, merged, arrived, order, spread, plane, terms,
    diff, load_sem, halo_send, halo_recv, row_send, row_recv, block_send, block_recv, pass_send, pass_recv, ready, open_sem,
):
    a, b, c = lax.axis_index("gx"), lax.axis_index("gy"), lax.axis_index("gz")
    is_end = jnp.logical_or(a == 0, a == n_x - 1)
    peers = n_x * n_y
    n_hubs, per_hub = hubs_of(n_y)
    served = n_x * per_hub
    step = work(
        n_x, n_y, fields, diff, out, qx, y_own, y_low, y_high, y_pad, z_own, z_low, z_high, z_rows,
        cells, src, tgt, msg, relay, merged, arrived, order, spread, plane, terms,
    )

    n_early = early_of(n_y)
    ends = (0, n_x - 1)
    corner = jnp.logical_and(jnp.logical_and(a == 0, b == 0), c == 0)
    is_first = jnp.logical_and(jnp.logical_and(is_end, b < n_early), jnp.logical_not(corner))
    is_hub = jnp.logical_and(jnp.logical_and(is_end, b < n_early), b >= n_early - n_hubs)
    is_late = jnp.logical_and(is_end, jnp.logical_not(is_first))
    with_corner = c == 0
    n_late = n_y - n_early
    first_hub = n_early - n_hubs
    hub_y = first_hub + lax.rem(b + (n_y * n_hubs - first_hub), n_hubs)
    half_served = served // 2
    row = 64 * lax.div(2 * a, n_x) + lax.rem(b, n_hubs) * half_served + lax.rem(a, n_x // 2) * per_hub + lax.div(b, n_hubs)

    def x_at(k):
        return (lax.rem(a + (k + n_x), n_x), b, c)

    def y_at(k):
        return (a, lax.rem(b + (k + n_y), n_y), c)

    def z_at(k):
        return (a, b, lax.rem(c + (k + n_z), n_z))

    load_cells = pltpu.make_async_copy(coarse, cells, load_sem.at[0])
    load_src = pltpu.make_async_copy(sources, src, load_sem.at[1])
    load_fine = pltpu.make_async_copy(fine, qx.at[:, pl.ds(16, 64)], load_sem.at[2])
    load_tgt = pltpu.make_async_copy(targets, tgt, load_sem.at[3])
    load_cells.start()
    load_src.start()

    barrier = pltpu.get_barrier_semaphore()

    def greet(device):
        pl.semaphore_signal(barrier, inc=1, device_id=device, device_id_type=MESH)

    has_low, has_high = a > 0, a < n_x - 1
    y_later = (b < n_y - 1, b == 0)
    z_later = (c < n_z // 2, jnp.logical_or(c == 0, c > n_z // 2))
    mutual = b < n_y // 2
    mutual_up, mutual_down = b < n_y // 2 - 1, jnp.logical_and(mutual, b > 0)

    def either(p, q):
        return jnp.logical_or(p, q)

    neighbours = [
        (y_at(1), either(jnp.logical_not(y_later[0]), mutual_up), either(y_later[0], mutual_up), 1),
        (y_at(-1), either(jnp.logical_not(y_later[1]), mutual_down), either(y_later[1], mutual_down), 0),
        (z_at(1), either(jnp.logical_not(z_later[0]), mutual), either(z_later[0], mutual), 3),
        (z_at(-1), either(jnp.logical_not(z_later[1]), mutual), either(z_later[1], mutual), 2),
        (x_at(1), jnp.logical_and(has_high, mutual), has_high, 5),
        (x_at(-1), has_low, jnp.logical_and(has_low, mutual), 4),
    ]
    n_greeting = 0
    for device, greeting, greeted, _ in neighbours:
        pl.when(greeted)(functools.partial(greet, device))
        n_greeting = n_greeting + jnp.where(greeting, 1, 0)

    load_fine.start()
    load_tgt.start()
    load_diff = pltpu.make_async_copy(diffusivity, diff, load_sem.at[4])
    load_diff.start()

    @pl.when(is_first)
    def _():
        for k in range(n_x):
            for peer in range(n_y):

                @pl.when(jnp.logical_or(a != k, b != peer))
                def _():
                    greet((k, peer, c))

    load_cells.wait()
    load_src.wait()
    step["pick"](a >= n_x // 2)
    pl.semaphore_wait(barrier, n_greeting + 2 * n_early - jnp.where(with_corner, 1, 0) - jnp.where(is_first, 1, 0))

    def tell(device, number):
        pl.semaphore_signal(open_sem.at[number], inc=1, device_id=device, device_id_type=MESH)

    for device, greeting, greeted, number in neighbours:
        pl.when(jnp.logical_and(greeting, jnp.logical_not(greeted)))(functools.partial(tell, device, number))

    def to_first(which, peer):
        return pltpu.make_async_remote_copy(
            src_ref=msg.at[which, pl.ds(n_late + peer, 1)], dst_ref=arrived.at[pl.ds(row, 1)],
            send_sem=row_send, recv_sem=row_recv,
            device_id=(ends[which], peer, c), device_id_type=MESH,
        )

    def to_hub(which):
        slot = a * per_hub + lax.div(b, n_hubs)
        return pltpu.make_async_remote_copy(
            src_ref=msg.at[which, pl.ds(0, n_late + 1)], dst_ref=relay.at[slot],
            send_sem=block_send.at[which], recv_sem=block_recv,
            device_id=(ends[which], hub_y, c), device_id_type=MESH,
        )

    for which in range(2):
        for peer in sorted(range(n_early), key=lambda p: p ^ 1):
            itself = jnp.logical_and(a == ends[which], b == peer)
            meant = jnp.logical_not(itself)
            if peer == 0 and which == 0:
                meant = jnp.logical_and(meant, jnp.logical_not(with_corner))
                itself = jnp.logical_and(itself, jnp.logical_not(with_corner))

            @pl.when(meant)
            def _():
                to_first(which, peer).start()

            @pl.when(itself)
            def _():
                arrived[pl.ds(row, 1)] = msg[which, pl.ds(n_late + peer, 1)]

    def own_hub(which):
        return jnp.logical_and(a == ends[which], b == hub_y)

    for which in range(2):

        @pl.when(jnp.logical_not(own_hub(which)))
        def _():
            to_hub(which).start()

        @pl.when(own_hub(which))
        def _():
            relay[a * per_hub + lax.div(b, n_hubs)] = msg[which, pl.ds(0, n_late + 1)]

    @pl.when(is_late)
    def _():
        for h in range(n_hubs):
            pl.semaphore_signal(ready, inc=1, device_id=(a, first_hub + h, c), device_id_type=MESH)

    def halo(i, source, target, device):
        return pltpu.make_async_remote_copy(
            src_ref=source, dst_ref=target, send_sem=halo_send.at[i], recv_sem=halo_recv.at[i],
            device_id=device, device_id_type=MESH,
        )

    load_fine.wait()
    step["pack"]()
    halos = [
        halo(0, y_own.at[1], y_low, y_at(1)),
        halo(1, y_own.at[0], y_high, y_at(-1)),
        halo(2, z_own, z_low, z_at(1)),
        halo(3, z_own, z_high, z_at(-1)),
        halo(4, qx.at[:, pl.ds(64, 16)], qx.at[:, pl.ds(0, 16)], x_at(1)),
        halo(5, qx.at[:, pl.ds(16, 16)], qx.at[:, pl.ds(80, 16)], x_at(-1)),
    ]
    to_high, to_low = halos[4:]

    def send_later(i):
        pl.semaphore_wait(open_sem.at[i], 1)
        halos[i].start()

    for i, (_, greeting, _, _) in enumerate(neighbours):
        pl.when(greeting)(halos[i].start)
    for i in (5, 4, 3, 2, 0, 1):
        unknown = jnp.logical_and(neighbours[i][2], jnp.logical_not(neighbours[i][1]))
        pl.when(unknown)(functools.partial(send_later, i))
    halos = halos[:4]
    load_tgt.wait()
    load_diff.wait()

    @pl.when(is_end)
    def _():
        step["place"]()

        @pl.when(is_late)
        def _():
            step["clear_upper"]()


    step["pad"]()
    for copy in halos[2:]:
        copy.wait_recv()
    step["spread_z"]()
    step["weights_zx"]()
    step["flux_zx"]()

    @pl.when(has_high)
    def _():
        to_low.wait_recv()
        step["edge_flux"](6)

    @pl.when(has_low)
    def _():
        to_high.wait_recv()
        step["edge_flux"](0)

    for copy in halos[:2]:
        copy.wait_recv()
    step["spread_y"]()
    step["weights_y"]()
    step["flux_y"]()

    def rows_of(count, send, recv):
        rows = arrived.at[pl.ds(0, count)]
        return pltpu.make_async_remote_copy(
            src_ref=rows, dst_ref=rows, send_sem=send, recv_sem=recv, device_id=y_at(1), device_id_type=MESH
        )

    rows_of(2 * n_early - 2, row_send, row_recv).wait_send()

    @pl.when(jnp.logical_not(is_first))
    def _():
        rows_of(1, row_send, row_recv).wait_send()

    @pl.when(jnp.logical_not(with_corner))
    def _():
        rows_of(1, row_send, row_recv).wait_send()

    for which in range(2):

        @pl.when(jnp.logical_not(own_hub(which)))
        def _():
            to_hub(which).wait_send()

    for copy in halos:
        copy.wait_send()

    @pl.when(has_low)
    def _():
        to_low.wait_send()

    @pl.when(has_high)
    def _():
        to_high.wait_send()

    def to_late(peer):
        return pltpu.make_async_remote_copy(
            src_ref=merged.at[(peer - n_early) % n_y],
            dst_ref=arrived.at[pl.ds(lax.rem(b, n_hubs) * half_served, half_served)],
            send_sem=pass_send, recv_sem=pass_recv,
            device_id=(a, peer, c), device_id_type=MESH,
        )

    has_corner = jnp.logical_and(with_corner, a == 0)

    @pl.when(is_hub)
    def _():
        blocks = relay.at[pl.ds(0, served - 1)]
        pltpu.make_async_remote_copy(
            src_ref=blocks, dst_ref=blocks, send_sem=block_send.at[0], recv_sem=block_recv,
            device_id=y_at(1), device_id_type=MESH,
        ).wait_recv()
        step["merge"]()
        pl.semaphore_wait(ready, n_late + jnp.where(has_corner, 1, 0))
        for peer in range(n_early, n_y):
            to_late(peer).start()

        @pl.when(has_corner)
        def _():
            to_late(0).start()

    @pl.when(is_first)
    def _():
        rows_of(peers - 1, row_send, row_recv).wait_recv()

    @pl.when(is_late)
    def _():
        rows_of(peers // 2, pass_send, pass_recv).wait_recv()

    @pl.when(is_end)
    def _():
        step["ghost"]()
        pl.when(a == 0)(functools.partial(step["ghost_flux"], 0))
        pl.when(a == n_x - 1)(functools.partial(step["ghost_flux"], 6))

    @pl.when(is_hub)
    def _():
        for _ in range(n_late):
            rows_of(half_served, pass_send, pass_recv).wait_send()

        @pl.when(has_corner)
        def _():
            rows_of(half_served, pass_send, pass_recv).wait_send()


def solution(mesh):
    n_x, n_y, n_z = (mesh.shape[name] for name in ("gx", "gy", "gz"))

    def on_device(fine_state, diffusivity, coarse_cells, copy_sources, copy_targets):
        fields, cells_x, cells_y, cells_z = fine_state.shape
        rows = cells_x * cells_y
        peers = n_x * n_y
        n_hubs, per_hub = hubs_of(n_y)
        sources = jnp.transpose(copy_sources, (0, 1, 4, 2, 3)).reshape(3, 1, peers)
        targets = jnp.transpose(copy_targets, (0, 1, 4, 2, 3)).reshape(3, 1, peers)
        f32 = jnp.float32
        vmem = pltpu.VMEM
        anywhere = pl.BlockSpec(memory_space=pl.ANY)
        result = pl.pallas_call(
            functools.partial(kernel, n_x, n_y, n_z, fields),
            out_shape=pltpu.VMEM((fields, rows, cells_z), f32),
            in_specs=[anywhere] * 5,
            out_specs=pl.BlockSpec(memory_space=pltpu.VMEM),
            scratch_shapes=[
                vmem((fields, rows + 32, cells_z), f32),
                vmem((2, fields, 2, 8, 128), f32),
                vmem((fields, 2, 8, 128), f32),
                vmem((fields, 2, 8, 128), f32),
                vmem((fields, 16 * 8 + 16, 128), f32),
                vmem((fields, 8, 128), f32),
                vmem((fields, 8, 128), f32),
                vmem((fields, 8, 128), f32),
                vmem((fields, rows, 128), f32),
                vmem((fields, 128), f32),
                vmem((3, 1, peers), jnp.int32),
                vmem((3, 1, peers), jnp.int32),
                vmem((2, n_y, 1, 128), f32),
                vmem((n_x * per_hub, n_y - early_of(n_y) + 1, 1, 128), f32),
                vmem((n_y - early_of(n_y) + 1, n_x // 2 * per_hub, 1, 128), f32),
                vmem((128, 1, 128), f32),
                vmem((128, 128), f32),
                vmem((384, 512), jnp.bfloat16),
                vmem((8 * SLOT, 128), f32),
                vmem((8, 22, 8, 128), f32),
                pltpu.SMEM((fields,), f32),
                pltpu.SemaphoreType.DMA((5,)),
                pltpu.SemaphoreType.DMA((6,)),
                pltpu.SemaphoreType.DMA((6,)),
                pltpu.SemaphoreType.DMA,
                pltpu.SemaphoreType.DMA,
                pltpu.SemaphoreType.DMA((2,)),
                pltpu.SemaphoreType.DMA,
                pltpu.SemaphoreType.DMA,
                pltpu.SemaphoreType.DMA,
                pltpu.SemaphoreType.REGULAR,
                pltpu.SemaphoreType.REGULAR((6,)),
            ],
            compiler_params=pltpu.CompilerParams(
                collective_id=0, has_side_effects=True, vmem_limit_bytes=56 * 1024 * 1024
            ),
        )(fine_state.reshape(fields, rows, cells_z), diffusivity, coarse_cells, sources, targets)
        return result.reshape(fine_state.shape)

    return jax.shard_map(
        on_device,
        mesh=mesh,
        in_specs=(
            P(None, "gx", "gy", "gz"),
            P(),
            P(None, ("gx", "gy", "gz")),
            P("gx", "gy", "gz", None, None),
            P("gx", "gy", "gz", None, None),
        ),
        out_specs=P(None, "gx", "gy", "gz"),
        check_vma=False,
    )
```

```python
import functools

import jax
import jax.numpy as jnp
from jax import lax
from jax.experimental import pallas as pl
from jax.experimental.pallas import tpu as pltpu
from jax.sharding import PartitionSpec as P

MESH = pl.DeviceIdType.MESH
time_step = 0.15
SLOT = 16


def hubs_of(n_y):
    n_hubs = max(1, n_y // 6)
    return n_hubs, n_y // n_hubs


def early_of(n_y):
    return max(2, n_y // 3)


def split3(value):
    hi = value.astype(jnp.bfloat16)
    rest = value - hi.astype(jnp.float32)
    mid = rest.astype(jnp.bfloat16)
    low = (rest - mid.astype(jnp.float32)).astype(jnp.bfloat16)
    return jnp.concatenate([hi, mid, low], axis=0)


def face_terms(rho_left, rho_right, mom_left, mom_right):
    inv_left, inv_right = 1.0 / rho_left, 1.0 / rho_right
    velocity = (0.5 * time_step) * (mom_left * inv_left + mom_right * inv_right)
    up, down = jnp.maximum(velocity, 0.0), jnp.minimum(velocity, 0.0)
    quarter_up, quarter_down = 0.25 * up, 0.25 * down
    mean_rho = (0.5 * time_step) * (rho_left + rho_right)
    return (
        up + quarter_down,
        down + quarter_up,
        quarter_up,
        quarter_down,
        mean_rho * inv_left,
        mean_rho * inv_right,
    )


def cell_terms(low, high):
    a_left, a_right, b_left, b_right, e_left, e_right = low
    next_left, next_right, next_b_left, next_b_right, next_e_left, next_e_right = high
    around = (
        -b_left,
        a_left + next_b_left,
        e_left,
        -(b_right + next_right),
        next_e_right,
        next_b_right,
    )
    return around, (a_right - next_left, -(e_right + next_e_left))


def weighted(found, diff, far_low, low, high, far_high):
    w_far_low, w_low, d_low, w_high, d_high, w_far_high = found
    return (
        (w_far_low * far_low + w_far_high * far_high)
        + (w_low + diff * d_low) * low
        + (w_high + diff * d_high) * high
    )


def work(n_x, n_y, fields, diff, out, qx, y_own, y_low, y_high, y_pad, z_own, z_low, z_high, z_rows,
         cells, src, tgt, msg, relay, merged, arrived, order, spread, plane, terms):
    peers = n_x * n_y
    n_hubs, per_hub = hubs_of(n_y)
    lane = lax.broadcasted_iota(jnp.int32, (8, 128), 1)
    line = lax.broadcasted_iota(jnp.int32, (8, 128), 0)
    blank = jnp.full((1, 128 - peers), -1, jnp.int32)

    def pick(upper):
        owned = jnp.concatenate([cells[...], jnp.zeros((SLOT - fields, 128), jnp.float32)], axis=0)
        owned = split3(owned)
        row = lax.broadcasted_iota(jnp.int32, (128, 128), 0)
        picked = []
        for s in range(3):
            wanted = jnp.concatenate([src[s], blank], axis=1)
            chosen = jnp.where(row == wanted, 1.0, 0.0).astype(jnp.bfloat16)
            part = jnp.dot(owned, chosen, preferred_element_type=jnp.float32)
            picked.append(part[:SLOT] + part[SLOT : 2 * SLOT] + part[2 * SLOT :])
        none = jnp.zeros((SLOT, 128), jnp.float32)
        low = jnp.concatenate(picked + [none] * 5, axis=0)
        high = jnp.concatenate([none] * 4 + picked + [none], axis=0)
        picked = jnp.where(upper, high, low).T
        n_early = early_of(n_y)
        for which, start in enumerate((0, peers - n_y)):
            msg[which, : n_y - n_early] = picked[start + n_early : start + n_y].reshape(n_y - n_early, 1, 128)
            msg[which, n_y - n_early :] = picked[start : start + n_early].reshape(n_early, 1, 128)

    def pack():
        for f in range(fields):
            y_own[0, f, 0] = qx[f, pl.ds(16, 8, stride=8), :]
            y_own[0, f, 1] = qx[f, pl.ds(17, 8, stride=8), :]
            y_own[1, f, 0] = qx[f, pl.ds(22, 8, stride=8), :]
            y_own[1, f, 1] = qx[f, pl.ds(23, 8, stride=8), :]
            packed = pltpu.roll(qx[f, pl.ds(16, 8), :], 2, 1)
            for x in range(1, 8):
                moved = pltpu.roll(qx[f, pl.ds(16 + 8 * x, 8), :], 4 * x + 2, 1)
                packed = jnp.where(lane >= 4 * x, moved, packed)
            z_own[f] = packed

    def pad():
        for f in range(fields):
            for x in range(8):
                y_pad[f, pl.ds(16 * x + 8, 8), :] = tile(f, x)

    def place():
        wide = [jnp.concatenate([tgt[s], blank], axis=1) for s in range(3)]
        wide.append(jnp.full((125, 128), -1, jnp.int32))
        wide = jnp.concatenate(wide, axis=0).astype(jnp.float32).T
        order[...] = jnp.full(order.shape, -1.0, jnp.float32)
        count = n_x // 2 * per_hub
        for a in range(n_x):
            for k in range(per_hub):
                start = a * n_y + k * n_hubs
                first = 64 * (2 * a // n_x) + a % (n_x // 2) * per_hub + k
                order[pl.ds(first, n_hubs, stride=count), :] = wide[start : start + n_hubs]
        half = (lax.broadcasted_iota(jnp.int32, (128, 128), 1) // 2).astype(jnp.float32)
        filled = order[...]
        for s in range(3):
            cell = filled[:, s : s + 1]
            for h in range(4):
                spread[128 * s : 128 * (s + 1), 128 * h : 128 * (h + 1)] = jnp.where(
                    cell - 64.0 * h == half, 1.0, 0.0
                ).astype(jnp.bfloat16)
        if peers < 128:
            unused = jnp.zeros((64 - peers // 2, 1, 128), jnp.float32)
            arrived[peers // 2 : 64] = unused
            arrived[64 + peers // 2 :] = unused

    def clear_upper():
        arrived[64 : 64 + peers // 2] = jnp.zeros((peers // 2, 1, 128), jnp.float32)

    def merge():
        half = n_x // 2 * per_hub
        for k in range(half):
            merged[:, k] = relay[k] + relay[half + k]

    def tile(f, x):
        return qx[f, pl.ds(16 + 8 * x, 8), :]

    def spread_z():
        for f in range(fields):
            kept = jnp.where(lane % 4 < 2, z_low[f], z_high[f])
            for x in range(8):
                z_rows[f, pl.ds(8 * x, 8), :] = pltpu.roll(kept, 126 - 4 * x, 1)

    def spread_y():
        for f in range(fields):
            y_pad[f, pl.ds(6, 8, stride=16), :] = y_low[f, 0]
            y_pad[f, pl.ds(7, 8, stride=16), :] = y_low[f, 1]
            y_pad[f, pl.ds(16, 8, stride=16), :] = y_high[f, 0]
            y_pad[f, pl.ds(17, 8, stride=16), :] = y_high[f, 1]

    def y_at(f, x, k):
        return y_pad[f, pl.ds(16 * x + 8 + k, 8), :]

    def x_at(f, x, k):
        return qx[f, pl.ds(8 * (x + k) + 16, 8), :]

    def z_all(f, x, here):
        beyond = z_rows[f, pl.ds(8 * x, 8), :]
        return (
            pltpu.roll(jnp.where(lane >= 126, beyond, here), 2, 1),
            pltpu.roll(jnp.where(lane == 127, beyond, here), 1, 1),
            pltpu.roll(jnp.where(lane == 0, beyond, here), 127, 1),
            pltpu.roll(jnp.where(lane < 2, beyond, here), 126, 1),
        )

    def three(rho, mom):
        low = face_terms(rho[0], rho[1], mom[0], mom[1])
        high = face_terms(rho[1], rho[2], mom[1], mom[2])
        return cell_terms(low, high)

    def x_terms(x):
        return three([x_at(9, x, k) for k in (-1, 0, 1)], [x_at(10, x, k) for k in (-1, 0, 1)])

    def store_terms(x, first, found):
        for i, value in enumerate(found):
            terms[x, first + i] = value

    def weights_zx():
        for x in range(8):
            rho, mom = tile(9, x), tile(12, x)
            _, rho_low, rho_high, _ = z_all(9, x, rho)
            _, mom_low, mom_high, _ = z_all(12, x, mom)
            found, (centre, d_centre) = three([rho_low, rho, rho_high], [mom_low, mom, mom_high])
            if 2 <= x < 6:
                more, (c, d) = x_terms(x)
                found, centre, d_centre = found + more, centre + c, d_centre + d
            store_terms(x, 0, found + (1.0 + centre, d_centre))

    def weights_y():
        for x in range(8):
            found, centre = three([y_at(9, x, k) for k in (-1, 0, 1)], [y_at(11, x, k) for k in (-1, 0, 1)])
            store_terms(x, 14, found + centre)

    def flux_zx():
        def two_fields(g, carry):
            for x in range(8):
                for f in (2 * g, 2 * g + 1):
                    here = tile(f, x)
                    inner = 2 <= x < 6
                    found = [terms[x, i] for i in range(14 if inner else 8)]
                    total = here * (found[-2] + diff[f] * found[-1])
                    if inner:
                        total = total + weighted(found[6:12], diff[f], *[x_at(f, x, k) for k in (-2, -1, 1, 2)])
                    out[f, pl.ds(8 * x, 8), :] = total + weighted(found[:6], diff[f], *z_all(f, x, here))
            return carry

        lax.fori_loop(0, fields // 2, two_fields, 0)

    def flux_y():
        def two_fields(g, carry):
            for x in range(8):
                for f in (2 * g, 2 * g + 1):
                    rows = pl.ds(8 * x, 8)
                    found = [terms[x, 14 + i] for i in range(8)]
                    total = tile(f, x) * (found[6] + diff[f] * found[7])
                    total = total + weighted(found[:6], diff[f], *[y_at(f, x, k) for k in (-2, -1, 1, 2)])
                    out[f, rows, :] = out[f, rows, :] + total
            return carry

        lax.fori_loop(0, fields // 2, two_fields, 0)

    def edge_flux(first_x):
        kept = []
        for x in (first_x, first_x + 1):
            found, centre = x_terms(x)
            kept.append(found + centre)
        for f in range(fields):
            for x, found in zip((first_x, first_x + 1), kept):
                rows = pl.ds(8 * x, 8)
                total = tile(f, x) * (found[-2] + diff[f] * found[-1])
                total = total + weighted(found[:6], diff[f], *[x_at(f, x, k) for k in (-2, -1, 1, 2)])
                out[f, rows, :] = out[f, rows, :] + total

    def ghost():
        both = (arrived[:64] + arrived[64:]).reshape(64, 128)
        both = both.T
        parts = [both[SLOT * i : SLOT * (i + 1)] for s in range(3) for i in (s, 4 + s)]
        by_slot = jnp.concatenate(parts, axis=1)
        face = jnp.dot(split3(by_slot), spread[...], preferred_element_type=jnp.float32)
        face = face[:SLOT] + face[SLOT : 2 * SLOT] + face[2 * SLOT :]
        for y in range(8):
            h = y // 2
            plane[SLOT * y : SLOT * (y + 1), :] = face[:, 128 * h : 128 * (h + 1)]

    def ghost_flux(first_x):
        def at(f, x):
            if 0 <= x < 8:
                return tile(f, x)
            return plane[pl.ds(f, 8, stride=SLOT), :]

        planes = (first_x, first_x + 1)
        weights = [three([at(9, x + k) for k in (-1, 0, 1)], [at(10, x + k) for k in (-1, 0, 1)]) for x in planes]
        for f in range(fields):
            for x, (found, (centre, d_centre)) in zip(planes, weights):
                rows = pl.ds(8 * x, 8)
                total = tile(f, x) * (centre + diff[f] * d_centre)
                total = total + weighted(found, diff[f], *[at(f, x + k) for k in (-2, -1, 1, 2)])
                out[f, rows, :] = out[f, rows, :] + total

    return dict(
        pick=pick, pack=pack, pad=pad, place=place, clear_upper=clear_upper, merge=merge, spread_z=spread_z,
        spread_y=spread_y, weights_zx=weights_zx, weights_y=weights_y, flux_zx=flux_zx, flux_y=flux_y, ghost=ghost,
        ghost_flux=ghost_flux, edge_flux=edge_flux,
    )


def kernel(
    n_x, n_y, n_z, fields,
    fine, diffusivity, coarse, sources, targets,
    out,
    qx, y_own, y_low, y_high, y_pad, z_own, z_low, z_high, z_rows,
    cells, src, tgt, msg, relay, merged, arrived, order, spread, plane, terms,
    diff, load_sem, halo_send, halo_recv, row_send, row_recv, block_send, block_recv, pass_send, pass_recv, ready, open_sem,
):
    a, b, c = lax.axis_index("gx"), lax.axis_index("gy"), lax.axis_index("gz")
    is_end = jnp.logical_or(a == 0, a == n_x - 1)
    peers = n_x * n_y
    n_hubs, per_hub = hubs_of(n_y)
    served = n_x * per_hub
    step = work(
        n_x, n_y, fields, diff, out, qx, y_own, y_low, y_high, y_pad, z_own, z_low, z_high, z_rows,
        cells, src, tgt, msg, relay, merged, arrived, order, spread, plane, terms,
    )

    n_early = early_of(n_y)
    ends = (0, n_x - 1)
    corner = jnp.logical_and(jnp.logical_and(a == 0, b == 0), c == 0)
    is_first = jnp.logical_and(jnp.logical_and(is_end, b < n_early), jnp.logical_not(corner))
    is_hub = jnp.logical_and(jnp.logical_and(is_end, b < n_early), b >= n_early - n_hubs)
    is_late = jnp.logical_and(is_end, jnp.logical_not(is_first))
    with_corner = c == 0
    n_late = n_y - n_early
    first_hub = n_early - n_hubs
    hub_y = first_hub + lax.rem(b + (n_y * n_hubs - first_hub), n_hubs)
    half_served = served // 2
    row = 64 * lax.div(2 * a, n_x) + lax.rem(b, n_hubs) * half_served + lax.rem(a, n_x // 2) * per_hub + lax.div(b, n_hubs)

    def x_at(k):
        return (lax.rem(a + (k + n_x), n_x), b, c)

    def y_at(k):
        return (a, lax.rem(b + (k + n_y), n_y), c)

    def z_at(k):
        return (a, b, lax.rem(c + (k + n_z), n_z))

    load_cells = pltpu.make_async_copy(coarse, cells, load_sem.at[0])
    load_src = pltpu.make_async_copy(sources, src, load_sem.at[1])
    load_fine = pltpu.make_async_copy(fine, qx.at[:, pl.ds(16, 64)], load_sem.at[2])
    load_tgt = pltpu.make_async_copy(targets, tgt, load_sem.at[3])
    load_cells.start()
    load_src.start()

    barrier = pltpu.get_barrier_semaphore()

    def greet(device):
        pl.semaphore_signal(barrier, inc=1, device_id=device, device_id_type=MESH)

    has_low, has_high = a > 0, a < n_x - 1
    y_later = (b < n_y - 1, b == 0)
    z_later = (c < n_z // 2, jnp.logical_or(c == 0, c > n_z // 2))
    mutual = b < n_y // 2
    mutual_up, mutual_down = b < n_y // 2 - 1, jnp.logical_and(mutual, b > 0)

    def either(p, q):
        return jnp.logical_or(p, q)

    neighbours = [
        (y_at(1), either(jnp.logical_not(y_later[0]), mutual_up), either(y_later[0], mutual_up), 1),
        (y_at(-1), either(jnp.logical_not(y_later[1]), mutual_down), either(y_later[1], mutual_down), 0),
        (z_at(1), either(jnp.logical_not(z_later[0]), mutual), either(z_later[0], mutual), 3),
        (z_at(-1), either(jnp.logical_not(z_later[1]), mutual), either(z_later[1], mutual), 2),
        (x_at(1), jnp.logical_and(has_high, mutual), has_high, 5),
        (x_at(-1), has_low, jnp.logical_and(has_low, mutual), 4),
    ]
    n_greeting = 0
    for device, greeting, greeted, _ in neighbours:
        pl.when(greeted)(functools.partial(greet, device))
        n_greeting = n_greeting + jnp.where(greeting, 1, 0)

    load_fine.start()
    load_tgt.start()
    load_diff = pltpu.make_async_copy(diffusivity, diff, load_sem.at[4])
    load_diff.start()

    @pl.when(is_first)
    def _():
        for peer in sorted(range(n_y), key=lambda p: (p + n_y // 2) % n_y):
            for k in range(n_x):

                @pl.when(jnp.logical_or(a != k, b != peer))
                def _():
                    greet((k, peer, c))

    load_cells.wait()
    load_src.wait()
    step["pick"](a >= n_x // 2)
    pl.semaphore_wait(barrier, n_greeting + 2 * n_early - jnp.where(with_corner, 1, 0) - jnp.where(is_first, 1, 0))

    def tell(device, number):
        pl.semaphore_signal(open_sem.at[number], inc=1, device_id=device, device_id_type=MESH)

    for device, greeting, greeted, number in neighbours:
        pl.when(jnp.logical_and(greeting, jnp.logical_not(greeted)))(functools.partial(tell, device, number))

    def to_first(which, peer):
        return pltpu.make_async_remote_copy(
            src_ref=msg.at[which, pl.ds(n_late + peer, 1)], dst_ref=arrived.at[pl.ds(row, 1)],
            send_sem=row_send, recv_sem=row_recv,
            device_id=(ends[which], peer, c), device_id_type=MESH,
        )

    def to_hub(which):
        slot = a * per_hub + lax.div(b, n_hubs)
        return pltpu.make_async_remote_copy(
            src_ref=msg.at[which, pl.ds(0, n_late + 1)], dst_ref=relay.at[slot],
            send_sem=block_send.at[which], recv_sem=block_recv,
            device_id=(ends[which], hub_y, c), device_id_type=MESH,
        )

    for which in range(2):
        for peer in sorted(range(n_early), key=lambda p: p ^ 1):
            itself = jnp.logical_and(a == ends[which], b == peer)
            meant = jnp.logical_not(itself)
            if peer == 0 and which == 0:
                meant = jnp.logical_and(meant, jnp.logical_not(with_corner))
                itself = jnp.logical_and(itself, jnp.logical_not(with_corner))

            @pl.when(meant)
            def _():
                to_first(which, peer).start()

            @pl.when(itself)
            def _():
                arrived[pl.ds(row, 1)] = msg[which, pl.ds(n_late + peer, 1)]

    def own_hub(which):
        return jnp.logical_and(a == ends[which], b == hub_y)

    for which in range(2):

        @pl.when(jnp.logical_not(own_hub(which)))
        def _():
            to_hub(which).start()

        @pl.when(own_hub(which))
        def _():
            relay[a * per_hub + lax.div(b, n_hubs)] = msg[which, pl.ds(0, n_late + 1)]

    @pl.when(is_late)
    def _():
        for h in range(n_hubs):
            pl.semaphore_signal(ready, inc=1, device_id=(a, first_hub + h, c), device_id_type=MESH)

    def halo(i, source, target, device):
        return pltpu.make_async_remote_copy(
            src_ref=source, dst_ref=target, send_sem=halo_send.at[i], recv_sem=halo_recv.at[i],
            device_id=device, device_id_type=MESH,
        )

    load_fine.wait()
    step["pack"]()
    halos = [
        halo(0, y_own.at[1], y_low, y_at(1)),
        halo(1, y_own.at[0], y_high, y_at(-1)),
        halo(2, z_own, z_low, z_at(1)),
        halo(3, z_own, z_high, z_at(-1)),
        halo(4, qx.at[:, pl.ds(64, 16)], qx.at[:, pl.ds(0, 16)], x_at(1)),
        halo(5, qx.at[:, pl.ds(16, 16)], qx.at[:, pl.ds(80, 16)], x_at(-1)),
    ]
    to_high, to_low = halos[4:]

    def send_later(i):
        pl.semaphore_wait(open_sem.at[i], 1)
        halos[i].start()

    for i, (_, greeting, _, _) in enumerate(neighbours):
        pl.when(greeting)(halos[i].start)
    for i in (5, 4, 3, 2, 0, 1):
        unknown = jnp.logical_and(neighbours[i][2], jnp.logical_not(neighbours[i][1]))
        pl.when(unknown)(functools.partial(send_later, i))
    halos = halos[:4]
    load_tgt.wait()
    load_diff.wait()

    @pl.when(is_end)
    def _():
        step["place"]()

        @pl.when(is_late)
        def _():
            step["clear_upper"]()


    step["pad"]()
    for copy in halos[2:]:
        copy.wait_recv()
    step["spread_z"]()
    step["weights_zx"]()
    step["flux_zx"]()

    @pl.when(has_high)
    def _():
        to_low.wait_recv()
        step["edge_flux"](6)

    @pl.when(has_low)
    def _():
        to_high.wait_recv()
        step["edge_flux"](0)

    for copy in halos[:2]:
        copy.wait_recv()
    step["spread_y"]()
    step["weights_y"]()
    step["flux_y"]()

    def rows_of(count, send, recv):
        rows = arrived.at[pl.ds(0, count)]
        return pltpu.make_async_remote_copy(
            src_ref=rows, dst_ref=rows, send_sem=send, recv_sem=recv, device_id=y_at(1), device_id_type=MESH
        )

    rows_of(2 * n_early - 2, row_send, row_recv).wait_send()

    @pl.when(jnp.logical_not(is_first))
    def _():
        rows_of(1, row_send, row_recv).wait_send()

    @pl.when(jnp.logical_not(with_corner))
    def _():
        rows_of(1, row_send, row_recv).wait_send()

    for which in range(2):

        @pl.when(jnp.logical_not(own_hub(which)))
        def _():
            to_hub(which).wait_send()

    for copy in halos:
        copy.wait_send()

    @pl.when(has_low)
    def _():
        to_low.wait_send()

    @pl.when(has_high)
    def _():
        to_high.wait_send()

    def to_late(peer):
        return pltpu.make_async_remote_copy(
            src_ref=merged.at[(peer - n_early) % n_y],
            dst_ref=arrived.at[pl.ds(lax.rem(b, n_hubs) * half_served, half_served)],
            send_sem=pass_send, recv_sem=pass_recv,
            device_id=(a, peer, c), device_id_type=MESH,
        )

    has_corner = jnp.logical_and(with_corner, a == 0)

    @pl.when(is_hub)
    def _():
        blocks = relay.at[pl.ds(0, served - 1)]
        pltpu.make_async_remote_copy(
            src_ref=blocks, dst_ref=blocks, send_sem=block_send.at[0], recv_sem=block_recv,
            device_id=y_at(1), device_id_type=MESH,
        ).wait_recv()
        step["merge"]()
        pl.semaphore_wait(ready, n_late + jnp.where(has_corner, 1, 0))
        for peer in range(n_early, n_y):
            to_late(peer).start()

        @pl.when(has_corner)
        def _():
            to_late(0).start()

    @pl.when(is_first)
    def _():
        rows_of(peers - 1, row_send, row_recv).wait_recv()

    @pl.when(is_late)
    def _():
        rows_of(peers // 2, pass_send, pass_recv).wait_recv()

    @pl.when(is_end)
    def _():
        step["ghost"]()
        pl.when(a == 0)(functools.partial(step["ghost_flux"], 0))
        pl.when(a == n_x - 1)(functools.partial(step["ghost_flux"], 6))

    @pl.when(is_hub)
    def _():
        for _ in range(n_late):
            rows_of(half_served, pass_send, pass_recv).wait_send()

        @pl.when(has_corner)
        def _():
            rows_of(half_served, pass_send, pass_recv).wait_send()


def solution(mesh):
    n_x, n_y, n_z = (mesh.shape[name] for name in ("gx", "gy", "gz"))

    def on_device(fine_state, diffusivity, coarse_cells, copy_sources, copy_targets):
        fields, cells_x, cells_y, cells_z = fine_state.shape
        rows = cells_x * cells_y
        peers = n_x * n_y
        n_hubs, per_hub = hubs_of(n_y)
        sources = jnp.transpose(copy_sources, (0, 1, 4, 2, 3)).reshape(3, 1, peers)
        targets = jnp.transpose(copy_targets, (0, 1, 4, 2, 3)).reshape(3, 1, peers)
        f32 = jnp.float32
        vmem = pltpu.VMEM
        anywhere = pl.BlockSpec(memory_space=pl.ANY)
        result = pl.pallas_call(
            functools.partial(kernel, n_x, n_y, n_z, fields),
            out_shape=pltpu.VMEM((fields, rows, cells_z), f32),
            in_specs=[anywhere] * 5,
            out_specs=pl.BlockSpec(memory_space=pltpu.VMEM),
            scratch_shapes=[
                vmem((fields, rows + 32, cells_z), f32),
                vmem((2, fields, 2, 8, 128), f32),
                vmem((fields, 2, 8, 128), f32),
                vmem((fields, 2, 8, 128), f32),
                vmem((fields, 16 * 8 + 16, 128), f32),
                vmem((fields, 8, 128), f32),
                vmem((fields, 8, 128), f32),
                vmem((fields, 8, 128), f32),
                vmem((fields, rows, 128), f32),
                vmem((fields, 128), f32),
                vmem((3, 1, peers), jnp.int32),
                vmem((3, 1, peers), jnp.int32),
                vmem((2, n_y, 1, 128), f32),
                vmem((n_x * per_hub, n_y - early_of(n_y) + 1, 1, 128), f32),
                vmem((n_y - early_of(n_y) + 1, n_x // 2 * per_hub, 1, 128), f32),
                vmem((128, 1, 128), f32),
                vmem((128, 128), f32),
                vmem((384, 512), jnp.bfloat16),
                vmem((8 * SLOT, 128), f32),
                vmem((8, 22, 8, 128), f32),
                pltpu.SMEM((fields,), f32),
                pltpu.SemaphoreType.DMA((5,)),
                pltpu.SemaphoreType.DMA((6,)),
                pltpu.SemaphoreType.DMA((6,)),
                pltpu.SemaphoreType.DMA,
                pltpu.SemaphoreType.DMA,
                pltpu.SemaphoreType.DMA((2,)),
                pltpu.SemaphoreType.DMA,
                pltpu.SemaphoreType.DMA,
                pltpu.SemaphoreType.DMA,
                pltpu.SemaphoreType.REGULAR,
                pltpu.SemaphoreType.REGULAR((6,)),
            ],
            compiler_params=pltpu.CompilerParams(
                collective_id=0, has_side_effects=True, vmem_limit_bytes=56 * 1024 * 1024
            ),
        )(fine_state.reshape(fields, rows, cells_z), diffusivity, coarse_cells, sources, targets)
        return result.reshape(fine_state.shape)

    return jax.shard_map(
        on_device,
        mesh=mesh,
        in_specs=(
            P(None, "gx", "gy", "gz"),
            P(),
            P(None, ("gx", "gy", "gz")),
            P("gx", "gy", "gz", None, None),
            P("gx", "gy", "gz", None, None),
        ),
        out_specs=P(None, "gx", "gy", "gz"),
        check_vma=False,
    )
```

```python
import functools

import jax
import jax.numpy as jnp
from jax import lax
from jax.experimental import pallas as pl
from jax.experimental.pallas import tpu as pltpu
from jax.sharding import PartitionSpec as P

MESH = pl.DeviceIdType.MESH
time_step = 0.15
SLOT = 16


def hubs_of(n_y):
    n_hubs = max(1, n_y // 6)
    return n_hubs, n_y // n_hubs


def early_of(n_y):
    return max(2, n_y // 3)


def split3(value):
    hi = value.astype(jnp.bfloat16)
    rest = value - hi.astype(jnp.float32)
    mid = rest.astype(jnp.bfloat16)
    low = (rest - mid.astype(jnp.float32)).astype(jnp.bfloat16)
    return jnp.concatenate([hi, mid, low], axis=0)


def face_terms(rho_left, rho_right, mom_left, mom_right):
    inv_left, inv_right = 1.0 / rho_left, 1.0 / rho_right
    velocity = (0.5 * time_step) * (mom_left * inv_left + mom_right * inv_right)
    up, down = jnp.maximum(velocity, 0.0), jnp.minimum(velocity, 0.0)
    quarter_up, quarter_down = 0.25 * up, 0.25 * down
    mean_rho = (0.5 * time_step) * (rho_left + rho_right)
    return (
        up + quarter_down,
        down + quarter_up,
        quarter_up,
        quarter_down,
        mean_rho * inv_left,
        mean_rho * inv_right,
    )


def cell_terms(low, high):
    a_left, a_right, b_left, b_right, e_left, e_right = low
    next_left, next_right, next_b_left, next_b_right, next_e_left, next_e_right = high
    around = (
        -b_left,
        a_left + next_b_left,
        e_left,
        -(b_right + next_right),
        next_e_right,
        next_b_right,
    )
    return around, (a_right - next_left, -(e_right + next_e_left))


def weighted(found, diff, far_low, low, high, far_high):
    w_far_low, w_low, d_low, w_high, d_high, w_far_high = found
    return (
        (w_far_low * far_low + w_far_high * far_high)
        + (w_low + diff * d_low) * low
        + (w_high + diff * d_high) * high
    )


def work(n_x, n_y, fields, diff, out, qx, y_own, y_low, y_high, y_pad, z_own, z_low, z_high, z_rows,
         cells, src, tgt, msg, relay, merged, arrived, order, spread, plane, terms):
    peers = n_x * n_y
    n_hubs, per_hub = hubs_of(n_y)
    lane = lax.broadcasted_iota(jnp.int32, (8, 128), 1)
    line = lax.broadcasted_iota(jnp.int32, (8, 128), 0)
    blank = jnp.full((1, 128 - peers), -1, jnp.int32)

    def pick(upper):
        owned = jnp.concatenate([cells[...], jnp.zeros((SLOT - fields, 128), jnp.float32)], axis=0)
        owned = split3(owned)
        row = lax.broadcasted_iota(jnp.int32, (128, 128), 0)
        picked = []
        for s in range(3):
            wanted = jnp.concatenate([src[s], blank], axis=1)
            chosen = jnp.where(row == wanted, 1.0, 0.0).astype(jnp.bfloat16)
            part = jnp.dot(owned, chosen, preferred_element_type=jnp.float32)
            picked.append(part[:SLOT] + part[SLOT : 2 * SLOT] + part[2 * SLOT :])
        none = jnp.zeros((SLOT, 128), jnp.float32)
        low = jnp.concatenate(picked + [none] * 5, axis=0)
        high = jnp.concatenate([none] * 4 + picked + [none], axis=0)
        picked = jnp.where(upper, high, low).T
        n_early = early_of(n_y)
        for which, start in enumerate((0, peers - n_y)):
            msg[which, : n_y - n_early] = picked[start + n_early : start + n_y].reshape(n_y - n_early, 1, 128)
            msg[which, n_y - n_early :] = picked[start : start + n_early].reshape(n_early, 1, 128)

    def pack():
        for f in range(fields):
            y_own[0, f, 0] = qx[f, pl.ds(16, 8, stride=8), :]
            y_own[0, f, 1] = qx[f, pl.ds(17, 8, stride=8), :]
            y_own[1, f, 0] = qx[f, pl.ds(22, 8, stride=8), :]
            y_own[1, f, 1] = qx[f, pl.ds(23, 8, stride=8), :]
            packed = pltpu.roll(qx[f, pl.ds(16, 8), :], 2, 1)
            for x in range(1, 8):
                moved = pltpu.roll(qx[f, pl.ds(16 + 8 * x, 8), :], 4 * x + 2, 1)
                packed = jnp.where(lane >= 4 * x, moved, packed)
            z_own[f] = packed

    def pad():
        for f in range(fields):
            for x in range(8):
                y_pad[f, pl.ds(16 * x + 8, 8), :] = tile(f, x)

    def place():
        wide = [jnp.concatenate([tgt[s], blank], axis=1) for s in range(3)]
        wide.append(jnp.full((125, 128), -1, jnp.int32))
        wide = jnp.concatenate(wide, axis=0).astype(jnp.float32).T
        order[...] = jnp.full(order.shape, -1.0, jnp.float32)
        count = n_x // 2 * per_hub
        for a in range(n_x):
            for k in range(per_hub):
                start = a * n_y + k * n_hubs
                first = 64 * (2 * a // n_x) + a % (n_x // 2) * per_hub + k
                order[pl.ds(first, n_hubs, stride=count), :] = wide[start : start + n_hubs]
        half = (lax.broadcasted_iota(jnp.int32, (128, 128), 1) // 2).astype(jnp.float32)
        filled = order[...]
        for s in range(3):
            cell = filled[:, s : s + 1]
            for h in range(4):
                spread[128 * s : 128 * (s + 1), 128 * h : 128 * (h + 1)] = jnp.where(
                    cell - 64.0 * h == half, 1.0, 0.0
                ).astype(jnp.bfloat16)
        if peers < 128:
            unused = jnp.zeros((64 - peers // 2, 1, 128), jnp.float32)
            arrived[peers // 2 : 64] = unused
            arrived[64 + peers // 2 :] = unused

    def clear_upper():
        arrived[64 : 64 + peers // 2] = jnp.zeros((peers // 2, 1, 128), jnp.float32)

    def merge():
        half = n_x // 2 * per_hub
        for k in range(half):
            merged[:, k] = relay[k] + relay[half + k]

    def tile(f, x):
        return qx[f, pl.ds(16 + 8 * x, 8), :]

    def spread_z():
        for f in range(fields):
            kept = jnp.where(lane % 4 < 2, z_low[f], z_high[f])
            for x in range(8):
                z_rows[f, pl.ds(8 * x, 8), :] = pltpu.roll(kept, 126 - 4 * x, 1)

    def spread_y():
        for f in range(fields):
            y_pad[f, pl.ds(6, 8, stride=16), :] = y_low[f, 0]
            y_pad[f, pl.ds(7, 8, stride=16), :] = y_low[f, 1]
            y_pad[f, pl.ds(16, 8, stride=16), :] = y_high[f, 0]
            y_pad[f, pl.ds(17, 8, stride=16), :] = y_high[f, 1]

    def y_at(f, x, k):
        return y_pad[f, pl.ds(16 * x + 8 + k, 8), :]

    def x_at(f, x, k):
        return qx[f, pl.ds(8 * (x + k) + 16, 8), :]

    def z_all(f, x, here):
        beyond = z_rows[f, pl.ds(8 * x, 8), :]
        return (
            pltpu.roll(jnp.where(lane >= 126, beyond, here), 2, 1),
            pltpu.roll(jnp.where(lane == 127, beyond, here), 1, 1),
            pltpu.roll(jnp.where(lane == 0, beyond, here), 127, 1),
            pltpu.roll(jnp.where(lane < 2, beyond, here), 126, 1),
        )

    def three(rho, mom):
        low = face_terms(rho[0], rho[1], mom[0], mom[1])
        high = face_terms(rho[1], rho[2], mom[1], mom[2])
        return cell_terms(low, high)

    def x_terms(x):
        return three([x_at(9, x, k) for k in (-1, 0, 1)], [x_at(10, x, k) for k in (-1, 0, 1)])

    def store_terms(x, first, found):
        for i, value in enumerate(found):
            terms[x, first + i] = value

    def weights_zx():
        for x in range(8):
            rho, mom = tile(9, x), tile(12, x)
            _, rho_low, rho_high, _ = z_all(9, x, rho)
            _, mom_low, mom_high, _ = z_all(12, x, mom)
            found, (centre, d_centre) = three([rho_low, rho, rho_high], [mom_low, mom, mom_high])
            if 2 <= x < 6:
                more, (c, d) = x_terms(x)
                found, centre, d_centre = found + more, centre + c, d_centre + d
            store_terms(x, 0, found + (1.0 + centre, d_centre))

    def weights_y():
        for x in range(8):
            found, centre = three([y_at(9, x, k) for k in (-1, 0, 1)], [y_at(11, x, k) for k in (-1, 0, 1)])
            store_terms(x, 14, found + centre)

    def flux_zx():
        def two_fields(g, carry):
            for x in range(8):
                for f in (2 * g, 2 * g + 1):
                    here = tile(f, x)
                    inner = 2 <= x < 6
                    found = [terms[x, i] for i in range(14 if inner else 8)]
                    total = here * (found[-2] + diff[f] * found[-1])
                    if inner:
                        total = total + weighted(found[6:12], diff[f], *[x_at(f, x, k) for k in (-2, -1, 1, 2)])
                    out[f, pl.ds(8 * x, 8), :] = total + weighted(found[:6], diff[f], *z_all(f, x, here))
            return carry

        lax.fori_loop(0, fields // 2, two_fields, 0)

    def flux_y():
        def two_fields(g, carry):
            for x in range(8):
                for f in (2 * g, 2 * g + 1):
                    rows = pl.ds(8 * x, 8)
                    found = [terms[x, 14 + i] for i in range(8)]
                    total = tile(f, x) * (found[6] + diff[f] * found[7])
                    total = total + weighted(found[:6], diff[f], *[y_at(f, x, k) for k in (-2, -1, 1, 2)])
                    out[f, rows, :] = out[f, rows, :] + total
            return carry

        lax.fori_loop(0, fields // 2, two_fields, 0)

    def edge_flux(first_x):
        kept = []
        for x in (first_x, first_x + 1):
            found, centre = x_terms(x)
            kept.append(found + centre)
        for f in range(fields):
            for x, found in zip((first_x, first_x + 1), kept):
                rows = pl.ds(8 * x, 8)
                total = tile(f, x) * (found[-2] + diff[f] * found[-1])
                total = total + weighted(found[:6], diff[f], *[x_at(f, x, k) for k in (-2, -1, 1, 2)])
                out[f, rows, :] = out[f, rows, :] + total

    def ghost():
        both = (arrived[:64] + arrived[64:]).reshape(64, 128)
        both = both.T
        parts = [both[SLOT * i : SLOT * (i + 1)] for s in range(3) for i in (s, 4 + s)]
        by_slot = jnp.concatenate(parts, axis=1)
        face = jnp.dot(split3(by_slot), spread[...], preferred_element_type=jnp.float32)
        face = face[:SLOT] + face[SLOT : 2 * SLOT] + face[2 * SLOT :]
        for y in range(8):
            h = y // 2
            plane[SLOT * y : SLOT * (y + 1), :] = face[:, 128 * h : 128 * (h + 1)]

    def ghost_flux(first_x):
        def at(f, x):
            if 0 <= x < 8:
                return tile(f, x)
            return plane[pl.ds(f, 8, stride=SLOT), :]

        planes = (first_x, first_x + 1)
        weights = [three([at(9, x + k) for k in (-1, 0, 1)], [at(10, x + k) for k in (-1, 0, 1)]) for x in planes]
        for f in range(fields):
            for x, (found, (centre, d_centre)) in zip(planes, weights):
                rows = pl.ds(8 * x, 8)
                total = tile(f, x) * (centre + diff[f] * d_centre)
                total = total + weighted(found, diff[f], *[at(f, x + k) for k in (-2, -1, 1, 2)])
                out[f, rows, :] = out[f, rows, :] + total

    return dict(
        pick=pick, pack=pack, pad=pad, place=place, clear_upper=clear_upper, merge=merge, spread_z=spread_z,
        spread_y=spread_y, weights_zx=weights_zx, weights_y=weights_y, flux_zx=flux_zx, flux_y=flux_y, ghost=ghost,
        ghost_flux=ghost_flux, edge_flux=edge_flux,
    )


def kernel(
    n_x, n_y, n_z, fields,
    fine, diffusivity, coarse, sources, targets,
    out,
    qx, y_own, y_low, y_high, y_pad, z_own, z_low, z_high, z_rows,
    cells, src, tgt, msg, relay, merged, arrived, order, spread, plane, terms,
    diff, load_sem, halo_send, halo_recv, row_send, row_recv, block_send, block_recv, pass_send, pass_recv, ready, open_sem,
):
    a, b, c = lax.axis_index("gx"), lax.axis_index("gy"), lax.axis_index("gz")
    is_end = jnp.logical_or(a == 0, a == n_x - 1)
    peers = n_x * n_y
    n_hubs, per_hub = hubs_of(n_y)
    served = n_x * per_hub
    step = work(
        n_x, n_y, fields, diff, out, qx, y_own, y_low, y_high, y_pad, z_own, z_low, z_high, z_rows,
        cells, src, tgt, msg, relay, merged, arrived, order, spread, plane, terms,
    )

    n_early = early_of(n_y)
    ends = (0, n_x - 1)
    corner = jnp.logical_and(jnp.logical_and(a == 0, b == 0), c == 0)
    is_first = jnp.logical_and(jnp.logical_and(is_end, b < n_early), jnp.logical_not(corner))
    is_hub = jnp.logical_and(jnp.logical_and(is_end, b < n_early), b >= n_early - n_hubs)
    is_late = jnp.logical_and(is_end, jnp.logical_not(is_first))
    with_corner = c == 0
    n_late = n_y - n_early
    first_hub = n_early - n_hubs
    hub_y = first_hub + lax.rem(b + (n_y * n_hubs - first_hub), n_hubs)
    half_served = served // 2
    row = 64 * lax.div(2 * a, n_x) + lax.rem(b, n_hubs) * half_served + lax.rem(a, n_x // 2) * per_hub + lax.div(b, n_hubs)

    def x_at(k):
        return (lax.rem(a + (k + n_x), n_x), b, c)

    def y_at(k):
        return (a, lax.rem(b + (k + n_y), n_y), c)

    def z_at(k):
        return (a, b, lax.rem(c + (k + n_z), n_z))

    load_cells = pltpu.make_async_copy(coarse, cells, load_sem.at[0])
    load_src = pltpu.make_async_copy(sources, src, load_sem.at[1])
    load_fine = pltpu.make_async_copy(fine, qx.at[:, pl.ds(16, 64)], load_sem.at[2])
    load_tgt = pltpu.make_async_copy(targets, tgt, load_sem.at[3])
    load_cells.start()
    load_src.start()

    barrier = pltpu.get_barrier_semaphore()

    def greet(device):
        pl.semaphore_signal(barrier, inc=1, device_id=device, device_id_type=MESH)

    has_low, has_high = a > 0, a < n_x - 1
    y_later = (b < n_y - 1, b == 0)
    z_later = (c < n_z // 2, jnp.logical_or(c == 0, c > n_z // 2))
    mutual = b < n_y // 2
    mutual_up, mutual_down = b < n_y // 2 - 1, jnp.logical_and(mutual, b > 0)

    def either(p, q):
        return jnp.logical_or(p, q)

    neighbours = [
        (y_at(1), either(jnp.logical_not(y_later[0]), mutual_up), either(y_later[0], mutual_up), 1),
        (y_at(-1), either(jnp.logical_not(y_later[1]), mutual_down), either(y_later[1], mutual_down), 0),
        (z_at(1), either(jnp.logical_not(z_later[0]), mutual), either(z_later[0], mutual), 3),
        (z_at(-1), either(jnp.logical_not(z_later[1]), mutual), either(z_later[1], mutual), 2),
        (x_at(1), jnp.logical_and(has_high, mutual), has_high, 5),
        (x_at(-1), has_low, jnp.logical_and(has_low, mutual), 4),
    ]
    n_greeting = 0
    for device, greeting, greeted, _ in neighbours:
        pl.when(greeted)(functools.partial(greet, device))
        n_greeting = n_greeting + jnp.where(greeting, 1, 0)

    load_tgt.start()
    load_diff = pltpu.make_async_copy(diffusivity, diff, load_sem.at[4])
    load_diff.start()

    @pl.when(is_first)
    def _():
        for k in range(n_x):
            for peer in range(n_y):

                @pl.when(jnp.logical_or(a != k, b != peer))
                def _():
                    greet((k, peer, c))

    load_cells.wait()
    load_src.wait()
    load_fine.start()
    step["pick"](a >= n_x // 2)
    pl.semaphore_wait(barrier, n_greeting + 2 * n_early - jnp.where(with_corner, 1, 0) - jnp.where(is_first, 1, 0))

    def tell(device, number):
        pl.semaphore_signal(open_sem.at[number], inc=1, device_id=device, device_id_type=MESH)

    for device, greeting, greeted, number in neighbours:
        pl.when(jnp.logical_and(greeting, jnp.logical_not(greeted)))(functools.partial(tell, device, number))

    def to_first(which, peer):
        return pltpu.make_async_remote_copy(
            src_ref=msg.at[which, pl.ds(n_late + peer, 1)], dst_ref=arrived.at[pl.ds(row, 1)],
            send_sem=row_send, recv_sem=row_recv,
            device_id=(ends[which], peer, c), device_id_type=MESH,
        )

    def to_hub(which):
        slot = a * per_hub + lax.div(b, n_hubs)
        return pltpu.make_async_remote_copy(
            src_ref=msg.at[which, pl.ds(0, n_late + 1)], dst_ref=relay.at[slot],
            send_sem=block_send.at[which], recv_sem=block_recv,
            device_id=(ends[which], hub_y, c), device_id_type=MESH,
        )

    for which in range(2):
        for peer in sorted(range(n_early), key=lambda p: p ^ 1):
            itself = jnp.logical_and(a == ends[which], b == peer)
            meant = jnp.logical_not(itself)
            if peer == 0 and which == 0:
                meant = jnp.logical_and(meant, jnp.logical_not(with_corner))
                itself = jnp.logical_and(itself, jnp.logical_not(with_corner))

            @pl.when(meant)
            def _():
                to_first(which, peer).start()

            @pl.when(itself)
            def _():
                arrived[pl.ds(row, 1)] = msg[which, pl.ds(n_late + peer, 1)]

    def own_hub(which):
        return jnp.logical_and(a == ends[which], b == hub_y)

    for which in range(2):

        @pl.when(jnp.logical_not(own_hub(which)))
        def _():
            to_hub(which).start()

        @pl.when(own_hub(which))
        def _():
            relay[a * per_hub + lax.div(b, n_hubs)] = msg[which, pl.ds(0, n_late + 1)]

    @pl.when(is_late)
    def _():
        for h in range(n_hubs):
            pl.semaphore_signal(ready, inc=1, device_id=(a, first_hub + h, c), device_id_type=MESH)

    def halo(i, source, target, device):
        return pltpu.make_async_remote_copy(
            src_ref=source, dst_ref=target, send_sem=halo_send.at[i], recv_sem=halo_recv.at[i],
            device_id=device, device_id_type=MESH,
        )

    load_fine.wait()
    step["pack"]()
    halos = [
        halo(0, y_own.at[1], y_low, y_at(1)),
        halo(1, y_own.at[0], y_high, y_at(-1)),
        halo(2, z_own, z_low, z_at(1)),
        halo(3, z_own, z_high, z_at(-1)),
        halo(4, qx.at[:, pl.ds(64, 16)], qx.at[:, pl.ds(0, 16)], x_at(1)),
        halo(5, qx.at[:, pl.ds(16, 16)], qx.at[:, pl.ds(80, 16)], x_at(-1)),
    ]
    to_high, to_low = halos[4:]

    def send_later(i):
        pl.semaphore_wait(open_sem.at[i], 1)
        halos[i].start()

    for i, (_, greeting, _, _) in enumerate(neighbours):
        pl.when(greeting)(halos[i].start)
    for i in (5, 4, 3, 2, 0, 1):
        unknown = jnp.logical_and(neighbours[i][2], jnp.logical_not(neighbours[i][1]))
        pl.when(unknown)(functools.partial(send_later, i))
    halos = halos[:4]
    load_tgt.wait()
    load_diff.wait()

    @pl.when(is_end)
    def _():
        step["place"]()

        @pl.when(is_late)
        def _():
            step["clear_upper"]()


    step["pad"]()
    for copy in halos[2:]:
        copy.wait_recv()
    step["spread_z"]()
    step["weights_zx"]()
    step["flux_zx"]()

    @pl.when(has_high)
    def _():
        to_low.wait_recv()
        step["edge_flux"](6)

    @pl.when(has_low)
    def _():
        to_high.wait_recv()
        step["edge_flux"](0)

    for copy in halos[:2]:
        copy.wait_recv()
    step["spread_y"]()
    step["weights_y"]()
    step["flux_y"]()

    def rows_of(count, send, recv):
        rows = arrived.at[pl.ds(0, count)]
        return pltpu.make_async_remote_copy(
            src_ref=rows, dst_ref=rows, send_sem=send, recv_sem=recv, device_id=y_at(1), device_id_type=MESH
        )

    rows_of(2 * n_early - 2, row_send, row_recv).wait_send()

    @pl.when(jnp.logical_not(is_first))
    def _():
        rows_of(1, row_send, row_recv).wait_send()

    @pl.when(jnp.logical_not(with_corner))
    def _():
        rows_of(1, row_send, row_recv).wait_send()

    for which in range(2):

        @pl.when(jnp.logical_not(own_hub(which)))
        def _():
            to_hub(which).wait_send()

    for copy in halos:
        copy.wait_send()

    @pl.when(has_low)
    def _():
        to_low.wait_send()

    @pl.when(has_high)
    def _():
        to_high.wait_send()

    def to_late(peer):
        return pltpu.make_async_remote_copy(
            src_ref=merged.at[(peer - n_early) % n_y],
            dst_ref=arrived.at[pl.ds(lax.rem(b, n_hubs) * half_served, half_served)],
            send_sem=pass_send, recv_sem=pass_recv,
            device_id=(a, peer, c), device_id_type=MESH,
        )

    has_corner = jnp.logical_and(with_corner, a == 0)

    @pl.when(is_hub)
    def _():
        blocks = relay.at[pl.ds(0, served - 1)]
        pltpu.make_async_remote_copy(
            src_ref=blocks, dst_ref=blocks, send_sem=block_send.at[0], recv_sem=block_recv,
            device_id=y_at(1), device_id_type=MESH,
        ).wait_recv()
        step["merge"]()
        pl.semaphore_wait(ready, n_late + jnp.where(has_corner, 1, 0))
        for peer in range(n_early, n_y):
            to_late(peer).start()

        @pl.when(has_corner)
        def _():
            to_late(0).start()

    @pl.when(is_first)
    def _():
        rows_of(peers - 1, row_send, row_recv).wait_recv()

    @pl.when(is_late)
    def _():
        rows_of(peers // 2, pass_send, pass_recv).wait_recv()

    @pl.when(is_end)
    def _():
        step["ghost"]()
        pl.when(a == 0)(functools.partial(step["ghost_flux"], 0))
        pl.when(a == n_x - 1)(functools.partial(step["ghost_flux"], 6))

    @pl.when(is_hub)
    def _():
        for _ in range(n_late):
            rows_of(half_served, pass_send, pass_recv).wait_send()

        @pl.when(has_corner)
        def _():
            rows_of(half_served, pass_send, pass_recv).wait_send()


def solution(mesh):
    n_x, n_y, n_z = (mesh.shape[name] for name in ("gx", "gy", "gz"))

    def on_device(fine_state, diffusivity, coarse_cells, copy_sources, copy_targets):
        fields, cells_x, cells_y, cells_z = fine_state.shape
        rows = cells_x * cells_y
        peers = n_x * n_y
        n_hubs, per_hub = hubs_of(n_y)
        sources = jnp.transpose(copy_sources, (0, 1, 4, 2, 3)).reshape(3, 1, peers)
        targets = jnp.transpose(copy_targets, (0, 1, 4, 2, 3)).reshape(3, 1, peers)
        f32 = jnp.float32
        vmem = pltpu.VMEM
        anywhere = pl.BlockSpec(memory_space=pl.ANY)
        result = pl.pallas_call(
            functools.partial(kernel, n_x, n_y, n_z, fields),
            out_shape=pltpu.VMEM((fields, rows, cells_z), f32),
            in_specs=[anywhere] * 5,
            out_specs=pl.BlockSpec(memory_space=pltpu.VMEM),
            scratch_shapes=[
                vmem((fields, rows + 32, cells_z), f32),
                vmem((2, fields, 2, 8, 128), f32),
                vmem((fields, 2, 8, 128), f32),
                vmem((fields, 2, 8, 128), f32),
                vmem((fields, 16 * 8 + 16, 128), f32),
                vmem((fields, 8, 128), f32),
                vmem((fields, 8, 128), f32),
                vmem((fields, 8, 128), f32),
                vmem((fields, rows, 128), f32),
                vmem((fields, 128), f32),
                vmem((3, 1, peers), jnp.int32),
                vmem((3, 1, peers), jnp.int32),
                vmem((2, n_y, 1, 128), f32),
                vmem((n_x * per_hub, n_y - early_of(n_y) + 1, 1, 128), f32),
                vmem((n_y - early_of(n_y) + 1, n_x // 2 * per_hub, 1, 128), f32),
                vmem((128, 1, 128), f32),
                vmem((128, 128), f32),
                vmem((384, 512), jnp.bfloat16),
                vmem((8 * SLOT, 128), f32),
                vmem((8, 22, 8, 128), f32),
                pltpu.SMEM((fields,), f32),
                pltpu.SemaphoreType.DMA((5,)),
                pltpu.SemaphoreType.DMA((6,)),
                pltpu.SemaphoreType.DMA((6,)),
                pltpu.SemaphoreType.DMA,
                pltpu.SemaphoreType.DMA,
                pltpu.SemaphoreType.DMA((2,)),
                pltpu.SemaphoreType.DMA,
                pltpu.SemaphoreType.DMA,
                pltpu.SemaphoreType.DMA,
                pltpu.SemaphoreType.REGULAR,
                pltpu.SemaphoreType.REGULAR((6,)),
            ],
            compiler_params=pltpu.CompilerParams(
                collective_id=0, has_side_effects=True, vmem_limit_bytes=56 * 1024 * 1024
            ),
        )(fine_state.reshape(fields, rows, cells_z), diffusivity, coarse_cells, sources, targets)
        return result.reshape(fine_state.shape)

    return jax.shard_map(
        on_device,
        mesh=mesh,
        in_specs=(
            P(None, "gx", "gy", "gz"),
            P(),
            P(None, ("gx", "gy", "gz")),
            P("gx", "gy", "gz", None, None),
            P("gx", "gy", "gz", None, None),
        ),
        out_specs=P(None, "gx", "gy", "gz"),
        check_vma=False,
    )
```
